32 devices in a mesh: lat: 4 (over z), lon: 8 (over y, x, core).
Axes of the slice: x: 2, y: 2, z: 4, core: 2. Of those that a mesh axis runs over, the one named last changes fastest.
Arguments:
- features: bfloat16 [64, 256, 768], P('lat', 'lon'), may hold values from -10 to 10
- grad_output: bfloat16 [64, 256, 768], P('lat', 'lon'), may hold values from -6 to 6
- qkv_weight: bfloat16 [768, 2304], P(('lat', 'lon')), may hold values from -0.5 to 0.5
- out_weight: bfloat16 [768, 768], P(('lat', 'lon')), may hold values from -0.21875 to 0.21875
Outputs:
- grad_features: bfloat16 [64, 256, 768], P('lat', 'lon')
- grad_qkv_weight: float32 [768, 2304], P(('lat', 'lon'))
- grad_out_weight: float32 [768, 768], P(('lat', 'lon'))
The draws below stay inside these ranges and needn't reach their ends.
All inputs are finite; a program needn't handle non-finite values.
Results may differ from the reference program's by a relative error of at most 0.018.
Values may be sent and summed in bfloat16 or wider, within the bound.
No kernel may reach another device: no remote copies, remote signals or barrier semaphores. Data moves between devices by JAX's collectives and lax.ppermute only.
A program may use at most 128 MiB of HBM per device.

```python
import math
import jax
import jax.numpy as jnp
from jax import lax

D = 768
HEADS = 12
RADIUS = 6
QROWS = 16
QCOLS = 16
NLAT = 64
NLON = 256


def draw_features(key, part):
    values_f32 = jnp.clip(jax.random.normal(key, (NLAT, NLON, D), jnp.float32), -6.0, 6.0)
    return values_f32.astype(jnp.bfloat16)


def draw_qkv_weight(key, part):
    values_f32 = jax.random.normal(key, (D, 3 * D), jnp.float32) * (1.0 / math.sqrt(D))
    return jnp.clip(values_f32, -0.5, 0.5).astype(jnp.bfloat16)


def levels(key, shape, pieces, least, top_value):
    def one(axis_at, blocks):
        heights = jax.random.uniform(jax.random.fold_in(jax.random.fold_in(key, 6), axis_at), (blocks,), jnp.float32, least / len(pieces), top_value / len(pieces))
        return jnp.repeat(jnp.exp(heights), shape[axis_at] // blocks).reshape((-1,) + (1,) * (len(shape) - axis_at - 1))

    loudness = one(*pieces[0])
    for cut in pieces[1:]:
        loudness = loudness * one(*cut)
    return loudness


def gaussian(own_key, dims, spread, most, shards=(), kind=jnp.bfloat16):
    array = spread * jax.random.normal(own_key, dims, jnp.float32)
    if shards:
        array = array * levels(own_key, dims, shards, -0.22, 0.18)
    return jnp.clip(array, -most, most).astype(kind)


def setup_inputs(seed: int = 0) -> dict:
    arg_keys = jax.random.split(jax.random.key(seed), 5)
    return {
        "features": draw_features(jax.random.fold_in(arg_keys[4], 71), 0),
        "grad_output": gaussian(arg_keys[1], (NLAT, NLON, D), 1.0, 6.0, ((0, 4), (1, 8))),
        "qkv_weight": draw_qkv_weight(jax.random.fold_in(arg_keys[4], 71), 0),
        "out_weight": gaussian(arg_keys[3], (D, D), D ** -0.5, 0.21875, ((0, 32),)),
    }


def window_mask(row_first, query_rows, query_cols, key_rows, key_cols, radius, total_rows):
    q_rows = row_first + jnp.arange(query_rows, dtype=jnp.int32)
    k_rows = row_first - radius + jnp.arange(key_rows, dtype=jnp.int32)
    row_start = jnp.clip(q_rows - radius, 0, total_rows - 2 * radius - 1)
    row_valid = (k_rows[None, :] >= row_start[:, None]) & (k_rows[None, :] <= row_start[:, None] + 2 * radius)
    q_cols = jnp.arange(query_cols, dtype=jnp.int32)
    k_cols = jnp.arange(key_cols, dtype=jnp.int32)
    col_valid = (k_cols[None, :] >= q_cols[:, None]) & (k_cols[None, :] <= q_cols[:, None] + 2 * radius)
    allowed = row_valid[:, None, :, None] & col_valid[None, :, None, :]
    return allowed.reshape(query_rows * query_cols, key_rows * key_cols)

def tile_terms(queries, keys, values, grad_heads, window, head_count):
    q_count, model_width = queries.shape
    k_count = keys.shape[0]
    head_dim = model_width // head_count
    softmax_scale = 1.0 / math.sqrt(head_dim)
    query_f = queries.reshape(q_count, head_count, head_dim).astype(jnp.float32)
    key_f = keys.reshape(k_count, head_count, head_dim).astype(jnp.float32)
    value_f = values.reshape(k_count, head_count, head_dim).astype(jnp.float32)
    grad_f = grad_heads.reshape(q_count, head_count, head_dim).astype(jnp.float32)
    scores = jnp.einsum('qhe,khe->hqk', query_f, key_f) * softmax_scale
    scores = jnp.where(window[None], scores, -jnp.inf)
    row_max = lax.optimization_barrier(jnp.max(scores, axis=2, keepdims=True))
    exp_terms = jnp.exp(scores - row_max)
    prob_f32 = exp_terms / lax.optimization_barrier(jnp.sum(exp_terms, axis=2, keepdims=True))
    prob_b16 = prob_f32.astype(jnp.bfloat16)
    attended = jnp.einsum('hqk,khe->qhe', prob_b16.astype(jnp.float32), value_f).astype(jnp.bfloat16)
    row_term = lax.optimization_barrier(jnp.sum(grad_f * attended.astype(jnp.float32), axis=2))
    dprob = jnp.einsum('qhe,khe->hqk', grad_f, value_f)
    dscore = (prob_f32 * (dprob - row_term.T[:, :, None])).astype(jnp.bfloat16).astype(jnp.float32)
    grad_query = jnp.einsum('hqk,khe->qhe', dscore, key_f).reshape(q_count, model_width)
    grad_key = jnp.einsum('hqk,qhe->khe', dscore, query_f).reshape(k_count, model_width)
    grad_value = jnp.einsum('hqk,qhe->khe', prob_b16.astype(jnp.float32), grad_f).reshape(k_count, model_width)
    return (attended.reshape(q_count, model_width), grad_query, grad_key, grad_value)

def reference(features, grad_output, qkv_weight, out_weight):
    model_width = features.shape[2]
    radius = RADIUS
    x_rows = features.reshape(-1, model_width)
    grad_rows = grad_output.reshape(-1, model_width)
    projected = jnp.dot(x_rows, qkv_weight, preferred_element_type=jnp.float32).astype(jnp.bfloat16)
    projected = projected.reshape(NLAT, NLON, 3 * model_width)
    grad_attn = jnp.dot(grad_rows, out_weight.T, preferred_element_type=jnp.float32).astype(jnp.bfloat16)
    grad_attn = grad_attn.reshape(NLAT, NLON, model_width)
    queries = projected[..., :model_width]
    key_value = projected[..., model_width:]
    wrapped = jnp.concatenate([key_value[:, NLON - radius:], key_value, key_value[:, :radius]], axis=1)
    padded = jnp.pad(wrapped, ((radius, radius), (0, 0), (0, 0)))
    tiles_lon = NLON // QCOLS
    tile_count = NLAT // QROWS * tiles_lon
    key_rows = QROWS + 2 * radius
    key_cols = QCOLS + 2 * radius
    zero_index = jnp.int32(0)

    def tile_step(tile_index, state_tuple):
        out_all, query_all, grad_acc = state_tuple
        tile_lat = (tile_index // tiles_lon).astype(jnp.int32)
        tile_lon = (tile_index % tiles_lon).astype(jnp.int32)
        first_row = (tile_lat * QROWS).astype(jnp.int32)
        first_col = (tile_lon * QCOLS).astype(jnp.int32)
        q_tile = lax.dynamic_slice(queries, (first_row, first_col, zero_index), (QROWS, QCOLS, model_width)).reshape(-1, model_width)
        g_tile = lax.dynamic_slice(grad_attn, (first_row, first_col, zero_index), (QROWS, QCOLS, model_width)).reshape(-1, model_width)
        kv_tile = lax.dynamic_slice(padded, (first_row, first_col, zero_index), (key_rows, key_cols, 2 * model_width)).reshape(-1, 2 * model_width)
        window = window_mask(first_row, QROWS, QCOLS, key_rows, key_cols, radius, NLAT)
        attended, grad_query, grad_key, grad_value = tile_terms(q_tile, kv_tile[:, :model_width], kv_tile[:, model_width:], g_tile, window, HEADS)
        out_all = lax.dynamic_update_slice(out_all, attended.reshape(QROWS, QCOLS, model_width), (first_row, first_col, zero_index))
        query_all = lax.dynamic_update_slice(query_all, grad_query.reshape(QROWS, QCOLS, model_width), (first_row, first_col, zero_index))
        region = lax.dynamic_slice(grad_acc, (first_row, first_col, zero_index), (key_rows, key_cols, 2 * model_width))
        region = region + jnp.concatenate([grad_key, grad_value], axis=1).reshape(key_rows, key_cols, 2 * model_width)
        grad_acc = lax.dynamic_update_slice(grad_acc, region, (first_row, first_col, zero_index))
        return (out_all, query_all, grad_acc)
    start_state = (jnp.zeros((NLAT, NLON, model_width), jnp.bfloat16), jnp.zeros((NLAT, NLON, model_width), jnp.float32), jnp.zeros((NLAT + 2 * radius, NLON + 2 * radius, 2 * model_width), jnp.float32))
    out_all, query_all, grad_acc = lax.fori_loop(jnp.int32(0), jnp.int32(tile_count), tile_step, start_state)
    interior = grad_acc[radius:radius + NLAT]
    middle = interior[:, radius:radius + NLON]
    middle = middle.at[:, :radius].add(interior[:, radius + NLON:])
    middle = middle.at[:, NLON - radius:].add(interior[:, :radius])
    softmax_scale = 1.0 / math.sqrt(model_width // HEADS)
    grad_query = (query_all * softmax_scale).astype(jnp.bfloat16).reshape(-1, model_width)
    grad_key = (middle[..., :model_width] * softmax_scale).astype(jnp.bfloat16).reshape(-1, model_width)
    grad_value = middle[..., model_width:].astype(jnp.bfloat16).reshape(-1, model_width)
    grad_proj = jnp.concatenate([grad_query, grad_key, grad_value], axis=1)
    grad_features = jnp.dot(grad_proj, qkv_weight.T, preferred_element_type=jnp.float32).astype(jnp.bfloat16)
    grad_qkv = jnp.dot(x_rows.T, grad_proj, preferred_element_type=jnp.float32)
    grad_out = jnp.dot(out_all.reshape(-1, model_width).T, grad_rows, preferred_element_type=jnp.float32)
    return (grad_features.reshape(NLAT, NLON, model_width), grad_qkv, grad_out)
```

```python
import math

import jax
import jax.numpy as jnp
from jax import lax
from jax.experimental import pallas as pl
from jax.experimental.pallas import tpu as pltpu
from jax.sharding import PartitionSpec as P

HEADS = 12
RADIUS = 6
QROWS = 16
QCOLS = 16
MARGIN = 8
PAIR = 2
OUTSIDE = -1e30
LOG2E = math.log2(math.e)
GATHER_GROUPS = ((0,), (1, 2))
SCATTER_GROUPS = ((0, 1), (2,))

NT = (((1,), (1,)), ((), ()))
NN = (((1,), (0,)), ((), ()))


def dot(a, b, dims=NN):
    return lax.dot_general(a, b, dims, preferred_element_type=jnp.float32)


def attention_kernel(
    q_ref, g_ref, k_ref, v_ref, bias_ref, hot_ref,
    att_ref, dq_ref, dk_ref, dv_ref,
    scores, e_both, ds_both, dq_sum, dk_sum, dv_sum,
):
    tile_row, tile_col = pl.program_id(0), pl.program_id(1)
    key_rows, key_cols = QROWS + 2 * RADIUS, QCOLS + 2 * MARGIN
    keys, queries = key_rows * key_cols, QROWS * QCOLS
    lanes = q_ref.shape[-1]
    head = lanes // PAIR
    chunk = 64
    first_row = tile_row * QROWS
    first_col = pl.multiple_of(tile_col * QCOLS, QCOLS)
    at_rows, at_cols = pl.ds(first_row, key_rows), pl.ds(first_col, key_cols)

    @pl.when((tile_row == 0) & (tile_col == 0))
    def _():
        dq_sum[...] = jnp.zeros_like(dq_sum)
        dk_sum[...] = jnp.zeros_like(dk_sum)
        dv_sum[...] = jnp.zeros_like(dv_sum)

    q = q_ref[...].reshape(queries, lanes)
    g_t = g_ref[...].reshape(queries, lanes).astype(jnp.float32).T
    k = k_ref[at_rows, at_cols, :].reshape(keys, lanes)
    v = v_ref[at_rows, at_cols, :].reshape(keys, lanes)
    k_wide = jnp.concatenate([k, bias_ref[0]], axis=1)
    k_t, v_t = k.T, v.T
    ones = jnp.ones((16, keys), jnp.bfloat16)
    lane = lax.broadcasted_iota(jnp.int32, (queries, lanes), 1) // head
    q_heads, g_heads, att_t, dq_t = [], [], [], []
    for h in range(PAIR):
        rows = slice(h * head, (h + 1) * head)
        cols = slice(h * queries, (h + 1) * queries)
        q_one = jnp.where(lane == h, q, jnp.zeros_like(q))
        q_heads.append(q_one)
        scores[h] = dot(k_wide, jnp.concatenate([q_one, hot_ref[...]], axis=1), NT)
        top = jnp.max(scores[h], axis=0, keepdims=True)
        for c in range(0, keys, chunk):
            e_both[c : c + chunk, cols] = jnp.exp2(scores[h, c : c + chunk] - top).astype(jnp.bfloat16)
        out = dot(jnp.concatenate([v_t[rows], ones], axis=0), e_both[:, cols])
        inverse = 1.0 / out[head : head + 1]
        attended = (out[:head] * inverse).astype(jnp.bfloat16)
        g_one = g_t[rows] * inverse
        row_term = jnp.sum(g_one * attended.astype(jnp.float32), axis=0, keepdims=True)
        g_one = g_one.astype(jnp.bfloat16)
        empty = jnp.zeros_like(g_one)
        g_one = jnp.concatenate([empty] * h + [g_one] + [empty] * (PAIR - 1 - h), axis=0)
        g_heads.append(g_one)
        scores[h] = dot(v, g_one)
        for c in range(0, keys, chunk):
            ds_both[c : c + chunk, cols] = (
                e_both[c : c + chunk, cols].astype(jnp.float32) * (scores[h, c : c + chunk] - row_term)
            ).astype(jnp.bfloat16)
        att_t.append(attended.astype(jnp.float32))
        dq_t.append(dot(k_t[rows], ds_both[:, cols]))
    tile = (key_rows, key_cols, lanes)
    dv_sum[at_rows, at_cols, :] += dot(e_both[...], jnp.concatenate(g_heads, axis=1), NT).reshape(tile)
    dk_sum[at_rows, at_cols, :] += dot(ds_both[...], jnp.concatenate(q_heads, axis=0)).reshape(tile)
    att_ref[...] = jnp.concatenate(att_t, axis=0).T.astype(jnp.bfloat16).reshape(QROWS, QCOLS, lanes)
    dq = jnp.concatenate(dq_t, axis=0).T * (1.0 / math.sqrt(head))
    dq_sum[pl.ds(first_row + RADIUS, QROWS), pl.ds(pl.multiple_of(first_col + MARGIN, 8), QCOLS), :] = dq.reshape(
        QROWS, QCOLS, lanes
    )

    @pl.when((tile_row == pl.num_programs(0) - 1) & (tile_col == pl.num_programs(1) - 1))
    def _():
        dq_ref[...] = dq_sum[...].astype(jnp.bfloat16)
        dk_ref[...] = (dk_sum[...] * (1.0 / LOG2E)).astype(jnp.bfloat16)
        dv_ref[...] = dv_sum[...].astype(jnp.bfloat16)


def attention(q, g, k, v, bias, hot):
    rows, cols, lanes = q.shape
    wide = k.shape
    queries, keys = QROWS * QCOLS, (QROWS + 2 * RADIUS) * (QCOLS + 2 * MARGIN)
    tiles = (rows // QROWS, cols // QCOLS)
    tile = pl.BlockSpec((QROWS, QCOLS, lanes), lambda r, c: (r, c, 0))
    whole = pl.BlockSpec(wide, lambda r, c: (0, 0, 0))
    out = jax.ShapeDtypeStruct(wide, jnp.bfloat16)
    return pl.pallas_call(
        attention_kernel,
        grid=tiles,
        in_specs=[
            tile, tile, whole, whole,
            pl.BlockSpec((1, keys, lanes), lambda r, c: (r, 0, 0)),
            pl.BlockSpec((queries, lanes), lambda r, c: (0, 0)),
        ],
        out_specs=[tile, whole, whole, whole],
        out_shape=[jax.ShapeDtypeStruct(q.shape, jnp.bfloat16), out, out, out],
        scratch_shapes=[
            pltpu.VMEM((PAIR, keys, queries), jnp.float32),
            pltpu.VMEM((keys, PAIR * queries), jnp.bfloat16),
            pltpu.VMEM((keys, PAIR * queries), jnp.bfloat16),
            pltpu.VMEM(wide, jnp.float32),
            pltpu.VMEM(wide, jnp.float32),
            pltpu.VMEM(wide, jnp.float32),
        ],
        compiler_params=pltpu.CompilerParams(
            dimension_semantics=("arbitrary", "arbitrary"), vmem_limit_bytes=48 * 1024 * 1024
        ),
        cost_estimate=pl.CostEstimate(
            flops=2 * 6 * 256 * keys * queries * PAIR * tiles[0] * tiles[1],
            bytes_accessed=12 * rows * cols * lanes * 2,
            transcendentals=keys * queries * PAIR * tiles[0] * tiles[1],
        ),
    )(q, g, k, v, bias, hot)


def window_columns(lat_first, tile_rows, total_rows, lanes):
    key_rows, key_cols = QROWS + 2 * RADIUS, QCOLS + 2 * MARGIN
    base = lat_first + QROWS * jnp.arange(tile_rows, dtype=jnp.int32)[:, None, None]
    q_row = base + jnp.arange(QROWS, dtype=jnp.int32)[None, None, :]
    k_row = base - RADIUS + jnp.arange(key_rows, dtype=jnp.int32)[None, :, None]
    start = jnp.clip(q_row - RADIUS, 0, total_rows - 2 * RADIUS - 1)
    row_in = (k_row >= start) & (k_row <= start + 2 * RADIUS)
    q_col = jnp.arange(QCOLS, dtype=jnp.int32)[None, :]
    k_col = jnp.arange(key_cols, dtype=jnp.int32)[:, None] - MARGIN
    col_in = (k_col >= q_col - RADIUS) & (k_col <= q_col + RADIUS)
    shape = (tile_rows, key_rows, key_cols)
    row_part = jnp.broadcast_to(jnp.where(row_in, 0.0, OUTSIDE)[:, :, None, :], shape + (QROWS,))
    col_part = jnp.broadcast_to(jnp.where(col_in, 0.0, OUTSIDE)[None, None], shape + (QCOLS,))
    rest = jnp.zeros(shape + (lanes - QROWS - QCOLS,), jnp.float32)
    columns = jnp.concatenate([row_part, col_part, rest], axis=-1).astype(jnp.bfloat16)
    columns = columns.reshape(tile_rows, key_rows * key_cols, lanes)
    r, c = jnp.arange(QROWS * QCOLS) // QCOLS, jnp.arange(QROWS * QCOLS) % QCOLS
    lane = jnp.arange(lanes)[None, :]
    hot = ((lane == r[:, None]) | (lane == QROWS + c[:, None])).astype(jnp.bfloat16)
    return columns, hot


def routed(value, route):
    lats, lons = lax.axis_size("lat"), lax.axis_size("lon")
    pairs = []
    for a in range(lats):
        for o in range(lons):
            to_lat, to_lon = route(a, o)
            if 0 <= to_lat < lats:
                pairs.append((a * lons + o, to_lat * lons + to_lon % lons))
    return lax.ppermute(value, ("lat", "lon"), pairs)


def partner(value):
    return routed(value, lambda a, o: (a, o ^ 1))


def beside(o):
    return o + 1 if o % 2 else o - 1


def by_core(core, mine, other, axis):
    return jnp.where(
        core == 0, jnp.concatenate([mine, other], axis=axis), jnp.concatenate([other, mine], axis=axis)
    )


def turned(parts, by):
    stack = jnp.stack([parts[0]] + parts[:0:-1])
    return jnp.roll(stack, by, axis=0)


def gathered(block, lat, chip):
    lats, chips = lax.axis_size("lat"), lax.axis_size("lon") // 2
    parts = [block] + [routed(block, lambda a, o, d=d: ((a + d) % lats, o)) for d in range(1, lats)]
    column = turned(parts, lat)
    parts = [column] + [routed(column, lambda a, o, d=d: (a, o + 2 * d)) for d in range(1, chips)]
    grid = turned(parts, chip)
    return jnp.swapaxes(grid, 0, 1).reshape((-1,) + block.shape[1:])


def scattered(total, lat, chip):
    lats, chips = lax.axis_size("lat"), lax.axis_size("lon") // 2
    width = total.shape[1]
    total = total.reshape(lats, chips, -1, width)
    kept = lax.dynamic_index_in_dim(total, chip, 1, keepdims=False)
    moved = [
        routed(
            lax.dynamic_index_in_dim(total, (chip + d) % chips, 1, keepdims=False).astype(jnp.bfloat16),
            lambda a, o, d=d: (a, o + 2 * d),
        )
        for d in range(1, chips)
    ]
    for part in moved:
        kept = kept + part.astype(jnp.float32)
    mine = lax.dynamic_index_in_dim(kept, lat, 0, keepdims=False)
    moved = [
        routed(
            lax.dynamic_index_in_dim(kept, (lat + d) % lats, 0, keepdims=False).astype(jnp.bfloat16),
            lambda a, o, d=d: ((a + d) % lats, o),
        )
        for d in range(1, lats)
    ]
    for part in moved:
        mine = mine + part.astype(jnp.float32)
    return mine


def shards(features, grad_output, qkv_weight, out_weight):
    lat_rows, lon_cols, width = features.shape
    head = width // HEADS
    lanes = PAIR * head
    groups = HEADS // PAIR // 2
    half = width // 2
    lats = lax.axis_size("lat")
    lat, lon = lax.axis_index("lat"), lax.axis_index("lon")
    core, chip = lon % 2, lon // 2
    rows = qkv_weight.shape[0]

    by_heads = qkv_weight.reshape(rows, 3, 2, groups, lanes)
    qkv_mine = lax.dynamic_index_in_dim(by_heads, core, 2, keepdims=False)
    qkv_other = lax.dynamic_index_in_dim(by_heads, 1 - core, 2, keepdims=False)
    by_half = out_weight.reshape(rows, 2, half)
    out_mine = lax.dynamic_index_in_dim(by_half, core, 1, keepdims=False)
    out_other = lax.dynamic_index_in_dim(by_half, 1 - core, 1, keepdims=False)

    def flat(qkv, out):
        return jnp.concatenate([jnp.swapaxes(qkv, 1, 2).reshape(rows, -1), out], axis=1)

    mine, other = flat(qkv_mine, out_mine), flat(qkv_other, out_other)
    block = by_core(core, mine, partner(other), 0)
    per = 3 * lanes
    qkv_of, out_half = {}, None
    for n, members in enumerate(GATHER_GROUPS):
        part = block[:, members[0] * per : (members[-1] + 1) * per]
        if n == 0:
            part = jnp.concatenate([part, block[:, groups * per :]], axis=1)
        whole = gathered(part, lat, chip)
        for i, m in enumerate(members):
            qkv_of[m] = whole[:, i * per : (i + 1) * per]
        if n == 0:
            out_half = whole[:, len(members) * per :]
    by_rows = out_half.reshape(2, half, half)
    out_own = lax.dynamic_index_in_dim(by_rows, core, 0, keepdims=False)
    out_swap = partner(lax.dynamic_index_in_dim(by_rows, 1 - core, 0, keepdims=False))
    out_heads = by_core(core, out_own, out_swap, 1)

    edge = jnp.where(core == 0, features[:, :MARGIN], features[:, lon_cols - MARGIN :])
    x_partner, go_partner = partner(features), partner(grad_output)
    above = routed(features[lat_rows - RADIUS :], lambda a, o: (a + 1, o))
    below = routed(features[:RADIUS], lambda a, o: (a - 1, o))
    side = routed(edge, lambda a, o: (a, beside(o)))
    side_above = routed(edge[lat_rows - RADIUS :], lambda a, o: (a + 1, beside(o)))
    side_below = routed(edge[:RADIUS], lambda a, o: (a - 1, beside(o)))
    caps = jnp.concatenate([above, below], axis=0)
    flank = jnp.concatenate([side_above, side, side_below], axis=0)
    caps_partner, flank_partner = partner(caps), partner(flank)
    middle = by_core(core, features, x_partner, 1)
    caps = by_core(core, caps, caps_partner, 1)
    middle = jnp.concatenate([caps[:RADIUS], middle, caps[RADIUS:]], axis=0)
    left = jnp.where(core == 0, flank, flank_partner)
    right = jnp.where(core == 0, flank_partner, flank)
    x_wide = jnp.concatenate([left, middle, right], axis=1)
    wide_rows, wide_cols = x_wide.shape[:2]
    x_wide = x_wide.reshape(-1, width)
    go = by_core(core, grad_output, go_partner, 1)
    block_cols = 2 * lon_cols
    go_rows = go.reshape(-1, width)

    bias, hot = window_columns(lat * lat_rows, lat_rows // QROWS, lat_rows * lats, lanes)
    scale = jnp.concatenate(
        [jnp.full((lanes,), LOG2E / math.sqrt(head), jnp.float32), jnp.ones((2 * lanes,), jnp.float32)]
    )
    grads, attended, scattered_of = {}, {}, {}
    for m in range(groups):
        projected = (dot(x_wide, qkv_of[m]) * scale).astype(jnp.bfloat16)
        projected = projected.reshape(wide_rows, wide_cols, per)
        q = projected[RADIUS : RADIUS + lat_rows, MARGIN : MARGIN + block_cols, :lanes]
        g = dot(go_rows, out_heads[m * lanes : (m + 1) * lanes], NT).astype(jnp.bfloat16)
        g = g.reshape(lat_rows, block_cols, lanes)
        att, dq, dk, dv = attention(q, g, projected[..., lanes : 2 * lanes], projected[..., 2 * lanes :], bias, hot)
        attended[m] = att.reshape(-1, lanes)
        grads[m] = jnp.concatenate([dq, dk, dv], axis=-1).reshape(-1, per)

    tn = (((0,), (0,)), ((), ()))
    pieces = []
    for n, members in enumerate(SCATTER_GROUPS):
        parts = [dot(x_wide, grads[m], tn) for m in members]
        if n == len(SCATTER_GROUPS) - 1:
            all_attended = jnp.concatenate([attended[m] for m in range(groups)], axis=1)
            out_rows = dot(all_attended, go_rows, tn).reshape(half, 2, half)
            keep = lax.dynamic_index_in_dim(out_rows, core, 1, keepdims=False)
            give = lax.dynamic_index_in_dim(out_rows, 1 - core, 1, keepdims=False).astype(jnp.bfloat16)
            parts.append(by_core(core, keep, partner(give).astype(jnp.float32), 0))
        pieces.append(scattered(jnp.concatenate(parts, axis=1), lat, chip))

    all_grads = jnp.concatenate([grads[m] for m in range(groups)], axis=1)
    all_qkv = jnp.concatenate([qkv_of[m] for m in range(groups)], axis=1)
    gx = dot(all_grads, all_qkv, NT).reshape(wide_rows, 2, lon_cols + MARGIN, width)
    keep = lax.dynamic_index_in_dim(gx, core, 1, keepdims=False)
    give = lax.dynamic_index_in_dim(gx, 1 - core, 1, keepdims=False).astype(jnp.bfloat16)
    mine_x = keep + partner(give).astype(jnp.float32)
    middle = jnp.where(core == 0, mine_x[:, MARGIN:], mine_x[:, :lon_cols])
    flank = jnp.where(core == 0, mine_x[:, :MARGIN], mine_x[:, lon_cols:])
    low = flank.astype(jnp.bfloat16)
    ends = middle.astype(jnp.bfloat16)
    from_below = routed(ends[:RADIUS], lambda a, o: (a - 1, o)).astype(jnp.float32)
    from_above = routed(ends[RADIUS + lat_rows :], lambda a, o: (a + 1, o)).astype(jnp.float32)
    from_side = routed(low[RADIUS : RADIUS + lat_rows], lambda a, o: (a, beside(o))).astype(jnp.float32)
    corner_below = routed(low[:RADIUS], lambda a, o: (a - 1, beside(o))).astype(jnp.float32)
    corner_above = routed(low[RADIUS + lat_rows :], lambda a, o: (a + 1, beside(o))).astype(jnp.float32)

    def stacked(top, bottom):
        gap = jnp.zeros((lat_rows - 2 * RADIUS,) + top.shape[1:], jnp.float32)
        return jnp.concatenate([top, gap, bottom], axis=0)

    grad_x = middle[RADIUS : RADIUS + lat_rows] + stacked(from_above, from_below)
    edge = from_side + stacked(corner_above, corner_below)
    gap = jnp.zeros((lat_rows, lon_cols - MARGIN, width), jnp.float32)
    grad_x = grad_x + by_core(core, edge, gap, 1)
    grad_x = grad_x.astype(jnp.bfloat16)

    total = jnp.concatenate(pieces, axis=1).reshape(2, rows, -1)
    keep = lax.dynamic_index_in_dim(total, core, 0, keepdims=False)
    give = lax.dynamic_index_in_dim(total, 1 - core, 0, keepdims=False).astype(jnp.bfloat16)
    got = partner(give).astype(jnp.float32)
    order = jnp.where(core == 0, jnp.stack([keep, got]), jnp.stack([got, keep]))
    grad_qkv = order[:, :, : groups * per].reshape(2, rows, groups, 3, lanes)
    grad_qkv = jnp.transpose(grad_qkv, (1, 3, 0, 2, 4)).reshape(rows, 3 * width)
    grad_out = jnp.transpose(order[:, :, groups * per :], (1, 0, 2)).reshape(rows, width)
    return grad_x, grad_qkv, grad_out


def solution(mesh):
    placed = (
        P("lat", "lon", None),
        P("lat", "lon", None),
        P(("lat", "lon"), None),
        P(("lat", "lon"), None),
    )
    return jax.shard_map(
        shards,
        mesh=mesh,
        in_specs=placed,
        out_specs=(P("lat", "lon", None), P(("lat", "lon"), None), P(("lat", "lon"), None)),
        check_vma=False,
    )
```

```python
import math

import jax
import jax.numpy as jnp
from jax import lax
from jax.experimental import pallas as pl
from jax.experimental.pallas import tpu as pltpu
from jax.sharding import PartitionSpec as P

HEADS = 12
RADIUS = 6
QROWS = 16
QCOLS = 16
MARGIN = 8
PAIR = 2
OUTSIDE = -1e30
LOG2E = math.log2(math.e)

NT = (((1,), (1,)), ((), ()))
NN = (((1,), (0,)), ((), ()))


def dot(a, b, dims=NN):
    return lax.dot_general(a, b, dims, preferred_element_type=jnp.float32)


def attention_kernel(p_ref, g_ref, bias_ref, hot_ref, att_ref, grad_ref, *scratch):
    scores, e_both, ds_both, sums = scratch[:PAIR], scratch[PAIR], scratch[PAIR + 1], scratch[PAIR + 2]
    tile_row, tile_col = pl.program_id(0), pl.program_id(1)
    key_rows, key_cols = QROWS + 2 * RADIUS, QCOLS + 2 * MARGIN
    keys, queries = key_rows * key_cols, QROWS * QCOLS
    lanes = g_ref.shape[-1]
    head = lanes // PAIR
    chunk = 64
    first_row = tile_row * QROWS
    first_col = pl.multiple_of(tile_col * QCOLS, QCOLS)
    at_rows, at_cols = pl.ds(first_row, key_rows), pl.ds(first_col, key_cols)
    q_lanes, k_lanes, v_lanes = (slice(i * lanes, (i + 1) * lanes) for i in range(3))
    heads = range(PAIR)
    rows = [slice(h * head, (h + 1) * head) for h in heads]
    cols = [slice(h * queries, (h + 1) * queries) for h in heads]

    @pl.when((tile_row == 0) & (tile_col == 0))
    def _():
        sums[...] = jnp.zeros_like(sums)

    q = p_ref[pl.ds(first_row + RADIUS, QROWS), at_cols, q_lanes].astype(jnp.float32)
    q = q[:, MARGIN : MARGIN + QCOLS].reshape(queries, lanes).astype(jnp.bfloat16)
    g_t = g_ref[...].reshape(queries, lanes).astype(jnp.float32).T
    k = p_ref[at_rows, at_cols, k_lanes].reshape(keys, lanes)
    v = p_ref[at_rows, at_cols, v_lanes].reshape(keys, lanes)
    k_wide = jnp.concatenate([k, bias_ref[0]], axis=1)
    ones = jnp.ones((16, keys), jnp.bfloat16)
    lane = lax.broadcasted_iota(jnp.int32, (queries, lanes), 1) // head
    q_heads = [jnp.where(lane == h, q, jnp.zeros_like(q)) for h in heads]
    for h in heads:
        scores[h][...] = dot(k_wide, jnp.concatenate([q_heads[h], hot_ref[...]], axis=1), NT)
    k_t, v_t = k.T, v.T
    g_heads, att_t, dq_t, terms = [], [], [], []
    for h in heads:
        top = jnp.max(scores[h][...], axis=0, keepdims=True)
        for c in range(0, keys, chunk):
            e_both[c : c + chunk, cols[h]] = jnp.exp2(scores[h][c : c + chunk] - top).astype(jnp.bfloat16)
        out = dot(jnp.concatenate([v_t[rows[h]], ones], axis=0), e_both[:, cols[h]])
        inverse = 1.0 / out[head : head + 1]
        attended = (out[:head] * inverse).astype(jnp.bfloat16).astype(jnp.float32)
        att_t.append(attended)
        g_one = g_t[rows[h]] * inverse
        terms.append(jnp.sum(g_one * attended, axis=0, keepdims=True))
        empty = jnp.zeros_like(g_one)
        g_one = jnp.concatenate([empty] * h + [g_one] + [empty] * (PAIR - 1 - h), axis=0).astype(jnp.bfloat16)
        g_heads.append(g_one)
    for h in heads:
        scores[h][...] = dot(v, g_heads[h])
    for h in heads:
        for c in range(0, keys, chunk):
            ds_both[c : c + chunk, cols[h]] = (
                e_both[c : c + chunk, cols[h]].astype(jnp.float32) * (scores[h][c : c + chunk] - terms[h])
            ).astype(jnp.bfloat16)
        dq_t.append(dot(k_t[rows[h]], ds_both[:, cols[h]]))
    tile = (key_rows, key_cols, lanes)
    sums[at_rows, at_cols, v_lanes] += dot(e_both[...], jnp.concatenate(g_heads, axis=1), NT).reshape(tile)
    sums[at_rows, at_cols, k_lanes] += dot(ds_both[...], jnp.concatenate(q_heads, axis=0)).reshape(tile)
    att_ref[...] = jnp.concatenate(att_t, axis=0).T.astype(jnp.bfloat16).reshape(QROWS, QCOLS, lanes)
    dq = jnp.concatenate(dq_t, axis=0).T * (1.0 / math.sqrt(head))
    sums[pl.ds(first_row + RADIUS, QROWS), pl.ds(pl.multiple_of(first_col + MARGIN, 8), QCOLS), q_lanes] = dq.reshape(
        QROWS, QCOLS, lanes
    )

    @pl.when((tile_row == pl.num_programs(0) - 1) & (tile_col == pl.num_programs(1) - 1))
    def _():
        grad_ref[:, :, q_lanes] = sums[:, :, q_lanes].astype(jnp.bfloat16)
        grad_ref[:, :, k_lanes] = (sums[:, :, k_lanes] * (1.0 / LOG2E)).astype(jnp.bfloat16)
        grad_ref[:, :, v_lanes] = sums[:, :, v_lanes].astype(jnp.bfloat16)


def attention(projected, g, bias, hot, place, g_place, lanes):
    rows, cols = g.shape[:2]
    wide = projected.shape[:2] + (3 * lanes,)
    queries, keys = QROWS * QCOLS, (QROWS + 2 * RADIUS) * (QCOLS + 2 * MARGIN)
    tiles = (rows // QROWS, cols // QCOLS)
    tile = (QROWS, QCOLS, lanes)
    return pl.pallas_call(
        attention_kernel,
        grid=tiles,
        in_specs=[
            pl.BlockSpec(wide, lambda r, c: (0, 0, place)),
            pl.BlockSpec(tile, lambda r, c: (r, c, g_place)),
            pl.BlockSpec((1, keys, lanes), lambda r, c: (r, 0, 0)),
            pl.BlockSpec((queries, lanes), lambda r, c: (0, 0)),
        ],
        out_specs=[pl.BlockSpec(tile, lambda r, c: (r, c, 0)), pl.BlockSpec(wide, lambda r, c: (0, 0, 0))],
        out_shape=[
            jax.ShapeDtypeStruct((rows, cols, lanes), jnp.bfloat16),
            jax.ShapeDtypeStruct(wide, jnp.bfloat16),
        ],
        scratch_shapes=[pltpu.VMEM((keys, queries), jnp.float32)] * PAIR
        + [pltpu.VMEM((keys, PAIR * queries), jnp.bfloat16)] * 2
        + [pltpu.VMEM(wide, jnp.float32)],
        compiler_params=pltpu.CompilerParams(
            dimension_semantics=("arbitrary", "arbitrary"), vmem_limit_bytes=48 * 1024 * 1024
        ),
        cost_estimate=pl.CostEstimate(
            flops=2 * 15 * 256 * keys * queries * PAIR * tiles[0] * tiles[1],
            bytes_accessed=12 * rows * cols * lanes * 2,
            transcendentals=keys * queries * PAIR * tiles[0] * tiles[1],
        ),
    )(projected, g, bias, hot)


def window_columns(lat_first, tile_rows, total_rows, lanes):
    key_rows, key_cols = QROWS + 2 * RADIUS, QCOLS + 2 * MARGIN
    base = lat_first + QROWS * jnp.arange(tile_rows, dtype=jnp.int32)[:, None, None]
    q_row = base + jnp.arange(QROWS, dtype=jnp.int32)[None, None, :]
    k_row = base - RADIUS + jnp.arange(key_rows, dtype=jnp.int32)[None, :, None]
    start = jnp.clip(q_row - RADIUS, 0, total_rows - 2 * RADIUS - 1)
    row_in = (k_row >= start) & (k_row <= start + 2 * RADIUS)
    q_col = jnp.arange(QCOLS, dtype=jnp.int32)[None, :]
    k_col = jnp.arange(key_cols, dtype=jnp.int32)[:, None] - MARGIN
    col_in = (k_col >= q_col - RADIUS) & (k_col <= q_col + RADIUS)
    shape = (tile_rows, key_rows, key_cols)
    row_part = jnp.broadcast_to(jnp.where(row_in, 0.0, OUTSIDE)[:, :, None, :], shape + (QROWS,))
    col_part = jnp.broadcast_to(jnp.where(col_in, 0.0, OUTSIDE)[None, None], shape + (QCOLS,))
    rest = jnp.zeros(shape + (lanes - QROWS - QCOLS,), jnp.float32)
    columns = jnp.concatenate([row_part, col_part, rest], axis=-1).astype(jnp.bfloat16)
    columns = columns.reshape(tile_rows, key_rows * key_cols, lanes)
    r, c = jnp.arange(QROWS * QCOLS) // QCOLS, jnp.arange(QROWS * QCOLS) % QCOLS
    lane = jnp.arange(lanes)[None, :]
    hot = ((lane == r[:, None]) | (lane == QROWS + c[:, None])).astype(jnp.bfloat16)
    return columns, hot


def routed(value, route):
    lats, lons = lax.axis_size("lat"), lax.axis_size("lon")
    pairs = []
    for a in range(lats):
        for o in range(lons):
            to_lat, to_lon = route(a, o)
            if 0 <= to_lat < lats:
                pairs.append((a * lons + o, to_lat * lons + to_lon % lons))
    return lax.ppermute(value, ("lat", "lon"), pairs)


def partner(value):
    return routed(value, lambda a, o: (a, o ^ 1))


def beside(o):
    return o + 1 if o % 2 else o - 1


def by_core(core, mine, other, axis):
    return jnp.where(
        core == 0, jnp.concatenate([mine, other], axis=axis), jnp.concatenate([other, mine], axis=axis)
    )


def turned(parts, by):
    stack = jnp.stack([parts[0]] + parts[:0:-1])
    return jnp.roll(stack, by, axis=0)


def lat_moves(blocks):
    lats = lax.axis_size("lat")
    return [routed(part, lambda a, o, d=d + 1: ((a + d) % lats, o)) for d, part in enumerate(blocks)]


def chip_moves(blocks):
    return [routed(part, lambda a, o, d=d + 1: (a, o + 2 * d)) for d, part in enumerate(blocks)]


def gather_rows(parts, chip):
    grid = turned(parts, chip)
    return jnp.swapaxes(grid, 0, 1).reshape((-1,) + grid.shape[3:])


def pick(value, index, count, dim):
    return lax.dynamic_index_in_dim(value, index % count, dim, keepdims=False)


def scatter_split(total, chip):
    lats, chips = lax.axis_size("lat"), lax.axis_size("lon") // 2
    total = total.reshape(lats, chips, -1, total.shape[1])
    return pick(total, chip, chips, 1), [
        pick(total, chip + d, chips, 1).astype(jnp.bfloat16) for d in range(1, chips)
    ]


def added(kept, parts):
    for part in parts:
        kept = kept + part.astype(jnp.float32)
    return kept


def scatter_rest(kept, lat):
    lats = lax.axis_size("lat")
    moved = lat_moves([pick(kept, lat + d, lats, 0).astype(jnp.bfloat16) for d in range(1, lats)])
    return added(pick(kept, lat, lats, 0), moved)


def after(value, *others):
    return lax.optimization_barrier((value,) + others)[0]


def shards(features, grad_output, qkv_weight, out_weight):
    lat_rows, lon_cols, width = features.shape
    head = width // HEADS
    lanes = PAIR * head
    groups = HEADS // PAIR // 2
    half = width // 2
    lats = lax.axis_size("lat")
    lat, lon = lax.axis_index("lat"), lax.axis_index("lon")
    core, chip = lon % 2, lon // 2
    rows = qkv_weight.shape[0]
    per = 3 * lanes
    cells = lat_rows * lon_cols

    by_heads = qkv_weight.reshape(rows, 3, 2, groups, lanes)
    by_half = out_weight.reshape(rows, 2, half)

    def columns(which):
        qkv = lax.dynamic_index_in_dim(by_heads, which, 2, keepdims=False)
        out = lax.dynamic_index_in_dim(by_half, which, 1, keepdims=False)
        return jnp.concatenate([jnp.swapaxes(qkv, 1, 2).reshape(rows, -1), out], axis=1)

    mine, other = columns(core), columns(1 - core)
    block = by_core(core, mine, partner(other), 0)
    both = jnp.concatenate([features.reshape(cells, width), grad_output.reshape(cells, width)], axis=0)
    both = partner(after(both, block))
    x_partner = both[:cells].reshape(features.shape)
    go_partner = both[cells:].reshape(features.shape)

    edge = jnp.where(core == 0, features[:, :MARGIN], features[:, lon_cols - MARGIN :])
    side = routed(edge, lambda a, o: (a, beside(o)))
    lats_less, chips_less = lats - 1, lax.axis_size("lon") // 2 - 1
    first = jnp.concatenate([block[:, :per], block[:, groups * per :]], axis=1)
    first = turned([first] + lat_moves([first] * lats_less), lat)
    first = gather_rows([first] + chip_moves([first] * chips_less), chip)
    qkv_first, out_half = first[:, :per], first[:, per:]
    by_rows = out_half.reshape(2, half, half)
    out_own = lax.dynamic_index_in_dim(by_rows, core, 0, keepdims=False)
    out_swap = partner(lax.dynamic_index_in_dim(by_rows, 1 - core, 0, keepdims=False))
    out_heads = by_core(core, out_own, out_swap, 1)
    rest = after(block[:, per : groups * per], first)
    rest = turned([rest] + lat_moves([rest] * lats_less), lat)
    rest_parts = [rest] + chip_moves([rest] * chips_less)

    half_cols = lon_cols + MARGIN
    near = jnp.where(
        core == 0, jnp.concatenate([side, features], axis=1), jnp.concatenate([features, side], axis=1)
    )
    above = routed(near[lat_rows - RADIUS :], lambda a, o: (a + 1, o))
    below = routed(near[:RADIUS], lambda a, o: (a - 1, o))
    rim = jnp.concatenate([above.reshape(-1, width), below.reshape(-1, width), side.reshape(-1, width)], axis=0)
    rim = partner(rim)
    cap = RADIUS * half_cols
    far_above = rim[:cap].reshape(above.shape)
    far_below = rim[cap : 2 * cap].reshape(below.shape)
    far_side = rim[2 * cap :].reshape(side.shape)
    far = jnp.where(
        core == 0,
        jnp.concatenate([x_partner, far_side], axis=1),
        jnp.concatenate([far_side, x_partner], axis=1),
    )
    near = jnp.concatenate([above, near, below], axis=0)
    far = jnp.concatenate([far_above, far, far_below], axis=0)
    x_wide = by_core(core, near, far, 1)
    wide_rows, wide_cols = x_wide.shape[:2]
    x_wide = x_wide.reshape(-1, width)
    go_rows = by_core(core, grad_output, go_partner, 1).reshape(-1, width)
    block_cols = 2 * lon_cols

    bias, hot = window_columns(lat * lat_rows, lat_rows // QROWS, lat_rows * lats, lanes)
    scale = jnp.concatenate(
        [jnp.full((lanes,), LOG2E / math.sqrt(head), jnp.float32), jnp.ones((2 * lanes,), jnp.float32)]
    )

    def project(weights):
        count = weights.shape[1] // per
        result = dot(x_wide, weights) * jnp.tile(scale, count)
        return result.astype(jnp.bfloat16).reshape(wide_rows, wide_cols, -1)

    tn = (((0,), (0,)), ((), ()))
    g = dot(go_rows, out_heads, NT).astype(jnp.bfloat16).reshape(lat_rows, block_cols, half)
    att_0, grads_0 = attention(project(qkv_first), g, bias, hot, 0, 0, lanes)
    grads_0, *rest_parts = lax.optimization_barrier((grads_0, *rest_parts))
    grads_0 = grads_0.reshape(-1, per)
    qkv_rest = gather_rows(rest_parts, chip)
    rest = project(qkv_rest)
    att_1, grads_1 = attention(rest, g, bias, hot, 0, 1, lanes)
    grads_1 = grads_1.reshape(-1, per)
    early = jnp.concatenate([dot(x_wide, grads_0, tn), dot(x_wide, grads_1, tn)], axis=1)
    early, early_moved = scatter_split(early, chip)
    g_last, early, *early_moved = lax.optimization_barrier((g, early, *early_moved))
    early_moved = chip_moves(early_moved)
    att_2, grads_2 = attention(rest, g_last, bias, hot, 1, 2, lanes)
    att_2, grads_2, *early_moved = lax.optimization_barrier((att_2, grads_2, *early_moved))
    grads_2 = grads_2.reshape(-1, per)

    attended = jnp.concatenate([part.reshape(-1, lanes) for part in (att_0, att_1, att_2)], axis=1)
    out_rows = dot(attended, go_rows, tn).reshape(half, 2, half)
    keep = lax.dynamic_index_in_dim(out_rows, core, 1, keepdims=False)
    give = lax.dynamic_index_in_dim(out_rows, 1 - core, 1, keepdims=False).astype(jnp.bfloat16)
    swapped = partner(give)
    late = dot(x_wide, grads_2, tn)
    late = jnp.concatenate([late, by_core(core, keep, swapped.astype(jnp.float32), 0)], axis=1)
    late_kept, late_moved = scatter_split(late, chip)
    late_moved = chip_moves(late_moved)
    pieces = [
        scatter_rest(added(early, early_moved), lat),
        scatter_rest(added(late_kept, late_moved), lat),
    ]

    grads_2 = after(grads_2, late)
    gx = dot(jnp.concatenate([grads_0, grads_1, grads_2], axis=1), jnp.concatenate([qkv_first, qkv_rest], axis=1), NT)
    gx = gx.reshape(wide_rows, 2, half_cols, width)
    keep = lax.dynamic_index_in_dim(gx, core, 1, keepdims=False)
    give = lax.dynamic_index_in_dim(gx, 1 - core, 1, keepdims=False).astype(jnp.bfloat16)
    near = keep + partner(give).astype(jnp.float32)
    middle = jnp.where(core == 0, near[:, MARGIN:], near[:, :lon_cols])
    flank = jnp.where(core == 0, near[:, :MARGIN], near[:, lon_cols:]).astype(jnp.bfloat16)
    flank = routed(flank, lambda a, o: (a, beside(o))).astype(jnp.float32)
    gap = jnp.zeros((wide_rows, lon_cols - MARGIN, width), jnp.float32)
    middle = middle + by_core(core, flank, gap, 1)
    ends = middle.astype(jnp.bfloat16)
    from_below = routed(ends[:RADIUS], lambda a, o: (a - 1, o)).astype(jnp.float32)
    from_above = routed(ends[RADIUS + lat_rows :], lambda a, o: (a + 1, o)).astype(jnp.float32)
    gap = jnp.zeros((lat_rows - 2 * RADIUS, lon_cols, width), jnp.float32)
    grad_x = middle[RADIUS : RADIUS + lat_rows] + jnp.concatenate([from_above, gap, from_below], axis=0)
    grad_x = grad_x.astype(jnp.bfloat16)

    total = jnp.concatenate(pieces, axis=1).reshape(2, rows, -1)
    keep = lax.dynamic_index_in_dim(total, core, 0, keepdims=False)
    give = lax.dynamic_index_in_dim(total, 1 - core, 0, keepdims=False).astype(jnp.bfloat16)
    got = partner(give).astype(jnp.float32)
    order = jnp.where(core == 0, jnp.stack([keep, got]), jnp.stack([got, keep]))
    grad_qkv = order[:, :, : groups * per].reshape(2, rows, groups, 3, lanes)
    grad_qkv = jnp.transpose(grad_qkv, (1, 3, 0, 2, 4)).reshape(rows, 3 * width)
    grad_out = jnp.transpose(order[:, :, groups * per :], (1, 0, 2)).reshape(rows, width)
    return grad_x, grad_qkv, grad_out


def solution(mesh):
    placed = (
        P("lat", "lon", None),
        P("lat", "lon", None),
        P(("lat", "lon"), None),
        P(("lat", "lon"), None),
    )
    return jax.shard_map(
        shards,
        mesh=mesh,
        in_specs=placed,
        out_specs=(P("lat", "lon", None), P(("lat", "lon"), None), P(("lat", "lon"), None)),
        check_vma=False,
    )
```

```python
import math

import jax
import jax.numpy as jnp
from jax import lax
from jax.experimental import pallas as pl
from jax.experimental.pallas import tpu as pltpu
from jax.sharding import PartitionSpec as P

HEADS = 12
RADIUS = 6
QROWS = 16
QCOLS = 16
MARGIN = 8
PAIR = 2
OUTSIDE = -1e30
LOG2E = math.log2(math.e)

NT = (((1,), (1,)), ((), ()))
NN = (((1,), (0,)), ((), ()))


def dot(a, b, dims=NN):
    return lax.dot_general(a, b, dims, preferred_element_type=jnp.float32)


def attention_kernel(p_ref, g_ref, bias_ref, hot_ref, att_ref, grad_ref, *scratch):
    scores, e_both, ds_both, sums = scratch[:PAIR], scratch[PAIR], scratch[PAIR + 1], scratch[PAIR + 2]
    tile_row, tile_col = pl.program_id(0), pl.program_id(1)
    key_rows, key_cols = QROWS + 2 * RADIUS, QCOLS + 2 * MARGIN
    keys, queries = key_rows * key_cols, QROWS * QCOLS
    lanes = g_ref.shape[-1]
    head = lanes // PAIR
    chunk = 64
    first_row = tile_row * QROWS
    first_col = pl.multiple_of(tile_col * QCOLS, QCOLS)
    at_rows, at_cols = pl.ds(first_row, key_rows), pl.ds(first_col, key_cols)
    q_lanes, k_lanes, v_lanes = (slice(i * lanes, (i + 1) * lanes) for i in range(3))
    heads = range(PAIR)
    rows = [slice(h * head, (h + 1) * head) for h in heads]
    cols = [slice(h * queries, (h + 1) * queries) for h in heads]

    @pl.when((tile_row == 0) & (tile_col == 0))
    def _():
        sums[...] = jnp.zeros_like(sums)

    q = p_ref[pl.ds(first_row + RADIUS, QROWS), at_cols, q_lanes].astype(jnp.float32)
    q = q[:, MARGIN : MARGIN + QCOLS].reshape(queries, lanes).astype(jnp.bfloat16)
    g_t = g_ref[...].astype(jnp.float32).T
    k = p_ref[at_rows, at_cols, k_lanes].reshape(keys, lanes)
    v = p_ref[at_rows, at_cols, v_lanes].reshape(keys, lanes)
    k_wide = jnp.concatenate([k, bias_ref[0]], axis=1)
    ones = jnp.ones((16, keys), jnp.bfloat16)
    lane = lax.broadcasted_iota(jnp.int32, (queries, lanes), 1) // head
    q_heads = [jnp.where(lane == h, q, jnp.zeros_like(q)) for h in heads]
    for h in heads:
        scores[h][...] = dot(k_wide, jnp.concatenate([q_heads[h], hot_ref[...]], axis=1), NT)
    k_t, v_t = k.T, v.T
    g_heads, att_t, dq_t, terms = [], [], [], []
    for h in heads:
        top = jnp.max(scores[h][...], axis=0, keepdims=True)
        for c in range(0, keys, chunk):
            e_both[c : c + chunk, cols[h]] = jnp.exp2(scores[h][c : c + chunk] - top).astype(jnp.bfloat16)
        out = dot(jnp.concatenate([v_t[rows[h]], ones], axis=0), e_both[:, cols[h]])
        inverse = 1.0 / out[head : head + 1]
        attended = (out[:head] * inverse).astype(jnp.bfloat16).astype(jnp.float32)
        att_t.append(attended)
        g_one = g_t[rows[h]] * inverse
        terms.append(jnp.sum(g_one * attended, axis=0, keepdims=True))
        empty = jnp.zeros_like(g_one)
        g_one = jnp.concatenate([empty] * h + [g_one] + [empty] * (PAIR - 1 - h), axis=0).astype(jnp.bfloat16)
        g_heads.append(g_one)
    for h in heads:
        scores[h][...] = dot(v, g_heads[h])
    for h in heads:
        for c in range(0, keys, chunk):
            ds_both[c : c + chunk, cols[h]] = (
                e_both[c : c + chunk, cols[h]].astype(jnp.float32) * (scores[h][c : c + chunk] - terms[h])
            ).astype(jnp.bfloat16)
        dq_t.append(dot(k_t[rows[h]], ds_both[:, cols[h]]))
    tile = (key_rows, key_cols, lanes)
    sums[at_rows, at_cols, v_lanes] += dot(e_both[...], jnp.concatenate(g_heads, axis=1), NT).reshape(tile)
    sums[at_rows, at_cols, k_lanes] += dot(ds_both[...], jnp.concatenate(q_heads, axis=0)).reshape(tile)
    att_ref[...] = jnp.concatenate(att_t, axis=0).astype(jnp.bfloat16)
    dq = jnp.concatenate(dq_t, axis=0).T * (1.0 / math.sqrt(head))
    sums[pl.ds(first_row + RADIUS, QROWS), pl.ds(pl.multiple_of(first_col + MARGIN, 8), QCOLS), q_lanes] = dq.reshape(
        QROWS, QCOLS, lanes
    )

    @pl.when((tile_row == pl.num_programs(0) - 1) & (tile_col == pl.num_programs(1) - 1))
    def _():
        grad_ref[:, :, q_lanes] = sums[:, :, q_lanes].astype(jnp.bfloat16)
        grad_ref[:, :, k_lanes] = (sums[:, :, k_lanes] * (1.0 / LOG2E)).astype(jnp.bfloat16)
        grad_ref[:, :, v_lanes] = sums[:, :, v_lanes].astype(jnp.bfloat16)


def attention(projected, g, bias, hot, place, g_place, lanes):
    wide = projected.shape[:2] + (3 * lanes,)
    queries, keys = QROWS * QCOLS, (QROWS + 2 * RADIUS) * (QCOLS + 2 * MARGIN)
    tiles = ((wide[0] - 2 * RADIUS) // QROWS, (wide[1] - 2 * MARGIN) // QCOLS)
    count = tiles[0] * tiles[1]
    return pl.pallas_call(
        attention_kernel,
        grid=tiles,
        in_specs=[
            pl.BlockSpec(wide, lambda r, c: (0, 0, place)),
            pl.BlockSpec((queries, lanes), lambda r, c: (r * tiles[1] + c, g_place)),
            pl.BlockSpec((1, keys, lanes), lambda r, c: (r, 0, 0)),
            pl.BlockSpec((queries, lanes), lambda r, c: (0, 0)),
        ],
        out_specs=[
            pl.BlockSpec((lanes, queries), lambda r, c: (0, r * tiles[1] + c)),
            pl.BlockSpec(wide, lambda r, c: (0, 0, 0)),
        ],
        out_shape=[
            jax.ShapeDtypeStruct((lanes, count * queries), jnp.bfloat16),
            jax.ShapeDtypeStruct(wide, jnp.bfloat16),
        ],
        scratch_shapes=[pltpu.VMEM((keys, queries), jnp.float32)] * PAIR
        + [pltpu.VMEM((keys, PAIR * queries), jnp.bfloat16)] * 2
        + [pltpu.VMEM(wide, jnp.float32)],
        compiler_params=pltpu.CompilerParams(
            dimension_semantics=("arbitrary", "arbitrary"), vmem_limit_bytes=48 * 1024 * 1024
        ),
        cost_estimate=pl.CostEstimate(
            flops=2 * 12 * 256 * keys * queries * PAIR * count,
            bytes_accessed=12 * count * queries * lanes * 2,
            transcendentals=keys * queries * PAIR * count,
        ),
    )(projected, g, bias, hot)


def window_columns(lat_first, tile_rows, total_rows, lanes):
    key_rows, key_cols = QROWS + 2 * RADIUS, QCOLS + 2 * MARGIN
    base = lat_first + QROWS * jnp.arange(tile_rows, dtype=jnp.int32)[:, None, None]
    q_row = base + jnp.arange(QROWS, dtype=jnp.int32)[None, None, :]
    k_row = base - RADIUS + jnp.arange(key_rows, dtype=jnp.int32)[None, :, None]
    start = jnp.clip(q_row - RADIUS, 0, total_rows - 2 * RADIUS - 1)
    row_in = (k_row >= start) & (k_row <= start + 2 * RADIUS)
    q_col = jnp.arange(QCOLS, dtype=jnp.int32)[None, :]
    k_col = jnp.arange(key_cols, dtype=jnp.int32)[:, None] - MARGIN
    col_in = (k_col >= q_col - RADIUS) & (k_col <= q_col + RADIUS)
    shape = (tile_rows, key_rows, key_cols)
    row_part = jnp.broadcast_to(jnp.where(row_in, 0.0, OUTSIDE)[:, :, None, :], shape + (QROWS,))
    col_part = jnp.broadcast_to(jnp.where(col_in, 0.0, OUTSIDE)[None, None], shape + (QCOLS,))
    rest = jnp.zeros(shape + (lanes - QROWS - QCOLS,), jnp.float32)
    columns = jnp.concatenate([row_part, col_part, rest], axis=-1).astype(jnp.bfloat16)
    columns = columns.reshape(tile_rows, key_rows * key_cols, lanes)
    r, c = jnp.arange(QROWS * QCOLS) // QCOLS, jnp.arange(QROWS * QCOLS) % QCOLS
    lane = jnp.arange(lanes)[None, :]
    hot = ((lane == r[:, None]) | (lane == QROWS + c[:, None])).astype(jnp.bfloat16)
    return columns, hot


def routed(value, route):
    lats, lons = lax.axis_size("lat"), lax.axis_size("lon")
    pairs = []
    for a in range(lats):
        for o in range(lons):
            to_lat, to_lon = route(a, o)
            if 0 <= to_lat < lats:
                pairs.append((a * lons + o, to_lat * lons + to_lon % lons))
    return lax.ppermute(value, ("lat", "lon"), pairs)


def partner(value):
    return routed(value, lambda a, o: (a, o ^ 1))


def beside(o):
    return o + 1 if o % 2 else o - 1


def by_core(core, mine, other, axis):
    return jnp.where(
        core == 0, jnp.concatenate([mine, other], axis=axis), jnp.concatenate([other, mine], axis=axis)
    )


def turned(parts, by):
    count = len(parts)
    whole = jnp.zeros((count,) + parts[0].shape, parts[0].dtype)
    for d, part in enumerate(parts):
        whole = lax.dynamic_update_index_in_dim(whole, part, (by - d) % count, 0)
    return whole


def lat_moves(blocks):
    lats = lax.axis_size("lat")
    return [routed(part, lambda a, o, d=d + 1: ((a + d) % lats, o)) for d, part in enumerate(blocks)]


def chip_moves(blocks):
    return [routed(part, lambda a, o, d=d + 1: (a, o + 2 * d)) for d, part in enumerate(blocks)]


def gather_rows(parts, chip):
    grid = turned(parts, chip)
    return jnp.swapaxes(grid, 0, 1).reshape((-1,) + grid.shape[3:])


def pick(value, index, count, dim):
    return lax.dynamic_index_in_dim(value, index % count, dim, keepdims=False)


def scatter_split(totals, chip):
    lats, chips = lax.axis_size("lat"), lax.axis_size("lon") // 2
    totals = [total.reshape(lats, chips, -1, total.shape[1]) for total in totals]
    blocks = [jnp.concatenate([pick(total, chip + d, chips, 1) for total in totals], axis=-1) for d in range(chips)]
    return blocks[0].astype(jnp.float32), blocks[1:]


def added(kept, parts):
    for part in parts:
        kept = kept + part.astype(jnp.float32)
    return kept


def scatter_rest(kept, lat):
    lats = lax.axis_size("lat")
    moved = lat_moves([pick(kept, lat + d, lats, 0).astype(jnp.bfloat16) for d in range(1, lats)])
    return added(pick(kept, lat, lats, 0), moved)


def after(value, *others):
    return lax.optimization_barrier((value,) + others)[0]


def shards(features, grad_output, qkv_weight, out_weight):
    lat_rows, lon_cols, width = features.shape
    head = width // HEADS
    lanes = PAIR * head
    groups = HEADS // PAIR // 2
    half = width // 2
    lats, chips = lax.axis_size("lat"), lax.axis_size("lon") // 2
    lat, lon = lax.axis_index("lat"), lax.axis_index("lon")
    core, chip = lon % 2, lon // 2
    rows = qkv_weight.shape[0]
    per = 3 * lanes
    cells = lat_rows * lon_cols
    block_cols = 2 * lon_cols
    half_cols = lon_cols + MARGIN

    by_heads = qkv_weight.reshape(rows, 3, 2, groups, lanes)
    first = [by_heads[:, i, c, 0] for c in range(2) for i in range(3)]
    first = jnp.concatenate(first + [out_weight], axis=1)
    first = turned([first] + lat_moves([first] * (lats - 1)), lat)
    first = turned([first] + chip_moves([first] * (chips - 1)), chip)
    first = jnp.swapaxes(first, 0, 1).reshape(lats * chips, rows, -1)

    def columns(which):
        qkv = lax.dynamic_index_in_dim(by_heads, which, 2, keepdims=False)[:, :, 1:]
        return jnp.swapaxes(qkv, 1, 2).reshape(rows, -1)

    edge = jnp.where(core == 0, features[:, :MARGIN], features[:, lon_cols - MARGIN :])
    side = routed(edge, lambda a, o: (a, beside(o)))
    both = [features.reshape(cells, width), grad_output.reshape(cells, width), columns(1 - core).reshape(-1, width)]
    both = partner(jnp.concatenate(both, axis=0))
    x_partner = both[:cells].reshape(features.shape)
    go_partner = both[cells : 2 * cells].reshape(features.shape)
    rest = by_core(core, columns(core), both[2 * cells :].reshape(rows, -1), 0)

    near = jnp.where(
        core == 0, jnp.concatenate([side, features], axis=1), jnp.concatenate([features, side], axis=1)
    )
    above = routed(near[lat_rows - RADIUS :], lambda a, o: (a + 1, o))
    below = routed(near[:RADIUS], lambda a, o: (a - 1, o))
    rim = jnp.concatenate([above.reshape(-1, width), below.reshape(-1, width), side.reshape(-1, width)], axis=0)
    rim = partner(rim)
    cap = RADIUS * half_cols
    far_above = rim[:cap].reshape(above.shape)
    far_below = rim[cap : 2 * cap].reshape(below.shape)
    far_side = rim[2 * cap :].reshape(side.shape)
    far = jnp.where(
        core == 0,
        jnp.concatenate([x_partner, far_side], axis=1),
        jnp.concatenate([far_side, x_partner], axis=1),
    )
    near = jnp.concatenate([above, near, below], axis=0)
    far = jnp.concatenate([far_above, far, far_below], axis=0)
    x_wide = by_core(core, near, far, 1)
    wide_rows, wide_cols = x_wide.shape[:2]
    x_wide = x_wide.reshape(-1, width)
    x_turned = lax.optimization_barrier(x_wide.T)
    go = by_core(core, grad_output, go_partner, 1)
    go = go.reshape(lat_rows // QROWS, QROWS, block_cols // QCOLS, QCOLS, width)
    go = lax.optimization_barrier(jnp.swapaxes(go, 1, 2).reshape(-1, width))

    def heads_of(which):
        qkv = lax.dynamic_slice_in_dim(first, which * per, per, 2).reshape(half, per)
        count = lats * chips // 2
        out = lax.dynamic_slice_in_dim(first, which * count, count, 0)[..., 2 * per :].reshape(-1, width)
        return qkv, out

    qkv_mine, out_mine = heads_of(core)
    qkv_other, out_other = heads_of(1 - core)
    cut = out_other.shape[0]
    swap = jnp.concatenate([jnp.concatenate([qkv_other[:cut], qkv_other[cut:]], axis=1), out_other], axis=0)
    swap = partner(swap)
    qkv_got = jnp.concatenate([swap[:cut, :per], swap[:cut, per:]], axis=0)

    def interleaved(mine, got):
        mine, got = (part.reshape(-1, rows, part.shape[1]) for part in (mine, got))
        return by_core(core, mine, got, 1).reshape(-1, mine.shape[2])

    qkv_first = interleaved(qkv_mine, qkv_got)
    out_heads = interleaved(out_mine, swap[cut:])

    bias, hot = window_columns(lat * lat_rows, lat_rows // QROWS, lat_rows * lats, lanes)
    scale = jnp.concatenate(
        [jnp.full((lanes,), LOG2E / math.sqrt(head), jnp.float32), jnp.ones((2 * lanes,), jnp.float32)]
    )

    def project(weights):
        result = dot(x_wide, weights) * jnp.tile(scale, weights.shape[1] // per)
        return result.astype(jnp.bfloat16).reshape(wide_rows, wide_cols, -1)

    def half_rows(grads, which):
        return lax.dynamic_slice_in_dim(grads, which * (grads.shape[0] // 2), grads.shape[0] // 2, 0)

    rest_moved = lat_moves([after(rest, first)] * (lats - 1))
    projected = project(qkv_first)
    g = dot(go, out_heads, NT).astype(jnp.bfloat16)
    projected, g, *rest_moved = lax.optimization_barrier((projected, g, *rest_moved))
    rest = turned([rest] + rest_moved, lat)
    rest_moved = chip_moves([rest] * (chips - 1))
    att_0, grads_0 = attention(projected, g, bias, hot, 0, 0, lanes)
    grads_0, *rest_moved = lax.optimization_barrier((grads_0, *rest_moved))
    qkv_rest = gather_rows([rest] + rest_moved, chip)
    projected = project(qkv_rest)
    att_1, grads_1 = attention(projected, g, bias, hot, 0, 1, lanes)

    grads_0, grads_1 = grads_0.reshape(-1, per), grads_1.reshape(-1, per)
    early = [dot(x_turned, part).astype(jnp.bfloat16) for part in (grads_0, grads_1)]
    early_kept, early_moved = scatter_split(early, chip)

    def gx_early(which):
        return dot(half_rows(grads_0, which), qkv_first, NT) + dot(half_rows(grads_1, which), qkv_rest[:, :per], NT)

    give_early, keep_early = gx_early(1 - core), gx_early(core)
    out_rows = [dot(part, go).astype(jnp.bfloat16) for part in (att_0, att_1)]
    g, early_kept, give_early, keep_early, *early_moved, = lax.optimization_barrier(
        (g, early_kept, give_early, keep_early, *early_moved)
    )
    early_moved = chip_moves(early_moved)
    att_2, grads_2 = attention(projected, g, bias, hot, 1, 2, lanes)
    att_2, grads_2, *early_moved = lax.optimization_barrier((att_2, grads_2, *early_moved))
    grads_2 = grads_2.reshape(-1, per)

    def gx_late(which, before):
        return dot(half_rows(grads_2, which), qkv_rest[:, per:], NT) + before

    out_rows.append(dot(att_2, go).astype(jnp.bfloat16))
    out_rows = jnp.concatenate(out_rows, axis=0)
    swapped = partner(lax.dynamic_slice_in_dim(out_rows, (1 - core) * half, half, 1))
    give = gx_late(1 - core, give_early).astype(jnp.bfloat16)
    given = partner(give)
    late = dot(x_turned, after(grads_2, give)).astype(jnp.bfloat16)
    out_mine = by_core(core, lax.dynamic_slice_in_dim(out_rows, core * half, half, 1), swapped, 0)
    late_kept, late_moved = scatter_split([late, out_mine], chip)
    late_moved = chip_moves(late_moved)
    early_total = scatter_rest(added(early_kept, early_moved), lat)
    gx = gx_late(core, after(keep_early, give)) + given.astype(jnp.float32)
    gx = gx.reshape(wide_rows // 2, wide_cols, width)
    own = wide_rows // 2 - RADIUS
    outer = jnp.where(core == 0, gx[:RADIUS], gx[own:]).astype(jnp.bfloat16)
    gx = jnp.where(core == 0, gx[RADIUS:], gx[:own])
    outer, gx, late_kept, early_total, *late_moved = lax.optimization_barrier(
        (outer, gx, late_kept, early_total, *late_moved)
    )
    inner = routed(outer, lambda a, o: (a + 1, o - 1) if o % 2 else (a - 1, o + 1)).astype(jnp.float32)
    late_total = scatter_rest(added(late_kept, late_moved), lat)
    inner, gx, late_total, early_total = lax.optimization_barrier((inner, gx, late_total, early_total))
    gap = jnp.zeros((own - RADIUS,) + gx.shape[1:], jnp.float32)
    gx = gx + by_core(core, inner, gap, 0)
    other_half = lax.dynamic_slice_in_dim(gx, MARGIN + (1 - core) * lon_cols, lon_cols, 1)
    mine_half = lax.dynamic_slice_in_dim(gx, MARGIN + core * lon_cols, lon_cols, 1)
    left, right = gx[:, :MARGIN].astype(jnp.bfloat16), gx[:, wide_cols - MARGIN :].astype(jnp.bfloat16)
    same = routed(jnp.where(core == 0, right, left), lambda a, o: (a, o - 2 if o % 2 else o + 2))
    cross = routed(jnp.where(core == 0, left, right), lambda a, o: (a, o + 1 if o % 2 else o - 1))
    swapped_x = partner(other_half.astype(jnp.bfloat16))
    pad = jnp.zeros((own, lon_cols - MARGIN, width), jnp.float32)
    here = mine_half + by_core(core, same.astype(jnp.float32), pad, 1)
    there = swapped_x.astype(jnp.float32) + by_core(core, cross.astype(jnp.float32), pad, 1)
    grad_x = by_core(core, here.astype(jnp.bfloat16), there.astype(jnp.bfloat16), 0)

    total = jnp.concatenate([early_total, late_total], axis=1).reshape(2, rows, -1)
    keep = lax.dynamic_index_in_dim(total, core, 0, keepdims=False)
    give = lax.dynamic_index_in_dim(total, 1 - core, 0, keepdims=False).astype(jnp.bfloat16)
    got = partner(give).astype(jnp.float32)
    order = jnp.where(core == 0, jnp.stack([keep, got]), jnp.stack([got, keep]))
    grad_qkv = order[:, :, : groups * per].reshape(2, rows, groups, 3, lanes)
    grad_qkv = jnp.transpose(grad_qkv, (1, 3, 0, 2, 4)).reshape(rows, 3 * width)
    grad_out = jnp.transpose(order[:, :, groups * per :], (1, 0, 2)).reshape(rows, width)
    return grad_x, grad_qkv, grad_out


def solution(mesh):
    placed = (
        P("lat", "lon", None),
        P("lat", "lon", None),
        P(("lat", "lon"), None),
        P(("lat", "lon"), None),
    )
    return jax.shard_map(
        shards,
        mesh=mesh,
        in_specs=placed,
        out_specs=(P("lat", "lon", None), P(("lat", "lon"), None), P(("lat", "lon"), None)),
        check_vma=False,
    )
```

```python
import math

import jax
import jax.numpy as jnp
from jax import lax
from jax.experimental import pallas as pl
from jax.experimental.pallas import tpu as pltpu
from jax.sharding import PartitionSpec as P

HEADS = 12
RADIUS = 6
QROWS = 16
QCOLS = 16
MARGIN = 8
PAIR = 2
OUTSIDE = -1e30
LOG2E = math.log2(math.e)

NT = (((1,), (1,)), ((), ()))
NN = (((1,), (0,)), ((), ()))


def dot(a, b, dims=NN):
    return lax.dot_general(a, b, dims, preferred_element_type=jnp.float32)


def attention_kernel(p_ref, g_ref, bias_ref, hot_ref, att_ref, grad_ref, *scratch):
    scores, e_both, ds_both, sums = scratch[:PAIR], scratch[PAIR], scratch[PAIR + 1], scratch[PAIR + 2]
    tile_row, tile_col = pl.program_id(0), pl.program_id(1)
    key_rows, key_cols = QROWS + 2 * RADIUS, QCOLS + 2 * MARGIN
    keys, queries = key_rows * key_cols, QROWS * QCOLS
    lanes = g_ref.shape[-1]
    head = lanes // PAIR
    chunk = 64
    first_row = tile_row * QROWS
    first_col = pl.multiple_of(tile_col * QCOLS, QCOLS)
    at_rows, at_cols = pl.ds(first_row, key_rows), pl.ds(first_col, key_cols)
    q_lanes, k_lanes, v_lanes = (slice(i * lanes, (i + 1) * lanes) for i in range(3))
    heads = range(PAIR)
    rows = [slice(h * head, (h + 1) * head) for h in heads]
    cols = [slice(h * queries, (h + 1) * queries) for h in heads]

    @pl.when((tile_row == 0) & (tile_col == 0))
    def _():
        sums[...] = jnp.zeros_like(sums)

    q = p_ref[pl.ds(first_row + RADIUS, QROWS), at_cols, q_lanes].astype(jnp.float32)
    q = q[:, MARGIN : MARGIN + QCOLS].reshape(queries, lanes).astype(jnp.bfloat16)
    g_t = g_ref[...].astype(jnp.float32).T
    k = p_ref[at_rows, at_cols, k_lanes].reshape(keys, lanes)
    v = p_ref[at_rows, at_cols, v_lanes].reshape(keys, lanes)
    k_wide = jnp.concatenate([k, bias_ref[0]], axis=1)
    ones = jnp.ones((16, keys), jnp.bfloat16)
    lane = lax.broadcasted_iota(jnp.int32, (queries, lanes), 1) // head
    q_heads = [jnp.where(lane == h, q, jnp.zeros_like(q)) for h in heads]
    for h in heads:
        scores[h][...] = dot(k_wide, jnp.concatenate([q_heads[h], hot_ref[...]], axis=1), NT)
    k_t, v_t = k.T, v.T
    g_heads, att_t, dq_t, terms = [], [], [], []
    for h in heads:
        top = jnp.max(scores[h][...], axis=0, keepdims=True)
        for c in range(0, keys, chunk):
            e_both[c : c + chunk, cols[h]] = jnp.exp2(scores[h][c : c + chunk] - top).astype(jnp.bfloat16)
        out = dot(jnp.concatenate([v_t[rows[h]], ones], axis=0), e_both[:, cols[h]])
        inverse = 1.0 / out[head : head + 1]
        attended = (out[:head] * inverse).astype(jnp.bfloat16).astype(jnp.float32)
        att_t.append(attended)
        g_one = g_t[rows[h]] * inverse
        terms.append(jnp.sum(g_one * attended, axis=0, keepdims=True))
        empty = jnp.zeros_like(g_one)
        g_one = jnp.concatenate([empty] * h + [g_one] + [empty] * (PAIR - 1 - h), axis=0).astype(jnp.bfloat16)
        g_heads.append(g_one)
    for h in heads:
        scores[h][...] = dot(v, g_heads[h])
    for h in heads:
        for c in range(0, keys, chunk):
            ds_both[c : c + chunk, cols[h]] = (
                e_both[c : c + chunk, cols[h]].astype(jnp.float32) * (scores[h][c : c + chunk] - terms[h])
            ).astype(jnp.bfloat16)
        dq_t.append(dot(k_t[rows[h]], ds_both[:, cols[h]]))
    tile = (key_rows, key_cols, lanes)
    sums[at_rows, at_cols, v_lanes] += dot(e_both[...], jnp.concatenate(g_heads, axis=1), NT).reshape(tile)
    sums[at_rows, at_cols, k_lanes] += dot(ds_both[...], jnp.concatenate(q_heads, axis=0)).reshape(tile)
    att_ref[...] = jnp.concatenate(att_t, axis=0).astype(jnp.bfloat16)
    dq = jnp.concatenate(dq_t, axis=0).T * (1.0 / math.sqrt(head))
    sums[pl.ds(first_row + RADIUS, QROWS), pl.ds(pl.multiple_of(first_col + MARGIN, 8), QCOLS), q_lanes] = dq.reshape(
        QROWS, QCOLS, lanes
    )

    @pl.when((tile_row == pl.num_programs(0) - 1) & (tile_col == pl.num_programs(1) - 1))
    def _():
        grad_ref[:, :, q_lanes] = sums[:, :, q_lanes].astype(jnp.bfloat16)
        grad_ref[:, :, k_lanes] = (sums[:, :, k_lanes] * (1.0 / LOG2E)).astype(jnp.bfloat16)
        grad_ref[:, :, v_lanes] = sums[:, :, v_lanes].astype(jnp.bfloat16)


def attention(projected, g, bias, hot, place, g_place, lanes):
    wide = projected.shape[:2] + (3 * lanes,)
    queries, keys = QROWS * QCOLS, (QROWS + 2 * RADIUS) * (QCOLS + 2 * MARGIN)
    tiles = ((wide[0] - 2 * RADIUS) // QROWS, (wide[1] - 2 * MARGIN) // QCOLS)
    count = tiles[0] * tiles[1]
    return pl.pallas_call(
        attention_kernel,
        grid=tiles,
        in_specs=[
            pl.BlockSpec(wide, lambda r, c: (0, 0, place)),
            pl.BlockSpec((queries, lanes), lambda r, c: (r * tiles[1] + c, g_place)),
            pl.BlockSpec((1, keys, lanes), lambda r, c: (r, 0, 0)),
            pl.BlockSpec((queries, lanes), lambda r, c: (0, 0)),
        ],
        out_specs=[
            pl.BlockSpec((lanes, queries), lambda r, c: (0, r * tiles[1] + c)),
            pl.BlockSpec(wide, lambda r, c: (0, 0, 0)),
        ],
        out_shape=[
            jax.ShapeDtypeStruct((lanes, count * queries), jnp.bfloat16),
            jax.ShapeDtypeStruct(wide, jnp.bfloat16),
        ],
        scratch_shapes=[pltpu.VMEM((keys, queries), jnp.float32)] * PAIR
        + [pltpu.VMEM((keys, PAIR * queries), jnp.bfloat16)] * 2
        + [pltpu.VMEM(wide, jnp.float32)],
        compiler_params=pltpu.CompilerParams(
            dimension_semantics=("arbitrary", "arbitrary"), vmem_limit_bytes=48 * 1024 * 1024
        ),
        cost_estimate=pl.CostEstimate(
            flops=2 * 12 * 256 * keys * queries * PAIR * count,
            bytes_accessed=12 * count * queries * lanes * 2,
            transcendentals=keys * queries * PAIR * count,
        ),
    )(projected, g, bias, hot)


def window_columns(lat_first, tile_rows, total_rows, lanes):
    key_rows, key_cols = QROWS + 2 * RADIUS, QCOLS + 2 * MARGIN
    base = lat_first + QROWS * jnp.arange(tile_rows, dtype=jnp.int32)[:, None, None]
    q_row = base + jnp.arange(QROWS, dtype=jnp.int32)[None, None, :]
    k_row = base - RADIUS + jnp.arange(key_rows, dtype=jnp.int32)[None, :, None]
    start = jnp.clip(q_row - RADIUS, 0, total_rows - 2 * RADIUS - 1)
    row_in = (k_row >= start) & (k_row <= start + 2 * RADIUS)
    q_col = jnp.arange(QCOLS, dtype=jnp.int32)[None, :]
    k_col = jnp.arange(key_cols, dtype=jnp.int32)[:, None] - MARGIN
    col_in = (k_col >= q_col - RADIUS) & (k_col <= q_col + RADIUS)
    shape = (tile_rows, key_rows, key_cols)
    row_part = jnp.broadcast_to(jnp.where(row_in, 0.0, OUTSIDE)[:, :, None, :], shape + (QROWS,))
    col_part = jnp.broadcast_to(jnp.where(col_in, 0.0, OUTSIDE)[None, None], shape + (QCOLS,))
    rest = jnp.zeros(shape + (lanes - QROWS - QCOLS,), jnp.float32)
    columns = jnp.concatenate([row_part, col_part, rest], axis=-1).astype(jnp.bfloat16)
    columns = columns.reshape(tile_rows, key_rows * key_cols, lanes)
    r, c = jnp.arange(QROWS * QCOLS) // QCOLS, jnp.arange(QROWS * QCOLS) % QCOLS
    lane = jnp.arange(lanes)[None, :]
    hot = ((lane == r[:, None]) | (lane == QROWS + c[:, None])).astype(jnp.bfloat16)
    return columns, hot


def routed(value, route):
    lats, lons = lax.axis_size("lat"), lax.axis_size("lon")
    pairs = []
    for a in range(lats):
        for o in range(lons):
            to_lat, to_lon = route(a, o)
            if 0 <= to_lat < lats:
                pairs.append((a * lons + o, to_lat * lons + to_lon % lons))
    return lax.ppermute(value, ("lat", "lon"), pairs)


def partner(value):
    return routed(value, lambda a, o: (a, o ^ 1))


def beside(o):
    return o + 1 if o % 2 else o - 1


def by_core(core, mine, other, axis):
    return jnp.where(
        core == 0, jnp.concatenate([mine, other], axis=axis), jnp.concatenate([other, mine], axis=axis)
    )


def over_lat(value):
    return lax.all_to_all(value, "lat", 0, 0)


def over_chips(value, axis=0):
    count = lax.axis_size("lon")
    same_core = [list(range(c, count, 2)) for c in range(2)]
    return lax.all_to_all(value, "lon", axis, axis, axis_index_groups=same_core)


def copies(value, count):
    return jnp.broadcast_to(value[None], (count,) + value.shape)


def chip_moves(blocks):
    return [routed(part, lambda a, o, d=d + 1: (a, o + 2 * d)) for d, part in enumerate(blocks)]


def ordered(parts, by):
    count = len(parts)
    whole = jnp.zeros((count,) + parts[0].shape, parts[0].dtype)
    for d, part in enumerate(parts):
        whole = lax.dynamic_update_index_in_dim(whole, part, (by - d) % count, 0)
    return whole


def pick(value, index, count, dim):
    return lax.dynamic_index_in_dim(value, index % count, dim, keepdims=False)


def after(value, *others):
    return lax.optimization_barrier((value,) + others)[0]


def shards(features, grad_output, qkv_weight, out_weight):
    lat_rows, lon_cols, width = features.shape
    head = width // HEADS
    lanes = PAIR * head
    groups = HEADS // PAIR // 2
    half = width // 2
    lats, chips = lax.axis_size("lat"), lax.axis_size("lon") // 2
    lat, lon = lax.axis_index("lat"), lax.axis_index("lon")
    core, chip = lon % 2, lon // 2
    rows = qkv_weight.shape[0]
    per = 3 * lanes
    cells = lat_rows * lon_cols
    block_cols = 2 * lon_cols
    half_cols = lon_cols + MARGIN

    def columns_of(pair, which):
        at = [i * width + which * half + pair * lanes for i in range(3)]
        return [qkv_weight[:, i : i + lanes] for i in at]

    edge = jnp.where(core == 0, features[:, :MARGIN], features[:, lon_cols - MARGIN :])
    side = routed(edge, lambda a, o: (a, beside(o)))
    weights = columns_of(0, 0) + columns_of(0, 1) + [out_weight]
    for c in range(2):
        for m in range(1, groups):
            weights += columns_of(m, c)
    weights = jnp.concatenate(weights, axis=1)
    split = 2 * per + width
    weights = over_lat(copies(weights, lats))

    both = [features.reshape(cells, width), grad_output.reshape(cells, width), side.reshape(-1, width)]
    both = partner(after(jnp.concatenate(both, axis=0), weights))
    x_partner = both[:cells].reshape(features.shape)
    go_partner = both[cells : 2 * cells].reshape(features.shape)
    side_partner = both[2 * cells :].reshape(side.shape)

    def flanked(block, flank, first):
        return jnp.where(
            first, jnp.concatenate([flank, block], axis=1), jnp.concatenate([block, flank], axis=1)
        )

    middle = by_core(core, flanked(features, side, core == 0), flanked(x_partner, side_partner, core == 1), 1)
    ends = jnp.where(core == 0, middle[lat_rows - RADIUS :], middle[:RADIUS])
    cap = routed(ends, lambda a, o: (a - 1, o) if o % 2 else (a + 1, o))
    first = over_chips(copies(after(weights[..., :split], ends), chips))
    cap, first = lax.optimization_barrier((cap, first))
    cap_partner = partner(cap)
    x_wide = jnp.concatenate(
        [jnp.where(core == 0, cap, cap_partner), middle, jnp.where(core == 0, cap_partner, cap)], axis=0
    )
    wide_rows, wide_cols = x_wide.shape[:2]
    x_wide = x_wide.reshape(-1, width)
    x_turned = lax.optimization_barrier(x_wide.T)
    go = by_core(core, grad_output, go_partner, 1)
    go = go.reshape(lat_rows // QROWS, QROWS, block_cols // QCOLS, QCOLS, width)
    go = lax.optimization_barrier(jnp.swapaxes(go, 1, 2).reshape(-1, width))

    def in_rows(grid):
        return jnp.swapaxes(grid, 0, 1).reshape(lats * chips, rows, -1)

    def interleaved(mine, got):
        mine, got = (part.reshape(-1, rows, part.shape[-1]) for part in (mine, got))
        return by_core(core, mine, got, 1).reshape(-1, mine.shape[2])

    first = in_rows(first)

    def heads_of(which):
        qkv = lax.dynamic_slice_in_dim(first, which * per, per, 2).reshape(half, per)
        count = lats * chips // 2
        out = lax.dynamic_slice_in_dim(first, which * count, count, 0)[..., 2 * per :].reshape(-1, width)
        return qkv, out

    qkv_mine, out_mine = heads_of(core)
    qkv_other, out_other = heads_of(1 - core)
    cut = out_other.shape[0]
    swap = jnp.concatenate([jnp.concatenate([qkv_other[:cut], qkv_other[cut:]], axis=1), out_other], axis=0)
    swap = partner(swap)
    qkv_got = jnp.concatenate([swap[:cut, :per], swap[:cut, per:]], axis=0)
    qkv_first = interleaved(qkv_mine, qkv_got)
    out_heads = interleaved(out_mine, swap[cut:])

    bias, hot = window_columns(lat * lat_rows, lat_rows // QROWS, lat_rows * lats, lanes)
    scale = jnp.concatenate(
        [jnp.full((lanes,), LOG2E / math.sqrt(head), jnp.float32), jnp.ones((2 * lanes,), jnp.float32)]
    )

    def project(weights):
        result = dot(x_wide, weights) * jnp.tile(scale, weights.shape[1] // per)
        return result.astype(jnp.bfloat16).reshape(wide_rows, wide_cols, -1)

    def half_rows(grads, which):
        return lax.dynamic_slice_in_dim(grads, which * (grads.shape[0] // 2), grads.shape[0] // 2, 0)

    projected = project(qkv_first)
    g = dot(go, out_heads, NT).astype(jnp.bfloat16)
    projected, g, rest = lax.optimization_barrier((projected, g, weights[..., split:]))
    rest_moved = chip_moves([rest] * (chips - 1))
    att_0, grads_0 = attention(projected, g, bias, hot, 0, 0, lanes)
    att_0, grads_0, *rest_moved = lax.optimization_barrier((att_0, grads_0, *rest_moved))
    rest = in_rows(ordered([rest] + rest_moved, chip)).reshape(half, -1)
    later = (groups - 1) * per
    rest_got = partner(lax.dynamic_slice_in_dim(rest, (1 - core) * later, later, 1))
    early_0 = dot(x_turned, grads_0.reshape(-1, per)).astype(jnp.bfloat16)
    out_0 = dot(att_0, go).astype(jnp.bfloat16)
    early_0, out_0, rest_got = lax.optimization_barrier((early_0, out_0, rest_got))
    qkv_rest = interleaved(lax.dynamic_slice_in_dim(rest, core * later, later, 1), rest_got)
    projected = project(qkv_rest)
    att_1, grads_1 = attention(projected, g, bias, hot, 0, 1, lanes)

    grads_0, grads_1 = grads_0.reshape(-1, per), grads_1.reshape(-1, per)
    early = [early_0, dot(x_turned, grads_1).astype(jnp.bfloat16)]
    early = [total.reshape(lats, chips, -1, per) for total in early]
    early = [jnp.concatenate([pick(total, chip + d, chips, 1) for total in early], axis=-1) for d in range(chips)]
    early_kept, early_moved = early[0], early[1:]

    def gx_early(which):
        return dot(half_rows(grads_0, which), qkv_first, NT) + dot(half_rows(grads_1, which), qkv_rest[:, :per], NT)

    give_early, keep_early = gx_early(1 - core), gx_early(core)
    out_rows = [out_0, dot(att_1, go).astype(jnp.bfloat16)]
    g, early_kept, give_early, keep_early, *early_moved, = lax.optimization_barrier(
        (g, early_kept, give_early, keep_early, *early_moved)
    )
    early_moved = chip_moves(early_moved)
    att_2, grads_2 = attention(projected, g, bias, hot, 1, 2, lanes)
    att_2, grads_2, *early_moved = lax.optimization_barrier((att_2, grads_2, *early_moved))
    grads_2 = grads_2.reshape(-1, per)

    def gx_late(which, before):
        return dot(half_rows(grads_2, which), qkv_rest[:, per:], NT) + before

    out_rows.append(dot(att_2, go).astype(jnp.bfloat16))
    out_rows = jnp.concatenate(out_rows, axis=0)
    swapped = partner(lax.dynamic_slice_in_dim(out_rows, (1 - core) * half, half, 1))
    give = gx_late(1 - core, give_early).astype(jnp.bfloat16)
    given = partner(give)
    late = dot(x_turned, after(grads_2, give)).astype(jnp.bfloat16)
    out_mine = by_core(core, lax.dynamic_slice_in_dim(out_rows, core * half, half, 1), swapped, 0)
    late = jnp.concatenate([late, out_mine], axis=1).reshape(lats, chips, -1, late.shape[1] + half)
    gx = gx_late(core, after(keep_early, give)) + given.astype(jnp.float32)
    gx = gx.reshape(wide_rows // 2, wide_cols, width)
    own = wide_rows // 2 - RADIUS
    outer = jnp.where(core == 0, gx[:RADIUS], gx[own:]).astype(jnp.bfloat16)
    gx = jnp.where(core == 0, gx[RADIUS:], gx[:own])
    inner = routed(outer, lambda a, o: (a + 1, o - 1) if o % 2 else (a - 1, o + 1))
    late = over_chips(after(late, outer), 1)
    late = jnp.sum(late.astype(jnp.float32), axis=1)
    early = early_kept.astype(jnp.float32)
    for part in early_moved:
        early = early + part.astype(jnp.float32)
    total = jnp.concatenate([early, late], axis=-1).astype(jnp.bfloat16)
    inner, total = lax.optimization_barrier((inner, total))
    inner = inner.astype(jnp.float32)
    gap = jnp.zeros((own - RADIUS,) + gx.shape[1:], jnp.float32)
    gx = gx + by_core(core, inner, gap, 0)
    other_half = lax.dynamic_slice_in_dim(gx, MARGIN + (1 - core) * lon_cols, lon_cols, 1)
    mine_half = lax.dynamic_slice_in_dim(gx, MARGIN + core * lon_cols, lon_cols, 1)
    left, right = gx[:, :MARGIN].astype(jnp.bfloat16), gx[:, wide_cols - MARGIN :].astype(jnp.bfloat16)
    same = routed(jnp.where(core == 0, right, left), lambda a, o: (a, o - 2 if o % 2 else o + 2))
    cross = routed(jnp.where(core == 0, left, right), lambda a, o: (a, o + 1 if o % 2 else o - 1))
    swapped_x = partner(other_half.astype(jnp.bfloat16))
    pad = jnp.zeros((own, lon_cols - MARGIN, width), jnp.float32)
    here = mine_half + by_core(core, same.astype(jnp.float32), pad, 1)
    there = swapped_x.astype(jnp.float32) + by_core(core, cross.astype(jnp.float32), pad, 1)
    grad_x = by_core(core, here.astype(jnp.bfloat16), there.astype(jnp.bfloat16), 0)

    total = jnp.sum(over_lat(after(total, other_half)).astype(jnp.float32), axis=0).reshape(2, rows, -1)
    keep = lax.dynamic_index_in_dim(total, core, 0, keepdims=False)
    give = lax.dynamic_index_in_dim(total, 1 - core, 0, keepdims=False).astype(jnp.bfloat16)
    got = partner(give).astype(jnp.float32)
    by_cores = (jnp.where(core == 0, keep, got), jnp.where(core == 0, got, keep))
    places = [(i, c, m) for i in range(3) for c in range(2) for m in range(groups)]
    grad_qkv = [by_cores[c][:, m * per + i * lanes : m * per + (i + 1) * lanes] for i, c, m in places]
    grad_qkv = jnp.concatenate(grad_qkv, axis=1)
    grad_out = jnp.concatenate([part[:, groups * per :] for part in by_cores], axis=1)
    return grad_x, grad_qkv, grad_out


def solution(mesh):
    placed = (
        P("lat", "lon", None),
        P("lat", "lon", None),
        P(("lat", "lon"), None),
        P(("lat", "lon"), None),
    )
    return jax.shard_map(
        shards,
        mesh=mesh,
        in_specs=placed,
        out_specs=(P("lat", "lon", None), P(("lat", "lon"), None), P(("lat", "lon"), None)),
        check_vma=False,
    )
```

```python
import math

import jax
import jax.numpy as jnp
from jax import lax
from jax.experimental import pallas as pl
from jax.experimental.pallas import tpu as pltpu
from jax.sharding import PartitionSpec as P

HEADS = 12
RADIUS = 6
QROWS = 16
QCOLS = 16
MARGIN = 8
PAIR = 2
OUTSIDE = -1e30
LOG2E = math.log2(math.e)

NT = (((1,), (1,)), ((), ()))
NN = (((1,), (0,)), ((), ()))


def dot(a, b, dims=NN):
    return lax.dot_general(a, b, dims, preferred_element_type=jnp.float32)


def attention_kernel(p_ref, g_ref, bias_ref, hot_ref, att_ref, grad_ref, *scratch):
    scores, e_both, ds_both, sums = scratch[:PAIR], scratch[PAIR], scratch[PAIR + 1], scratch[PAIR + 2]
    tile_row, tile_col = pl.program_id(0), pl.program_id(1)
    key_rows, key_cols = QROWS + 2 * RADIUS, QCOLS + 2 * MARGIN
    keys, queries = key_rows * key_cols, QROWS * QCOLS
    lanes = g_ref.shape[-1]
    head = lanes // PAIR
    chunk = 64
    first_row = tile_row * QROWS
    first_col = pl.multiple_of(tile_col * QCOLS, QCOLS)
    at_rows, at_cols = pl.ds(first_row, key_rows), pl.ds(first_col, key_cols)
    q_lanes, k_lanes, v_lanes = (slice(i * lanes, (i + 1) * lanes) for i in range(3))
    heads = range(PAIR)
    rows = [slice(h * head, (h + 1) * head) for h in heads]
    cols = [slice(h * queries, (h + 1) * queries) for h in heads]

    @pl.when((tile_row == 0) & (tile_col == 0))
    def _():
        sums[...] = jnp.zeros_like(sums)

    q = p_ref[pl.ds(first_row + RADIUS, QROWS), at_cols, q_lanes].astype(jnp.float32)
    q = q[:, MARGIN : MARGIN + QCOLS].reshape(queries, lanes).astype(jnp.bfloat16)
    g_t = g_ref[...].astype(jnp.float32).T
    k = p_ref[at_rows, at_cols, k_lanes].reshape(keys, lanes)
    v = p_ref[at_rows, at_cols, v_lanes].reshape(keys, lanes)
    k_wide = jnp.concatenate([k, bias_ref[0]], axis=1)
    ones = jnp.ones((16, keys), jnp.bfloat16)
    lane = lax.broadcasted_iota(jnp.int32, (queries, lanes), 1) // head
    q_heads = [jnp.where(lane == h, q, jnp.zeros_like(q)) for h in heads]
    for h in heads:
        scores[h][...] = dot(k_wide, jnp.concatenate([q_heads[h], hot_ref[...]], axis=1), NT)
    k_t, v_t = k.T, v.T
    g_heads, att_t, dq_t, terms = [], [], [], []
    for h in heads:
        top = jnp.max(scores[h][...], axis=0, keepdims=True)
        for c in range(0, keys, chunk):
            e_both[c : c + chunk, cols[h]] = jnp.exp2(scores[h][c : c + chunk] - top).astype(jnp.bfloat16)
        out = dot(jnp.concatenate([v_t[rows[h]], ones], axis=0), e_both[:, cols[h]])
        inverse = 1.0 / out[head : head + 1]
        attended = (out[:head] * inverse).astype(jnp.bfloat16).astype(jnp.float32)
        att_t.append(attended)
        g_one = g_t[rows[h]] * inverse
        terms.append(jnp.sum(g_one * attended, axis=0, keepdims=True))
        empty = jnp.zeros_like(g_one)
        g_one = jnp.concatenate([empty] * h + [g_one] + [empty] * (PAIR - 1 - h), axis=0).astype(jnp.bfloat16)
        g_heads.append(g_one)
    for h in heads:
        scores[h][...] = dot(v, g_heads[h])
    for h in heads:
        for c in range(0, keys, chunk):
            ds_both[c : c + chunk, cols[h]] = (
                e_both[c : c + chunk, cols[h]].astype(jnp.float32) * (scores[h][c : c + chunk] - terms[h])
            ).astype(jnp.bfloat16)
        dq_t.append(dot(k_t[rows[h]], ds_both[:, cols[h]]))
    tile = (key_rows, key_cols, lanes)
    sums[at_rows, at_cols, v_lanes] += dot(e_both[...], jnp.concatenate(g_heads, axis=1), NT).reshape(tile)
    sums[at_rows, at_cols, k_lanes] += dot(ds_both[...], jnp.concatenate(q_heads, axis=0)).reshape(tile)
    att_ref[...] = jnp.concatenate(att_t, axis=0).astype(jnp.bfloat16)
    dq = jnp.concatenate(dq_t, axis=0).T * (1.0 / math.sqrt(head))
    sums[pl.ds(first_row + RADIUS, QROWS), pl.ds(pl.multiple_of(first_col + MARGIN, 8), QCOLS), q_lanes] = dq.reshape(
        QROWS, QCOLS, lanes
    )

    @pl.when((tile_row == pl.num_programs(0) - 1) & (tile_col == pl.num_programs(1) - 1))
    def _():
        grad_ref[:, :, q_lanes] = sums[:, :, q_lanes].astype(jnp.bfloat16)
        grad_ref[:, :, k_lanes] = (sums[:, :, k_lanes] * (1.0 / LOG2E)).astype(jnp.bfloat16)
        grad_ref[:, :, v_lanes] = sums[:, :, v_lanes].astype(jnp.bfloat16)


def attention(projected, g, bias, hot, place, g_place, lanes):
    wide = projected.shape[:2] + (3 * lanes,)
    queries, keys = QROWS * QCOLS, (QROWS + 2 * RADIUS) * (QCOLS + 2 * MARGIN)
    tiles = ((wide[0] - 2 * RADIUS) // QROWS, (wide[1] - 2 * MARGIN) // QCOLS)
    count = tiles[0] * tiles[1]
    return pl.pallas_call(
        attention_kernel,
        grid=tiles,
        in_specs=[
            pl.BlockSpec(wide, lambda r, c: (0, 0, place)),
            pl.BlockSpec((queries, lanes), lambda r, c: (r * tiles[1] + c, g_place)),
            pl.BlockSpec((1, keys, lanes), lambda r, c: (r, 0, 0)),
            pl.BlockSpec((queries, lanes), lambda r, c: (0, 0)),
        ],
        out_specs=[
            pl.BlockSpec((lanes, queries), lambda r, c: (0, r * tiles[1] + c)),
            pl.BlockSpec(wide, lambda r, c: (0, 0, 0)),
        ],
        out_shape=[
            jax.ShapeDtypeStruct((lanes, count * queries), jnp.bfloat16),
            jax.ShapeDtypeStruct(wide, jnp.bfloat16),
        ],
        scratch_shapes=[pltpu.VMEM((keys, queries), jnp.float32)] * PAIR
        + [pltpu.VMEM((keys, PAIR * queries), jnp.bfloat16)] * 2
        + [pltpu.VMEM(wide, jnp.float32)],
        compiler_params=pltpu.CompilerParams(
            dimension_semantics=("arbitrary", "arbitrary"), vmem_limit_bytes=48 * 1024 * 1024
        ),
        cost_estimate=pl.CostEstimate(
            flops=2 * 12 * 256 * keys * queries * PAIR * count,
            bytes_accessed=12 * count * queries * lanes * 2,
            transcendentals=keys * queries * PAIR * count,
        ),
    )(projected, g, bias, hot)


def window_columns(lat_first, tile_rows, total_rows, lanes):
    key_rows, key_cols = QROWS + 2 * RADIUS, QCOLS + 2 * MARGIN
    base = lat_first + QROWS * jnp.arange(tile_rows, dtype=jnp.int32)[:, None, None]
    q_row = base + jnp.arange(QROWS, dtype=jnp.int32)[None, None, :]
    k_row = base - RADIUS + jnp.arange(key_rows, dtype=jnp.int32)[None, :, None]
    start = jnp.clip(q_row - RADIUS, 0, total_rows - 2 * RADIUS - 1)
    row_in = (k_row >= start) & (k_row <= start + 2 * RADIUS)
    q_col = jnp.arange(QCOLS, dtype=jnp.int32)[None, :]
    k_col = jnp.arange(key_cols, dtype=jnp.int32)[:, None] - MARGIN
    col_in = (k_col >= q_col - RADIUS) & (k_col <= q_col + RADIUS)
    shape = (tile_rows, key_rows, key_cols)
    row_part = jnp.broadcast_to(jnp.where(row_in, 0.0, OUTSIDE)[:, :, None, :], shape + (QROWS,))
    col_part = jnp.broadcast_to(jnp.where(col_in, 0.0, OUTSIDE)[None, None], shape + (QCOLS,))
    rest = jnp.zeros(shape + (lanes - QROWS - QCOLS,), jnp.float32)
    columns = jnp.concatenate([row_part, col_part, rest], axis=-1).astype(jnp.bfloat16)
    columns = columns.reshape(tile_rows, key_rows * key_cols, lanes)
    r, c = jnp.arange(QROWS * QCOLS) // QCOLS, jnp.arange(QROWS * QCOLS) % QCOLS
    lane = jnp.arange(lanes)[None, :]
    hot = ((lane == r[:, None]) | (lane == QROWS + c[:, None])).astype(jnp.bfloat16)
    return columns, hot


def routed(value, route):
    lats, lons = lax.axis_size("lat"), lax.axis_size("lon")
    pairs = []
    for a in range(lats):
        for o in range(lons):
            to_lat, to_lon = route(a, o)
            if 0 <= to_lat < lats:
                pairs.append((a * lons + o, to_lat * lons + to_lon % lons))
    return lax.ppermute(value, ("lat", "lon"), pairs)


def partner(value):
    return routed(value, lambda a, o: (a, o ^ 1))


def beside(o):
    return o + 1 if o % 2 else o - 1


def by_core(core, mine, other, axis):
    return jnp.where(
        core == 0, jnp.concatenate([mine, other], axis=axis), jnp.concatenate([other, mine], axis=axis)
    )


def turned(parts, by):
    count = len(parts)
    whole = jnp.zeros((count,) + parts[0].shape, parts[0].dtype)
    for d, part in enumerate(parts):
        whole = lax.dynamic_update_index_in_dim(whole, part, (by - d) % count, 0)
    return whole


def lat_moves(blocks):
    lats = lax.axis_size("lat")
    return [routed(part, lambda a, o, d=d + 1: ((a + d) % lats, o)) for d, part in enumerate(blocks)]


def chip_moves(blocks):
    return [routed(part, lambda a, o, d=d + 1: (a, o + 2 * d)) for d, part in enumerate(blocks)]


def gather_rows(parts, chip):
    grid = turned(parts, chip)
    return jnp.swapaxes(grid, 0, 1).reshape((-1,) + grid.shape[3:])


def pick(value, index, count, dim):
    return lax.dynamic_index_in_dim(value, index % count, dim, keepdims=False)


def scatter_split(totals, chip):
    lats, chips = lax.axis_size("lat"), lax.axis_size("lon") // 2
    totals = [total.reshape(lats, chips, -1, total.shape[1]) for total in totals]
    blocks = [jnp.concatenate([pick(total, chip + d, chips, 1) for total in totals], axis=-1) for d in range(chips)]
    return blocks[0].astype(jnp.float32), blocks[1:]


def added(kept, parts):
    for part in parts:
        kept = kept + part.astype(jnp.float32)
    return kept


def scatter_rest(kept, lat):
    lats = lax.axis_size("lat")
    moved = lat_moves([pick(kept, lat + d, lats, 0).astype(jnp.bfloat16) for d in range(1, lats)])
    return added(pick(kept, lat, lats, 0), moved)


def after(value, *others):
    return lax.optimization_barrier((value,) + others)[0]


def shards(features, grad_output, qkv_weight, out_weight):
    lat_rows, lon_cols, width = features.shape
    head = width // HEADS
    lanes = PAIR * head
    groups = HEADS // PAIR // 2
    half = width // 2
    lats, chips = lax.axis_size("lat"), lax.axis_size("lon") // 2
    lat, lon = lax.axis_index("lat"), lax.axis_index("lon")
    core, chip = lon % 2, lon // 2
    rows = qkv_weight.shape[0]
    per = 3 * lanes
    cells = lat_rows * lon_cols
    block_cols = 2 * lon_cols
    half_cols = lon_cols + MARGIN

    edge = jnp.where(core == 0, features[:, :MARGIN], features[:, lon_cols - MARGIN :])
    side = routed(edge, lambda a, o: (a, beside(o)))

    by_heads = qkv_weight.reshape(rows, 3, 2, groups, lanes)
    first = [by_heads[:, i, c, 0] for c in range(2) for i in range(3)]
    first = after(jnp.concatenate(first + [out_weight], axis=1), edge)
    first_moved = lat_moves([first] * (lats - 1))

    def columns(which):
        qkv = lax.dynamic_index_in_dim(by_heads, which, 2, keepdims=False)[:, :, 1:]
        return jnp.swapaxes(qkv, 1, 2).reshape(rows, -1)

    both = [features.reshape(cells, width), grad_output.reshape(cells, width), side.reshape(-1, width)]
    both.append(columns(1 - core).reshape(-1, width))
    both = jnp.concatenate(both, axis=0)
    first = after(turned([first] + first_moved, lat), both)
    first_moved = chip_moves([first] * (chips - 1))
    both = partner(both)

    x_partner = both[:cells].reshape(features.shape)
    go_partner = both[cells : 2 * cells].reshape(features.shape)
    margin = MARGIN * lat_rows
    side_partner = both[2 * cells : 2 * cells + margin].reshape(side.shape)
    rest = by_core(core, columns(core), both[2 * cells + margin :].reshape(rows, -1), 0)

    def flanked(block, flank, first):
        return jnp.where(
            first, jnp.concatenate([flank, block], axis=1), jnp.concatenate([block, flank], axis=1)
        )

    middle = by_core(core, flanked(features, side, core == 0), flanked(x_partner, side_partner, core == 1), 1)
    ends = jnp.where(core == 0, middle[lat_rows - RADIUS :], middle[:RADIUS])
    cap = routed(ends, lambda a, o: (a - 1, o) if o % 2 else (a + 1, o))
    cap, *first_moved = lax.optimization_barrier((cap, *first_moved))
    first = turned([first] + first_moved, chip)
    first = jnp.swapaxes(first, 0, 1).reshape(lats * chips, rows, -1)
    cap_partner = partner(cap)
    x_wide = jnp.concatenate(
        [jnp.where(core == 0, cap, cap_partner), middle, jnp.where(core == 0, cap_partner, cap)], axis=0
    )
    wide_rows, wide_cols = x_wide.shape[:2]
    x_wide = x_wide.reshape(-1, width)
    x_turned = lax.optimization_barrier(x_wide.T)
    go = by_core(core, grad_output, go_partner, 1)
    go = go.reshape(lat_rows // QROWS, QROWS, block_cols // QCOLS, QCOLS, width)
    go = lax.optimization_barrier(jnp.swapaxes(go, 1, 2).reshape(-1, width))

    def heads_of(which):
        qkv = lax.dynamic_slice_in_dim(first, which * per, per, 2).reshape(half, per)
        count = lats * chips // 2
        out = lax.dynamic_slice_in_dim(first, which * count, count, 0)[..., 2 * per :].reshape(-1, width)
        return qkv, out

    qkv_mine, out_mine = heads_of(core)
    qkv_other, out_other = heads_of(1 - core)
    cut = out_other.shape[0]
    swap = jnp.concatenate([jnp.concatenate([qkv_other[:cut], qkv_other[cut:]], axis=1), out_other], axis=0)
    swap = partner(swap)
    qkv_got = jnp.concatenate([swap[:cut, :per], swap[:cut, per:]], axis=0)

    def interleaved(mine, got):
        mine, got = (part.reshape(-1, rows, part.shape[1]) for part in (mine, got))
        return by_core(core, mine, got, 1).reshape(-1, mine.shape[2])

    qkv_first = interleaved(qkv_mine, qkv_got)
    out_heads = interleaved(out_mine, swap[cut:])

    bias, hot = window_columns(lat * lat_rows, lat_rows // QROWS, lat_rows * lats, lanes)
    scale = jnp.concatenate(
        [jnp.full((lanes,), LOG2E / math.sqrt(head), jnp.float32), jnp.ones((2 * lanes,), jnp.float32)]
    )

    def project(weights):
        result = dot(x_wide, weights) * jnp.tile(scale, weights.shape[1] // per)
        return result.astype(jnp.bfloat16).reshape(wide_rows, wide_cols, -1)

    def half_rows(grads, which):
        return lax.dynamic_slice_in_dim(grads, which * (grads.shape[0] // 2), grads.shape[0] // 2, 0)

    rest_moved = lat_moves([after(rest, first)] * (lats - 1))
    projected = project(qkv_first)
    g = dot(go, out_heads, NT).astype(jnp.bfloat16)
    projected, g, *rest_moved = lax.optimization_barrier((projected, g, *rest_moved))
    rest = turned([rest] + rest_moved, lat)
    rest_moved = chip_moves([rest] * (chips - 1))
    att_0, grads_0 = attention(projected, g, bias, hot, 0, 0, lanes)
    grads_0, *rest_moved = lax.optimization_barrier((grads_0, *rest_moved))
    qkv_rest = gather_rows([rest] + rest_moved, chip)
    projected = project(qkv_rest[:, :per])
    att_1, grads_1 = attention(projected, g, bias, hot, 0, 1, lanes)
    projected = project(qkv_rest[:, per:])

    grads_0, grads_1 = grads_0.reshape(-1, per), grads_1.reshape(-1, per)
    early = [dot(x_turned, part).astype(jnp.bfloat16) for part in (grads_0, grads_1)]
    early_kept, early_moved = scatter_split(early, chip)

    def gx_early(which):
        return dot(half_rows(grads_0, which), qkv_first, NT) + dot(half_rows(grads_1, which), qkv_rest[:, :per], NT)

    give_early, keep_early = gx_early(1 - core), gx_early(core)
    out_rows = [dot(part, go).astype(jnp.bfloat16) for part in (att_0, att_1)]
    g, early_kept, give_early, keep_early, *early_moved, = lax.optimization_barrier(
        (g, early_kept, give_early, keep_early, *early_moved)
    )
    early_moved = chip_moves(early_moved)
    att_2, grads_2 = attention(projected, g, bias, hot, 0, 2, lanes)
    att_2, grads_2, *early_moved = lax.optimization_barrier((att_2, grads_2, *early_moved))
    grads_2 = grads_2.reshape(-1, per)

    def gx_late(which, before):
        return dot(half_rows(grads_2, which), qkv_rest[:, per:], NT) + before

    out_rows.append(dot(att_2, go).astype(jnp.bfloat16))
    out_rows = jnp.concatenate(out_rows, axis=0)
    swapped = partner(lax.dynamic_slice_in_dim(out_rows, (1 - core) * half, half, 1))
    give = gx_late(1 - core, give_early).astype(jnp.bfloat16)
    given = partner(give)
    late = dot(x_turned, after(grads_2, give)).astype(jnp.bfloat16)
    out_mine = by_core(core, lax.dynamic_slice_in_dim(out_rows, core * half, half, 1), swapped, 0)
    late_kept, late_moved = scatter_split([late, out_mine], chip)
    late_moved = chip_moves(late_moved)
    gx = gx_late(core, after(keep_early, give)) + given.astype(jnp.float32)
    gx = gx.reshape(wide_rows // 2, wide_cols, width)
    own = wide_rows // 2 - RADIUS
    outer = jnp.where(core == 0, gx[:RADIUS], gx[own:]).astype(jnp.bfloat16)
    gx = jnp.where(core == 0, gx[RADIUS:], gx[:own])
    inner = routed(outer, lambda a, o: (a + 1, o - 1) if o % 2 else (a - 1, o + 1))
    inner, *late_moved = lax.optimization_barrier((inner, *late_moved))
    inner = inner.astype(jnp.float32)
    total = jnp.concatenate([added(early_kept, early_moved), added(late_kept, late_moved)], axis=-1)
    gap = jnp.zeros((own - RADIUS,) + gx.shape[1:], jnp.float32)
    gx = gx + by_core(core, inner, gap, 0)
    other_half = lax.dynamic_slice_in_dim(gx, MARGIN + (1 - core) * lon_cols, lon_cols, 1)
    mine_half = lax.dynamic_slice_in_dim(gx, MARGIN + core * lon_cols, lon_cols, 1)
    left, right = gx[:, :MARGIN].astype(jnp.bfloat16), gx[:, wide_cols - MARGIN :].astype(jnp.bfloat16)
    same = routed(jnp.where(core == 0, right, left), lambda a, o: (a, o - 2 if o % 2 else o + 2))
    cross = routed(jnp.where(core == 0, left, right), lambda a, o: (a, o + 1 if o % 2 else o - 1))
    swapped_x = partner(other_half.astype(jnp.bfloat16))
    pad = jnp.zeros((own, lon_cols - MARGIN, width), jnp.float32)
    here = mine_half + by_core(core, same.astype(jnp.float32), pad, 1)
    there = swapped_x.astype(jnp.float32) + by_core(core, cross.astype(jnp.float32), pad, 1)
    grad_x = by_core(core, here.astype(jnp.bfloat16), there.astype(jnp.bfloat16), 0)

    total = scatter_rest(total, lat).reshape(2, rows, -1)
    keep = lax.dynamic_index_in_dim(total, core, 0, keepdims=False)
    give = lax.dynamic_index_in_dim(total, 1 - core, 0, keepdims=False).astype(jnp.bfloat16)
    got = partner(give).astype(jnp.float32)
    order = jnp.where(core == 0, jnp.stack([keep, got]), jnp.stack([got, keep]))
    grad_qkv = order[:, :, : groups * per].reshape(2, rows, groups, 3, lanes)
    grad_qkv = jnp.transpose(grad_qkv, (1, 3, 0, 2, 4)).reshape(rows, 3 * width)
    grad_out = jnp.transpose(order[:, :, groups * per :], (1, 0, 2)).reshape(rows, width)
    return grad_x, grad_qkv, grad_out


def solution(mesh):
    placed = (
        P("lat", "lon", None),
        P("lat", "lon", None),
        P(("lat", "lon"), None),
        P(("lat", "lon"), None),
    )
    return jax.shard_map(
        shards,
        mesh=mesh,
        in_specs=placed,
        out_specs=(P("lat", "lon", None), P(("lat", "lon"), None), P(("lat", "lon"), None)),
        check_vma=False,
    )
```

```python
import math

import jax
import jax.numpy as jnp
from jax import lax
from jax.experimental import pallas as pl
from jax.experimental.pallas import tpu as pltpu
from jax.sharding import PartitionSpec as P

HEADS = 12
RADIUS = 6
QROWS = 16
QCOLS = 16
MARGIN = 8
PAIR = 2
OUTSIDE = -1e30
LOG2E = math.log2(math.e)

NT = (((1,), (1,)), ((), ()))
NN = (((1,), (0,)), ((), ()))


def dot(a, b, dims=NN):
    return lax.dot_general(a, b, dims, preferred_element_type=jnp.float32)


def attention_kernel(p_ref, g_ref, bias_ref, hot_ref, att_ref, grad_ref, *scratch):
    scores, e_both, ds_both, sums = scratch[:PAIR], scratch[PAIR], scratch[PAIR + 1], scratch[PAIR + 2]
    tile_row, tile_col = pl.program_id(0), pl.program_id(1)
    key_rows, key_cols = QROWS + 2 * RADIUS, QCOLS + 2 * MARGIN
    keys, queries = key_rows * key_cols, QROWS * QCOLS
    lanes = g_ref.shape[-1]
    head = lanes // PAIR
    chunk = 64
    first_row = tile_row * QROWS
    first_col = pl.multiple_of(tile_col * QCOLS, QCOLS)
    at_rows, at_cols = pl.ds(first_row, key_rows), pl.ds(first_col, key_cols)
    q_lanes, k_lanes, v_lanes = (slice(i * lanes, (i + 1) * lanes) for i in range(3))
    heads = range(PAIR)
    rows = [slice(h * head, (h + 1) * head) for h in heads]
    cols = [slice(h * queries, (h + 1) * queries) for h in heads]

    @pl.when((tile_row == 0) & (tile_col == 0))
    def _():
        sums[...] = jnp.zeros_like(sums)

    q = p_ref[pl.ds(first_row + RADIUS, QROWS), at_cols, q_lanes].astype(jnp.float32)
    q = q[:, MARGIN : MARGIN + QCOLS].reshape(queries, lanes).astype(jnp.bfloat16)
    g_t = g_ref[...].astype(jnp.float32).T
    k = p_ref[at_rows, at_cols, k_lanes].reshape(keys, lanes)
    v = p_ref[at_rows, at_cols, v_lanes].reshape(keys, lanes)
    k_wide = jnp.concatenate([k, bias_ref[0]], axis=1)
    ones = jnp.ones((16, keys), jnp.bfloat16)
    lane = lax.broadcasted_iota(jnp.int32, (queries, lanes), 1) // head
    q_heads = [jnp.where(lane == h, q, jnp.zeros_like(q)) for h in heads]
    for h in heads:
        scores[h][...] = dot(k_wide, jnp.concatenate([q_heads[h], hot_ref[...]], axis=1), NT)
    k_t, v_t = k.T, v.T
    g_heads, att_t, dq_t, terms = [], [], [], []
    for h in heads:
        top = jnp.max(scores[h][...], axis=0, keepdims=True)
        for c in range(0, keys, chunk):
            e_both[c : c + chunk, cols[h]] = jnp.exp2(scores[h][c : c + chunk] - top).astype(jnp.bfloat16)
        out = dot(jnp.concatenate([v_t[rows[h]], ones], axis=0), e_both[:, cols[h]])
        inverse = 1.0 / out[head : head + 1]
        attended = (out[:head] * inverse).astype(jnp.bfloat16).astype(jnp.float32)
        att_t.append(attended)
        g_one = g_t[rows[h]] * inverse
        terms.append(jnp.sum(g_one * attended, axis=0, keepdims=True))
        empty = jnp.zeros_like(g_one)
        g_one = jnp.concatenate([empty] * h + [g_one] + [empty] * (PAIR - 1 - h), axis=0).astype(jnp.bfloat16)
        g_heads.append(g_one)
    for h in heads:
        scores[h][...] = dot(v, g_heads[h])
    for h in heads:
        for c in range(0, keys, chunk):
            ds_both[c : c + chunk, cols[h]] = (
                e_both[c : c + chunk, cols[h]].astype(jnp.float32) * (scores[h][c : c + chunk] - terms[h])
            ).astype(jnp.bfloat16)
        dq_t.append(dot(k_t[rows[h]], ds_both[:, cols[h]]))
    tile = (key_rows, key_cols, lanes)
    sums[at_rows, at_cols, v_lanes] += dot(e_both[...], jnp.concatenate(g_heads, axis=1), NT).reshape(tile)
    sums[at_rows, at_cols, k_lanes] += dot(ds_both[...], jnp.concatenate(q_heads, axis=0)).reshape(tile)
    att_ref[...] = jnp.concatenate(att_t, axis=0).astype(jnp.bfloat16)
    dq = jnp.concatenate(dq_t, axis=0).T * (1.0 / math.sqrt(head))
    sums[pl.ds(first_row + RADIUS, QROWS), pl.ds(pl.multiple_of(first_col + MARGIN, 8), QCOLS), q_lanes] = dq.reshape(
        QROWS, QCOLS, lanes
    )

    @pl.when((tile_row == pl.num_programs(0) - 1) & (tile_col == pl.num_programs(1) - 1))
    def _():
        grad_ref[:, :, q_lanes] = sums[:, :, q_lanes].astype(jnp.bfloat16)
        grad_ref[:, :, k_lanes] = (sums[:, :, k_lanes] * (1.0 / LOG2E)).astype(jnp.bfloat16)
        grad_ref[:, :, v_lanes] = sums[:, :, v_lanes].astype(jnp.bfloat16)


def attention(projected, g, bias, hot, place, g_place, lanes):
    wide = projected.shape[:2] + (3 * lanes,)
    queries, keys = QROWS * QCOLS, (QROWS + 2 * RADIUS) * (QCOLS + 2 * MARGIN)
    tiles = ((wide[0] - 2 * RADIUS) // QROWS, (wide[1] - 2 * MARGIN) // QCOLS)
    count = tiles[0] * tiles[1]
    return pl.pallas_call(
        attention_kernel,
        grid=tiles,
        in_specs=[
            pl.BlockSpec(wide, lambda r, c: (0, 0, place)),
            pl.BlockSpec((queries, lanes), lambda r, c: (r * tiles[1] + c, g_place)),
            pl.BlockSpec((1, keys, lanes), lambda r, c: (r, 0, 0)),
            pl.BlockSpec((queries, lanes), lambda r, c: (0, 0)),
        ],
        out_specs=[
            pl.BlockSpec((lanes, queries), lambda r, c: (0, r * tiles[1] + c)),
            pl.BlockSpec(wide, lambda r, c: (0, 0, 0)),
        ],
        out_shape=[
            jax.ShapeDtypeStruct((lanes, count * queries), jnp.bfloat16),
            jax.ShapeDtypeStruct(wide, jnp.bfloat16),
        ],
        scratch_shapes=[pltpu.VMEM((keys, queries), jnp.float32)] * PAIR
        + [pltpu.VMEM((keys, PAIR * queries), jnp.bfloat16)] * 2
        + [pltpu.VMEM(wide, jnp.float32)],
        compiler_params=pltpu.CompilerParams(
            dimension_semantics=("arbitrary", "arbitrary"), vmem_limit_bytes=48 * 1024 * 1024
        ),
        cost_estimate=pl.CostEstimate(
            flops=2 * 12 * 256 * keys * queries * PAIR * count,
            bytes_accessed=12 * count * queries * lanes * 2,
            transcendentals=keys * queries * PAIR * count,
        ),
    )(projected, g, bias, hot)


def window_columns(lat_first, tile_rows, total_rows, lanes):
    key_rows, key_cols = QROWS + 2 * RADIUS, QCOLS + 2 * MARGIN
    base = lat_first + QROWS * jnp.arange(tile_rows, dtype=jnp.int32)[:, None, None]
    q_row = base + jnp.arange(QROWS, dtype=jnp.int32)[None, None, :]
    k_row = base - RADIUS + jnp.arange(key_rows, dtype=jnp.int32)[None, :, None]
    start = jnp.clip(q_row - RADIUS, 0, total_rows - 2 * RADIUS - 1)
    row_in = (k_row >= start) & (k_row <= start + 2 * RADIUS)
    q_col = jnp.arange(QCOLS, dtype=jnp.int32)[None, :]
    k_col = jnp.arange(key_cols, dtype=jnp.int32)[:, None] - MARGIN
    col_in = (k_col >= q_col - RADIUS) & (k_col <= q_col + RADIUS)
    shape = (tile_rows, key_rows, key_cols)
    row_part = jnp.broadcast_to(jnp.where(row_in, 0.0, OUTSIDE)[:, :, None, :], shape + (QROWS,))
    col_part = jnp.broadcast_to(jnp.where(col_in, 0.0, OUTSIDE)[None, None], shape + (QCOLS,))
    rest = jnp.zeros(shape + (lanes - QROWS - QCOLS,), jnp.float32)
    columns = jnp.concatenate([row_part, col_part, rest], axis=-1).astype(jnp.bfloat16)
    columns = columns.reshape(tile_rows, key_rows * key_cols, lanes)
    r, c = jnp.arange(QROWS * QCOLS) // QCOLS, jnp.arange(QROWS * QCOLS) % QCOLS
    lane = jnp.arange(lanes)[None, :]
    hot = ((lane == r[:, None]) | (lane == QROWS + c[:, None])).astype(jnp.bfloat16)
    return columns, hot


def routed(value, route):
    lats, lons = lax.axis_size("lat"), lax.axis_size("lon")
    pairs = []
    for a in range(lats):
        for o in range(lons):
            to_lat, to_lon = route(a, o)
            if 0 <= to_lat < lats:
                pairs.append((a * lons + o, to_lat * lons + to_lon % lons))
    return lax.ppermute(value, ("lat", "lon"), pairs)


def partner(value):
    return routed(value, lambda a, o: (a, o ^ 1))


def beside(o):
    return o + 1 if o % 2 else o - 1


def by_core(core, mine, other, axis):
    return jnp.where(
        core == 0, jnp.concatenate([mine, other], axis=axis), jnp.concatenate([other, mine], axis=axis)
    )


def turned(parts, by):
    count = len(parts)
    whole = jnp.zeros((count,) + parts[0].shape, parts[0].dtype)
    for d, part in enumerate(parts):
        whole = lax.dynamic_update_index_in_dim(whole, part, (by - d) % count, 0)
    return whole


def lat_moves(blocks):
    lats = lax.axis_size("lat")
    return [routed(part, lambda a, o, d=d + 1: ((a + d) % lats, o)) for d, part in enumerate(blocks)]


def chip_moves(blocks):
    return [routed(part, lambda a, o, d=d + 1: (a, o + 2 * d)) for d, part in enumerate(blocks)]


def gather_rows(parts, chip):
    grid = turned(parts, chip)
    return jnp.swapaxes(grid, 0, 1).reshape((-1,) + grid.shape[3:])


def pick(value, index, count, dim):
    return lax.dynamic_index_in_dim(value, index % count, dim, keepdims=False)


def scatter_split(totals, chip):
    lats, chips = lax.axis_size("lat"), lax.axis_size("lon") // 2
    totals = [total.reshape(lats, chips, -1, total.shape[1]) for total in totals]
    blocks = [jnp.concatenate([pick(total, chip + d, chips, 1) for total in totals], axis=-1) for d in range(chips)]
    return blocks[0].astype(jnp.float32), blocks[1:]


def added(kept, parts):
    for part in parts:
        kept = kept + part.astype(jnp.float32)
    return kept


def scatter_rest(kept, lat):
    lats = lax.axis_size("lat")
    moved = lat_moves([pick(kept, lat + d, lats, 0).astype(jnp.bfloat16) for d in range(1, lats)])
    return added(pick(kept, lat, lats, 0), moved)


def after(value, *others):
    return lax.optimization_barrier((value,) + others)[0]


def shards(features, grad_output, qkv_weight, out_weight):
    lat_rows, lon_cols, width = features.shape
    head = width // HEADS
    lanes = PAIR * head
    groups = HEADS // PAIR // 2
    half = width // 2
    lats, chips = lax.axis_size("lat"), lax.axis_size("lon") // 2
    lat, lon = lax.axis_index("lat"), lax.axis_index("lon")
    core, chip = lon % 2, lon // 2
    rows = qkv_weight.shape[0]
    per = 3 * lanes
    cells = lat_rows * lon_cols
    block_cols = 2 * lon_cols
    half_cols = lon_cols + MARGIN

    edge = jnp.where(core == 0, features[:, :MARGIN], features[:, lon_cols - MARGIN :])
    side = routed(edge, lambda a, o: (a, beside(o)))

    by_heads = qkv_weight.reshape(rows, 3, 2, groups, lanes)
    first = [by_heads[:, i, c, 0] for c in range(2) for i in range(3)]
    first = after(jnp.concatenate(first + [out_weight], axis=1), edge)
    first_moved = lat_moves([first] * (lats - 1))

    def columns(which):
        qkv = lax.dynamic_index_in_dim(by_heads, which, 2, keepdims=False)[:, :, 1:]
        return jnp.swapaxes(qkv, 1, 2).reshape(rows, -1)

    both = [features.reshape(cells, width), grad_output.reshape(cells, width), side.reshape(-1, width)]
    both.append(columns(1 - core).reshape(-1, width))
    both = jnp.concatenate(both, axis=0)
    near = jnp.where(
        core == 0, jnp.concatenate([side, features], axis=1), jnp.concatenate([features, side], axis=1)
    )
    top, bottom = near[:RADIUS], near[lat_rows - RADIUS :]
    first = after(turned([first] + first_moved, lat), both, top, bottom)
    both = partner(both)
    above = routed(bottom, lambda a, o: (a + 1, o))
    below = routed(top, lambda a, o: (a - 1, o))
    first_moved = chip_moves([first] * (chips - 1))
    margin = MARGIN * lat_rows
    x_partner = both[:cells].reshape(features.shape)
    go_partner = both[cells : 2 * cells].reshape(features.shape)
    side_partner = both[2 * cells : 2 * cells + margin].reshape(side.shape)
    rest = by_core(core, columns(core), both[2 * cells + margin :].reshape(rows, -1), 0)
    far = jnp.where(
        core == 0,
        jnp.concatenate([x_partner, side_partner], axis=1),
        jnp.concatenate([side_partner, x_partner], axis=1),
    )
    rest, above, below, far = lax.optimization_barrier((rest, above, below, far))
    rest_moved = lat_moves([rest] * (lats - 1))
    moved = lax.optimization_barrier((above, below, *first_moved, *rest_moved[:-1]))
    above, below, first_moved, rest_moved[:-1] = moved[0], moved[1], list(moved[2 : chips + 1]), moved[chips + 1 :]
    caps = partner(jnp.concatenate([above, below], axis=0))
    near = jnp.concatenate([above, near, below], axis=0)
    far = jnp.concatenate([caps[:RADIUS], far, caps[RADIUS:]], axis=0)
    wide_rows = near.shape[0]
    first = turned([first] + first_moved, chip)
    first = jnp.swapaxes(first, 0, 1).reshape(lats * chips, rows, -1)
    x_wide = by_core(core, near, far, 1)
    wide_cols = x_wide.shape[1]
    x_wide = x_wide.reshape(-1, width)
    x_turned = lax.optimization_barrier(x_wide.T)
    go = by_core(core, grad_output, go_partner, 1)
    go = go.reshape(lat_rows // QROWS, QROWS, block_cols // QCOLS, QCOLS, width)
    go = lax.optimization_barrier(jnp.swapaxes(go, 1, 2).reshape(-1, width))

    def heads_of(which):
        qkv = lax.dynamic_slice_in_dim(first, which * per, per, 2).reshape(half, per)
        count = lats * chips // 2
        out = lax.dynamic_slice_in_dim(first, which * count, count, 0)[..., 2 * per :].reshape(-1, width)
        return qkv, out

    qkv_mine, out_mine = heads_of(core)
    qkv_other, out_other = heads_of(1 - core)
    cut = out_other.shape[0]
    swap = jnp.concatenate([jnp.concatenate([qkv_other[:cut], qkv_other[cut:]], axis=1), out_other], axis=0)
    swap = partner(swap)
    qkv_got = jnp.concatenate([swap[:cut, :per], swap[:cut, per:]], axis=0)

    def interleaved(mine, got):
        mine, got = (part.reshape(-1, rows, part.shape[1]) for part in (mine, got))
        return by_core(core, mine, got, 1).reshape(-1, mine.shape[2])

    qkv_first = interleaved(qkv_mine, qkv_got)
    out_heads = interleaved(out_mine, swap[cut:])

    bias, hot = window_columns(lat * lat_rows, lat_rows // QROWS, lat_rows * lats, lanes)
    scale = jnp.concatenate(
        [jnp.full((lanes,), LOG2E / math.sqrt(head), jnp.float32), jnp.ones((2 * lanes,), jnp.float32)]
    )

    def project(weights):
        result = dot(x_wide, weights) * jnp.tile(scale, weights.shape[1] // per)
        return result.astype(jnp.bfloat16).reshape(wide_rows, wide_cols, -1)

    def half_rows(grads, which):
        return lax.dynamic_slice_in_dim(grads, which * (grads.shape[0] // 2), grads.shape[0] // 2, 0)

    projected = project(qkv_first)
    g = dot(go, out_heads, NT).astype(jnp.bfloat16)
    rest = turned([rest] + list(rest_moved), lat)
    projected, g, rest = lax.optimization_barrier((projected, g, rest))
    rest_moved = chip_moves([rest] * (chips - 1))
    att_0, grads_0 = attention(projected, g, bias, hot, 0, 0, lanes)
    grads_0 = grads_0.reshape(-1, per)
    early_0 = dot(x_turned, grads_0).astype(jnp.bfloat16)
    early_0, *rest_moved = lax.optimization_barrier((early_0, *rest_moved))
    qkv_rest = gather_rows([rest] + rest_moved, chip)
    projected = project(qkv_rest[:, :per])
    att_1, grads_1 = attention(projected, g, bias, hot, 0, 1, lanes)
    projected = project(qkv_rest[:, per:])

    grads_1 = grads_1.reshape(-1, per)
    early = [early_0, dot(x_turned, grads_1).astype(jnp.bfloat16)]
    early_kept, early_moved = scatter_split(early, chip)

    def gx_early(which):
        return dot(half_rows(grads_0, which), qkv_first, NT) + dot(half_rows(grads_1, which), qkv_rest[:, :per], NT)

    give_early, keep_early = gx_early(1 - core), gx_early(core)
    out_rows = [dot(part, go).astype(jnp.bfloat16) for part in (att_0, att_1)]
    g, early_kept, give_early, keep_early, *early_moved, = lax.optimization_barrier(
        (g, early_kept, give_early, keep_early, *early_moved)
    )
    early_moved = chip_moves(early_moved)
    att_2, grads_2 = attention(projected, g, bias, hot, 0, 2, lanes)
    grads_2 = grads_2.reshape(-1, per)

    def gx_late(which, before):
        return dot(half_rows(grads_2, which), qkv_rest[:, per:], NT) + before

    out_rows.append(dot(att_2, go).astype(jnp.bfloat16))
    out_rows = jnp.concatenate(out_rows, axis=0)
    swapped = partner(lax.dynamic_slice_in_dim(out_rows, (1 - core) * half, half, 1))
    give = gx_late(1 - core, give_early).astype(jnp.bfloat16)
    given = partner(give)
    late = dot(x_turned, after(grads_2, give)).astype(jnp.bfloat16)
    late, *early_moved = lax.optimization_barrier((late, *early_moved))
    out_mine = by_core(core, lax.dynamic_slice_in_dim(out_rows, core * half, half, 1), swapped, 0)
    late_kept, late_moved = scatter_split([late, out_mine], chip)
    given, *late_moved = lax.optimization_barrier((given, *late_moved))
    late_moved = chip_moves(late_moved)
    early = added(early_kept, early_moved)
    gx = gx_late(core, after(keep_early, give)) + given.astype(jnp.float32)
    gx = gx.reshape(wide_rows // 2, wide_cols, width)
    own = wide_rows // 2 - RADIUS
    outer = jnp.where(core == 0, gx[:RADIUS], gx[own:]).astype(jnp.bfloat16)
    gx = jnp.where(core == 0, gx[RADIUS:], gx[:own])
    inner = routed(outer, lambda a, o: (a + 1, o - 1) if o % 2 else (a - 1, o + 1))
    early = after(early, outer)
    early_moved = [pick(early, lat + d, lats, 0).astype(jnp.bfloat16) for d in range(1, lats)]
    for d in range(1, min(lats, chips) - 1):
        early_moved[d], late_moved[d - 1] = lax.optimization_barrier((early_moved[d], late_moved[d - 1]))
    early_moved = lat_moves(early_moved)
    inner, *moved = lax.optimization_barrier((inner, *early_moved, *late_moved))
    early = added(pick(early, lat, lats, 0), moved[: lats - 1])
    late_moved = moved[lats - 1 :]
    inner = inner.astype(jnp.float32)
    late = scatter_rest(added(late_kept, late_moved), lat)
    gap = jnp.zeros((own - RADIUS,) + gx.shape[1:], jnp.float32)
    gx = gx + by_core(core, inner, gap, 0)
    other_half = lax.dynamic_slice_in_dim(gx, MARGIN + (1 - core) * lon_cols, lon_cols, 1)
    mine_half = lax.dynamic_slice_in_dim(gx, MARGIN + core * lon_cols, lon_cols, 1)
    left, right = gx[:, :MARGIN].astype(jnp.bfloat16), gx[:, wide_cols - MARGIN :].astype(jnp.bfloat16)
    same = routed(jnp.where(core == 0, right, left), lambda a, o: (a, o - 2 if o % 2 else o + 2))
    cross = routed(jnp.where(core == 0, left, right), lambda a, o: (a, o + 1 if o % 2 else o - 1))
    swapped_x = partner(other_half.astype(jnp.bfloat16))
    pad = jnp.zeros((own, lon_cols - MARGIN, width), jnp.float32)
    here = mine_half + by_core(core, same.astype(jnp.float32), pad, 1)
    there = swapped_x.astype(jnp.float32) + by_core(core, cross.astype(jnp.float32), pad, 1)
    grad_x = by_core(core, here.astype(jnp.bfloat16), there.astype(jnp.bfloat16), 0)

    total = jnp.concatenate([early, late], axis=1).reshape(2, rows, -1)
    keep = lax.dynamic_index_in_dim(total, core, 0, keepdims=False)
    give = lax.dynamic_index_in_dim(total, 1 - core, 0, keepdims=False).astype(jnp.bfloat16)
    got = partner(give).astype(jnp.float32)
    order = jnp.where(core == 0, jnp.stack([keep, got]), jnp.stack([got, keep]))
    grad_qkv = order[:, :, : groups * per].reshape(2, rows, groups, 3, lanes)
    grad_qkv = jnp.transpose(grad_qkv, (1, 3, 0, 2, 4)).reshape(rows, 3 * width)
    grad_out = jnp.transpose(order[:, :, groups * per :], (1, 0, 2)).reshape(rows, width)
    return grad_x, grad_qkv, grad_out


def solution(mesh):
    placed = (
        P("lat", "lon", None),
        P("lat", "lon", None),
        P(("lat", "lon"), None),
        P(("lat", "lon"), None),
    )
    return jax.shard_map(
        shards,
        mesh=mesh,
        in_specs=placed,
        out_specs=(P("lat", "lon", None), P(("lat", "lon"), None), P(("lat", "lon"), None)),
        check_vma=False,
    )
```

```python
import math

import jax
import jax.numpy as jnp
from jax import lax
from jax.experimental import pallas as pl
from jax.experimental.pallas import tpu as pltpu
from jax.sharding import PartitionSpec as P

HEADS = 12
RADIUS = 6
QROWS = 16
QCOLS = 16
MARGIN = 8
PAIR = 2
OUTSIDE = -1e30
LOG2E = math.log2(math.e)

NT = (((1,), (1,)), ((), ()))
NN = (((1,), (0,)), ((), ()))


def dot(a, b, dims=NN):
    return lax.dot_general(a, b, dims, preferred_element_type=jnp.float32)


def attention_kernel(p_ref, g_ref, bias_ref, hot_ref, *rest):
    att_ref, grad_ref, *scratch = rest[-PAIR - 5 :]
    scores, e_both, ds_both, sums = scratch[:PAIR], scratch[PAIR], scratch[PAIR + 1], scratch[PAIR + 2]
    tile_row, tile_col = pl.program_id(0), pl.program_id(1)
    key_rows, key_cols = QROWS + 2 * RADIUS, QCOLS + 2 * MARGIN
    keys, queries = key_rows * key_cols, QROWS * QCOLS
    lanes = g_ref.shape[-1]
    head = lanes // PAIR
    chunk = 64
    first_row = tile_row * QROWS
    first_col = pl.multiple_of(tile_col * QCOLS, QCOLS)
    at_rows, at_cols = pl.ds(first_row, key_rows), pl.ds(first_col, key_cols)
    q_lanes, k_lanes, v_lanes = (slice(i * lanes, (i + 1) * lanes) for i in range(3))
    heads = range(PAIR)
    rows = [slice(h * head, (h + 1) * head) for h in heads]
    cols = [slice(h * queries, (h + 1) * queries) for h in heads]

    @pl.when((tile_row == 0) & (tile_col == 0))
    def _():
        sums[...] = jnp.zeros_like(sums)

    q = p_ref[pl.ds(first_row + RADIUS, QROWS), at_cols, q_lanes].astype(jnp.float32)
    q = q[:, MARGIN : MARGIN + QCOLS].reshape(queries, lanes).astype(jnp.bfloat16)
    g_t = g_ref[...].astype(jnp.float32).T
    k = p_ref[at_rows, at_cols, k_lanes].reshape(keys, lanes)
    v = p_ref[at_rows, at_cols, v_lanes].reshape(keys, lanes)
    k_wide = jnp.concatenate([k, bias_ref[0]], axis=1)
    ones = jnp.ones((16, keys), jnp.bfloat16)
    lane = lax.broadcasted_iota(jnp.int32, (queries, lanes), 1) // head
    q_heads = [jnp.where(lane == h, q, jnp.zeros_like(q)) for h in heads]
    for h in heads:
        scores[h][...] = dot(k_wide, jnp.concatenate([q_heads[h], hot_ref[...]], axis=1), NT)
    k_t, v_t = k.T, v.T
    g_heads, att_t, dq_t, terms = [], [], [], []
    for h in heads:
        top = jnp.max(scores[h][...], axis=0, keepdims=True)
        for c in range(0, keys, chunk):
            e_both[c : c + chunk, cols[h]] = jnp.exp2(scores[h][c : c + chunk] - top).astype(jnp.bfloat16)
        out = dot(jnp.concatenate([v_t[rows[h]], ones], axis=0), e_both[:, cols[h]])
        inverse = 1.0 / out[head : head + 1]
        attended = (out[:head] * inverse).astype(jnp.bfloat16).astype(jnp.float32)
        att_t.append(attended)
        g_one = g_t[rows[h]] * inverse
        terms.append(jnp.sum(g_one * attended, axis=0, keepdims=True))
        empty = jnp.zeros_like(g_one)
        g_one = jnp.concatenate([empty] * h + [g_one] + [empty] * (PAIR - 1 - h), axis=0).astype(jnp.bfloat16)
        g_heads.append(g_one)
    for h in heads:
        scores[h][...] = dot(v, g_heads[h])
    for h in heads:
        for c in range(0, keys, chunk):
            ds_both[c : c + chunk, cols[h]] = (
                e_both[c : c + chunk, cols[h]].astype(jnp.float32) * (scores[h][c : c + chunk] - terms[h])
            ).astype(jnp.bfloat16)
        dq_t.append(dot(k_t[rows[h]], ds_both[:, cols[h]]))
    tile = (key_rows, key_cols, lanes)
    sums[at_rows, at_cols, v_lanes] += dot(e_both[...], jnp.concatenate(g_heads, axis=1), NT).reshape(tile)
    sums[at_rows, at_cols, k_lanes] += dot(ds_both[...], jnp.concatenate(q_heads, axis=0)).reshape(tile)
    att_ref[...] = jnp.concatenate(att_t, axis=0).astype(jnp.bfloat16)
    dq = jnp.concatenate(dq_t, axis=0).T * (1.0 / math.sqrt(head))
    sums[pl.ds(first_row + RADIUS, QROWS), pl.ds(pl.multiple_of(first_col + MARGIN, 8), QCOLS), q_lanes] = dq.reshape(
        QROWS, QCOLS, lanes
    )

    @pl.when((tile_row == pl.num_programs(0) - 1) & (tile_col == pl.num_programs(1) - 1))
    def _():
        grad_ref[:, :, q_lanes] = sums[:, :, q_lanes].astype(jnp.bfloat16)
        grad_ref[:, :, k_lanes] = (sums[:, :, k_lanes] * (1.0 / LOG2E)).astype(jnp.bfloat16)
        grad_ref[:, :, v_lanes] = sums[:, :, v_lanes].astype(jnp.bfloat16)


def attention(projected, g, bias, hot, pair, lanes, total=1, place=0, grads=None):
    wide = projected.shape
    extra = () if grads is None else (grads,)
    queries, keys = QROWS * QCOLS, (QROWS + 2 * RADIUS) * (QCOLS + 2 * MARGIN)
    tiles = ((wide[0] - 2 * RADIUS) // QROWS, (wide[1] - 2 * MARGIN) // QCOLS)
    count = tiles[0] * tiles[1]
    return pl.pallas_call(
        attention_kernel,
        grid=tiles,
        in_specs=[
            pl.BlockSpec(wide, lambda r, c: (0, 0, 0)),
            pl.BlockSpec((queries, lanes), lambda r, c: (r * tiles[1] + c, pair)),
            pl.BlockSpec((1, keys, lanes), lambda r, c: (r, 0, 0)),
            pl.BlockSpec((queries, lanes), lambda r, c: (0, 0)),
        ]
        + [pl.BlockSpec(memory_space=pl.ANY)] * len(extra),
        input_output_aliases={4: 1} if extra else {},
        out_specs=[
            pl.BlockSpec((lanes, queries), lambda r, c: (0, r * tiles[1] + c)),
            pl.BlockSpec(wide, lambda r, c: (0, 0, place)),
        ],
        out_shape=[
            jax.ShapeDtypeStruct((lanes, count * queries), jnp.bfloat16),
            jax.ShapeDtypeStruct(wide[:2] + (total * wide[2],), jnp.bfloat16),
        ],
        scratch_shapes=[pltpu.VMEM((keys, queries), jnp.float32)] * PAIR
        + [pltpu.VMEM((keys, PAIR * queries), jnp.bfloat16)] * 2
        + [pltpu.VMEM(wide, jnp.float32)],
        compiler_params=pltpu.CompilerParams(
            dimension_semantics=("arbitrary", "arbitrary"), vmem_limit_bytes=48 * 1024 * 1024
        ),
        cost_estimate=pl.CostEstimate(
            flops=2 * 12 * 256 * keys * queries * PAIR * count,
            bytes_accessed=12 * count * queries * lanes * 2,
            transcendentals=keys * queries * PAIR * count,
        ),
    )(projected, g, bias, hot, *extra)


def window_columns(lat_first, tile_rows, total_rows, lanes):
    key_rows, key_cols = QROWS + 2 * RADIUS, QCOLS + 2 * MARGIN
    base = lat_first + QROWS * jnp.arange(tile_rows, dtype=jnp.int32)[:, None, None]
    q_row = base + jnp.arange(QROWS, dtype=jnp.int32)[None, None, :]
    k_row = base - RADIUS + jnp.arange(key_rows, dtype=jnp.int32)[None, :, None]
    start = jnp.clip(q_row - RADIUS, 0, total_rows - 2 * RADIUS - 1)
    row_in = (k_row >= start) & (k_row <= start + 2 * RADIUS)
    q_col = jnp.arange(QCOLS, dtype=jnp.int32)[None, :]
    k_col = jnp.arange(key_cols, dtype=jnp.int32)[:, None] - MARGIN
    col_in = (k_col >= q_col - RADIUS) & (k_col <= q_col + RADIUS)
    shape = (tile_rows, key_rows, key_cols)
    row_part = jnp.broadcast_to(jnp.where(row_in, 0.0, OUTSIDE)[:, :, None, :], shape + (QROWS,))
    col_part = jnp.broadcast_to(jnp.where(col_in, 0.0, OUTSIDE)[None, None], shape + (QCOLS,))
    rest = jnp.zeros(shape + (lanes - QROWS - QCOLS,), jnp.float32)
    columns = jnp.concatenate([row_part, col_part, rest], axis=-1).astype(jnp.bfloat16)
    columns = columns.reshape(tile_rows, key_rows * key_cols, lanes)
    r, c = jnp.arange(QROWS * QCOLS) // QCOLS, jnp.arange(QROWS * QCOLS) % QCOLS
    lane = jnp.arange(lanes)[None, :]
    hot = ((lane == r[:, None]) | (lane == QROWS + c[:, None])).astype(jnp.bfloat16)
    return columns, hot


def routed(value, route):
    lats, lons = lax.axis_size("lat"), lax.axis_size("lon")
    pairs = []
    for a in range(lats):
        for o in range(lons):
            to_lat, to_lon = route(a, o)
            if 0 <= to_lat < lats:
                pairs.append((a * lons + o, to_lat * lons + to_lon % lons))
    return lax.ppermute(value, ("lat", "lon"), pairs)


def partner(value):
    return routed(value, lambda a, o: (a, o ^ 1))


def beside(o):
    return o + 1 if o % 2 else o - 1


def by_core(core, mine, other, axis):
    return jnp.where(
        core == 0, jnp.concatenate([mine, other], axis=axis), jnp.concatenate([other, mine], axis=axis)
    )


def turned(parts, by):
    count = len(parts)
    whole = jnp.zeros((count,) + parts[0].shape, parts[0].dtype)
    for d, part in enumerate(parts):
        whole = lax.dynamic_update_index_in_dim(whole, part, (by - d) % count, 0)
    return whole


def lat_moves(blocks):
    lats = lax.axis_size("lat")
    return [routed(part, lambda a, o, d=d + 1: ((a + d) % lats, o)) for d, part in enumerate(blocks)]


def chip_moves(blocks):
    return [routed(part, lambda a, o, d=d + 1: (a, o + 2 * d)) for d, part in enumerate(blocks)]


def gather_rows(parts, chip):
    grid = turned(parts, chip)
    return jnp.swapaxes(grid, 0, 1).reshape((-1,) + grid.shape[3:])


def pick(value, index, count, dim):
    return lax.dynamic_index_in_dim(value, index % count, dim, keepdims=False)


def scatter_split(totals, chip):
    lats, chips = lax.axis_size("lat"), lax.axis_size("lon") // 2
    totals = [total.reshape(lats, chips, -1, total.shape[1]) for total in totals]
    blocks = [jnp.concatenate([pick(total, chip + d, chips, 1) for total in totals], axis=-1) for d in range(chips)]
    return blocks[0].astype(jnp.float32), blocks[1:]


def added(kept, parts):
    for part in parts:
        kept = kept + part.astype(jnp.float32)
    return kept


def scatter_rest(kept, lat):
    lats = lax.axis_size("lat")
    moved = lat_moves([pick(kept, lat + d, lats, 0).astype(jnp.bfloat16) for d in range(1, lats)])
    return added(pick(kept, lat, lats, 0), moved)


def after(value, *others):
    return lax.optimization_barrier((value,) + others)[0]


def shards(features, grad_output, qkv_weight, out_weight):
    lat_rows, lon_cols, width = features.shape
    head = width // HEADS
    lanes = PAIR * head
    groups = HEADS // PAIR // 2
    half = width // 2
    lats, chips = lax.axis_size("lat"), lax.axis_size("lon") // 2
    lat, lon = lax.axis_index("lat"), lax.axis_index("lon")
    core, chip = lon % 2, lon // 2
    rows = qkv_weight.shape[0]
    per = 3 * lanes
    cells = lat_rows * lon_cols
    block_cols = 2 * lon_cols
    half_cols = lon_cols + MARGIN

    by_heads = qkv_weight.reshape(rows, 3, 2, groups, lanes)
    first = [by_heads[:, i, c, 0] for c in range(2) for i in range(3)]
    first = jnp.concatenate(first + [out_weight], axis=1)
    first_moved = lat_moves([first] * (lats - 1))

    def columns(which):
        qkv = lax.dynamic_index_in_dim(by_heads, which, 2, keepdims=False)[:, :, 1:]
        return jnp.swapaxes(qkv, 1, 2).reshape(rows, -1)

    both = [features.reshape(cells, width), grad_output.reshape(cells, width), columns(1 - core).reshape(-1, width)]
    both = partner(jnp.concatenate(both, axis=0))
    x_partner = both[:cells].reshape(features.shape)
    go_partner = both[cells : 2 * cells].reshape(features.shape)
    rest = by_core(core, columns(core), both[2 * cells :].reshape(rows, -1), 0)
    above = routed(features[lat_rows - RADIUS :], lambda a, o: (a + 1, o))
    below = routed(features[:RADIUS], lambda a, o: (a - 1, o))
    first, above, below, rest = lax.optimization_barrier((turned([first] + first_moved, lat), above, below, rest))
    first_moved = chip_moves([first] * (chips - 1))
    rest_moved = lat_moves([rest] * (lats - 1))

    middle = jnp.concatenate([above, features, below], axis=0)
    side = jnp.where(core == 0, middle[:, :MARGIN], middle[:, lon_cols - MARGIN :])
    side = routed(side, lambda a, o: (a, beside(o)))
    side, *moved = lax.optimization_barrier((side, *first_moved, *rest_moved[:-1]))
    first_moved, rest_moved[:-1] = moved[: chips - 1], moved[chips - 1 :]
    wide_rows = middle.shape[0]
    rim = jnp.concatenate([part.reshape(-1, width) for part in (side, above, below)], axis=0)
    rim = partner(rim)
    margin, cap = wide_rows * MARGIN, RADIUS * lon_cols
    far_side = rim[:margin].reshape(side.shape)
    far_above = rim[margin : margin + cap].reshape(above.shape)
    far_below = rim[margin + cap :].reshape(below.shape)
    far_middle = jnp.concatenate([far_above, x_partner, far_below], axis=0)

    def flanked(block, flank, first):
        return jnp.where(
            first, jnp.concatenate([flank, block], axis=1), jnp.concatenate([block, flank], axis=1)
        )

    near = flanked(middle, side, core == 0)
    far = flanked(far_middle, far_side, core == 1)
    first = turned([first] + first_moved, chip)
    first = jnp.swapaxes(first, 0, 1).reshape(lats * chips, rows, -1)
    x_wide = by_core(core, near, far, 1)
    wide_cols = x_wide.shape[1]
    x_wide = x_wide.reshape(-1, width)
    x_turned = lax.optimization_barrier(x_wide.T)
    go = by_core(core, grad_output, go_partner, 1)
    go = go.reshape(lat_rows // QROWS, QROWS, block_cols // QCOLS, QCOLS, width)
    go = lax.optimization_barrier(jnp.swapaxes(go, 1, 2).reshape(-1, width))

    def heads_of(which):
        qkv = lax.dynamic_slice_in_dim(first, which * per, per, 2).reshape(half, per)
        count = lats * chips // 2
        out = lax.dynamic_slice_in_dim(first, which * count, count, 0)[..., 2 * per :].reshape(-1, width)
        return qkv, out

    qkv_mine, out_mine = heads_of(core)
    qkv_other, out_other = heads_of(1 - core)
    cut = out_other.shape[0]
    swap = jnp.concatenate([jnp.concatenate([qkv_other[:cut], qkv_other[cut:]], axis=1), out_other], axis=0)
    swap = partner(swap)
    qkv_got = jnp.concatenate([swap[:cut, :per], swap[:cut, per:]], axis=0)

    def interleaved(mine, got):
        mine, got = (part.reshape(-1, rows, part.shape[1]) for part in (mine, got))
        return by_core(core, mine, got, 1).reshape(-1, mine.shape[2])

    qkv_first = interleaved(qkv_mine, qkv_got)
    out_heads = interleaved(out_mine, swap[cut:])

    bias, hot = window_columns(lat * lat_rows, lat_rows // QROWS, lat_rows * lats, lanes)
    scale = jnp.concatenate(
        [jnp.full((lanes,), LOG2E / math.sqrt(head), jnp.float32), jnp.ones((2 * lanes,), jnp.float32)]
    )

    def project(weights):
        result = dot(x_wide, weights) * jnp.tile(scale, weights.shape[1] // per)
        return result.astype(jnp.bfloat16).reshape(wide_rows, wide_cols, -1)

    def half_rows(grads, which):
        return lax.dynamic_slice_in_dim(grads, which * (grads.shape[0] // 2), grads.shape[0] // 2, 0)

    projected = project(qkv_first)
    g = dot(go, out_heads, NT).astype(jnp.bfloat16)
    rest = turned([rest] + list(rest_moved), lat)
    projected, g, rest = lax.optimization_barrier((projected, g, rest))
    rest_moved = chip_moves([rest] * (chips - 1))
    att_0, grads = attention(projected, g, bias, hot, 0, lanes, 2, 0)
    out_rows = [dot(att_0, go).astype(jnp.bfloat16)]
    att_0, grads, *rest_moved = lax.optimization_barrier((att_0, grads, *rest_moved))
    qkv_rest = gather_rows([rest] + rest_moved, chip)
    projected = project(qkv_rest[:, :per])
    att_1, grads = attention(projected, g, bias, hot, 1, lanes, 2, 1, grads)
    projected = project(qkv_rest[:, per:])
    out_rows.append(dot(att_1, go).astype(jnp.bfloat16))

    grads = grads.reshape(-1, 2 * per)
    early = dot(x_turned, grads).astype(jnp.bfloat16).reshape(lats, chips, -1, 2 * per)
    early_kept, *early_moved = [pick(early, chip + d, chips, 1) for d in range(chips)]
    qkv_early = jnp.concatenate([qkv_first, qkv_rest[:, :per]], axis=1)

    def gx_early(which):
        return dot(half_rows(grads, which), qkv_early, NT).astype(jnp.bfloat16)

    give_early, keep_early = gx_early(1 - core), gx_early(core)
    g, early_kept, give_early, keep_early, *early_moved = lax.optimization_barrier(
        (g, early_kept, give_early, keep_early, *early_moved)
    )
    early_moved = chip_moves(early_moved)
    att_2, grads_2 = attention(projected, g, bias, hot, 2, lanes)
    att_2, grads_2, *early_moved = lax.optimization_barrier((att_2, grads_2, *early_moved))
    grads_2 = grads_2.reshape(-1, per)

    def gx_late(which, before):
        return dot(half_rows(grads_2, which), qkv_rest[:, per:], NT) + before.astype(jnp.float32)

    out_rows.append(dot(att_2, go).astype(jnp.bfloat16))
    out_rows = jnp.concatenate(out_rows, axis=0)
    swapped = partner(lax.dynamic_slice_in_dim(out_rows, (1 - core) * half, half, 1))
    give = gx_late(1 - core, give_early).astype(jnp.bfloat16)
    given = partner(give)
    late = dot(x_turned, after(grads_2, give)).astype(jnp.bfloat16)
    out_mine = by_core(core, lax.dynamic_slice_in_dim(out_rows, core * half, half, 1), swapped, 0)
    late_kept, late_moved = scatter_split([late, out_mine], chip)
    given, *late_moved = lax.optimization_barrier((given, *late_moved))
    late_moved = chip_moves(late_moved)
    early = added(early_kept.astype(jnp.float32), early_moved)
    gx = gx_late(core, after(keep_early, give)) + given.astype(jnp.float32)
    gx = gx.reshape(wide_rows // 2, wide_cols, width)
    own = wide_rows // 2 - RADIUS
    outer = jnp.where(core == 0, gx[:RADIUS], gx[own:]).astype(jnp.bfloat16)
    gx = jnp.where(core == 0, gx[RADIUS:], gx[:own])
    inner = routed(outer, lambda a, o: (a + 1, o - 1) if o % 2 else (a - 1, o + 1))
    early = after(early, outer)
    early_moved = [pick(early, lat + d, lats, 0).astype(jnp.bfloat16) for d in range(1, lats)]
    for d in range(1, min(lats, chips) - 1):
        early_moved[d], late_moved[d - 1] = lax.optimization_barrier((early_moved[d], late_moved[d - 1]))
    early_moved = lat_moves(early_moved)
    inner, *moved = lax.optimization_barrier((inner, *early_moved, *late_moved))
    early = added(pick(early, lat, lats, 0), moved[: lats - 1])
    late_moved = moved[lats - 1 :]
    inner = inner.astype(jnp.float32)
    late = scatter_rest(added(late_kept, late_moved), lat)
    gap = jnp.zeros((own - RADIUS,) + gx.shape[1:], jnp.float32)
    gx = gx + by_core(core, inner, gap, 0)
    other_half = lax.dynamic_slice_in_dim(gx, MARGIN + (1 - core) * lon_cols, lon_cols, 1)
    mine_half = lax.dynamic_slice_in_dim(gx, MARGIN + core * lon_cols, lon_cols, 1)
    left, right = gx[:, :MARGIN].astype(jnp.bfloat16), gx[:, wide_cols - MARGIN :].astype(jnp.bfloat16)
    same = routed(jnp.where(core == 0, right, left), lambda a, o: (a, o - 2 if o % 2 else o + 2))
    cross = routed(jnp.where(core == 0, left, right), lambda a, o: (a, o + 1 if o % 2 else o - 1))
    swapped_x = partner(other_half.astype(jnp.bfloat16))
    pad = jnp.zeros((own, lon_cols - MARGIN, width), jnp.float32)
    here = mine_half + by_core(core, same.astype(jnp.float32), pad, 1)
    there = swapped_x.astype(jnp.float32) + by_core(core, cross.astype(jnp.float32), pad, 1)
    grad_x = by_core(core, here.astype(jnp.bfloat16), there.astype(jnp.bfloat16), 0)

    total = jnp.concatenate([early, late], axis=1).reshape(2, rows, -1)
    keep = lax.dynamic_index_in_dim(total, core, 0, keepdims=False)
    give = lax.dynamic_index_in_dim(total, 1 - core, 0, keepdims=False).astype(jnp.bfloat16)
    got = partner(give).astype(jnp.float32)
    order = jnp.where(core == 0, jnp.stack([keep, got]), jnp.stack([got, keep]))
    grad_qkv = order[:, :, : groups * per].reshape(2, rows, groups, 3, lanes)
    grad_qkv = jnp.transpose(grad_qkv, (1, 3, 0, 2, 4)).reshape(rows, 3 * width)
    grad_out = jnp.transpose(order[:, :, groups * per :], (1, 0, 2)).reshape(rows, width)
    return grad_x, grad_qkv, grad_out


def solution(mesh):
    placed = (
        P("lat", "lon", None),
        P("lat", "lon", None),
        P(("lat", "lon"), None),
        P(("lat", "lon"), None),
    )
    return jax.shard_map(
        shards,
        mesh=mesh,
        in_specs=placed,
        out_specs=(P("lat", "lon", None), P(("lat", "lon"), None), P(("lat", "lon"), None)),
        check_vma=False,
    )
```

```python
import math

import jax
import jax.numpy as jnp
from jax import lax
from jax.experimental import pallas as pl
from jax.experimental.pallas import tpu as pltpu
from jax.sharding import PartitionSpec as P

HEADS = 12
RADIUS = 6
QROWS = 16
QCOLS = 16
MARGIN = 8
PAIR = 2
OUTSIDE = -1e30
LOG2E = math.log2(math.e)

NT = (((1,), (1,)), ((), ()))
NN = (((1,), (0,)), ((), ()))


def dot(a, b, dims=NN):
    return lax.dot_general(a, b, dims, preferred_element_type=jnp.float32)


def attention_kernel(p_ref, g_ref, bias_ref, hot_ref, att_ref, grad_ref, *scratch):
    scores, e_both, ds_both, sums = scratch[:PAIR], scratch[PAIR], scratch[PAIR + 1], scratch[PAIR + 2]
    tile_row, tile_col = pl.program_id(0), pl.program_id(1)
    key_rows, key_cols = QROWS + 2 * RADIUS, QCOLS + 2 * MARGIN
    keys, queries = key_rows * key_cols, QROWS * QCOLS
    lanes = g_ref.shape[-1]
    head = lanes // PAIR
    chunk = 64
    first_row = tile_row * QROWS
    first_col = pl.multiple_of(tile_col * QCOLS, QCOLS)
    at_rows, at_cols = pl.ds(first_row, key_rows), pl.ds(first_col, key_cols)
    q_lanes, k_lanes, v_lanes = (slice(i * lanes, (i + 1) * lanes) for i in range(3))
    heads = range(PAIR)
    rows = [slice(h * head, (h + 1) * head) for h in heads]
    cols = [slice(h * queries, (h + 1) * queries) for h in heads]

    @pl.when((tile_row == 0) & (tile_col == 0))
    def _():
        sums[...] = jnp.zeros_like(sums)

    q = p_ref[pl.ds(first_row + RADIUS, QROWS), at_cols, q_lanes].astype(jnp.float32)
    q = q[:, MARGIN : MARGIN + QCOLS].reshape(queries, lanes).astype(jnp.bfloat16)
    g_t = g_ref[...].astype(jnp.float32).T
    k = p_ref[at_rows, at_cols, k_lanes].reshape(keys, lanes)
    v = p_ref[at_rows, at_cols, v_lanes].reshape(keys, lanes)
    k_wide = jnp.concatenate([k, bias_ref[0]], axis=1)
    ones = jnp.ones((16, keys), jnp.bfloat16)
    lane = lax.broadcasted_iota(jnp.int32, (queries, lanes), 1) // head
    q_heads = [jnp.where(lane == h, q, jnp.zeros_like(q)) for h in heads]
    for h in heads:
        scores[h][...] = dot(k_wide, jnp.concatenate([q_heads[h], hot_ref[...]], axis=1), NT)
    k_t, v_t = k.T, v.T
    g_heads, att_t, dq_t, terms = [], [], [], []
    for h in heads:
        top = jnp.max(scores[h][...], axis=0, keepdims=True)
        for c in range(0, keys, chunk):
            e_both[c : c + chunk, cols[h]] = jnp.exp2(scores[h][c : c + chunk] - top).astype(jnp.bfloat16)
        out = dot(jnp.concatenate([v_t[rows[h]], ones], axis=0), e_both[:, cols[h]])
        inverse = 1.0 / out[head : head + 1]
        attended = (out[:head] * inverse).astype(jnp.bfloat16).astype(jnp.float32)
        att_t.append(attended)
        g_one = g_t[rows[h]] * inverse
        terms.append(jnp.sum(g_one * attended, axis=0, keepdims=True))
        empty = jnp.zeros_like(g_one)
        g_one = jnp.concatenate([empty] * h + [g_one] + [empty] * (PAIR - 1 - h), axis=0).astype(jnp.bfloat16)
        g_heads.append(g_one)
    for h in heads:
        scores[h][...] = dot(v, g_heads[h])
    for h in heads:
        for c in range(0, keys, chunk):
            ds_both[c : c + chunk, cols[h]] = (
                e_both[c : c + chunk, cols[h]].astype(jnp.float32) * (scores[h][c : c + chunk] - terms[h])
            ).astype(jnp.bfloat16)
        dq_t.append(dot(k_t[rows[h]], ds_both[:, cols[h]]))
    tile = (key_rows, key_cols, lanes)
    sums[at_rows, at_cols, v_lanes] += dot(e_both[...], jnp.concatenate(g_heads, axis=1), NT).reshape(tile)
    sums[at_rows, at_cols, k_lanes] += dot(ds_both[...], jnp.concatenate(q_heads, axis=0)).reshape(tile)
    att_ref[...] = jnp.concatenate(att_t, axis=0).astype(jnp.bfloat16)
    dq = jnp.concatenate(dq_t, axis=0).T * (1.0 / math.sqrt(head))
    sums[pl.ds(first_row + RADIUS, QROWS), pl.ds(pl.multiple_of(first_col + MARGIN, 8), QCOLS), q_lanes] = dq.reshape(
        QROWS, QCOLS, lanes
    )

    @pl.when((tile_row == pl.num_programs(0) - 1) & (tile_col == pl.num_programs(1) - 1))
    def _():
        grad_ref[:, :, q_lanes] = sums[:, :, q_lanes].astype(jnp.bfloat16)
        grad_ref[:, :, k_lanes] = (sums[:, :, k_lanes] * (1.0 / LOG2E)).astype(jnp.bfloat16)
        grad_ref[:, :, v_lanes] = sums[:, :, v_lanes].astype(jnp.bfloat16)


def attention(projected, g, bias, hot, place, g_place, lanes):
    wide = projected.shape[:2] + (3 * lanes,)
    queries, keys = QROWS * QCOLS, (QROWS + 2 * RADIUS) * (QCOLS + 2 * MARGIN)
    tiles = ((wide[0] - 2 * RADIUS) // QROWS, (wide[1] - 2 * MARGIN) // QCOLS)
    count = tiles[0] * tiles[1]
    return pl.pallas_call(
        attention_kernel,
        grid=tiles,
        in_specs=[
            pl.BlockSpec(wide, lambda r, c: (0, 0, place)),
            pl.BlockSpec((queries, lanes), lambda r, c: (r * tiles[1] + c, g_place)),
            pl.BlockSpec((1, keys, lanes), lambda r, c: (r, 0, 0)),
            pl.BlockSpec((queries, lanes), lambda r, c: (0, 0)),
        ],
        out_specs=[
            pl.BlockSpec((lanes, queries), lambda r, c: (0, r * tiles[1] + c)),
            pl.BlockSpec(wide, lambda r, c: (0, 0, 0)),
        ],
        out_shape=[
            jax.ShapeDtypeStruct((lanes, count * queries), jnp.bfloat16),
            jax.ShapeDtypeStruct(wide, jnp.bfloat16),
        ],
        scratch_shapes=[pltpu.VMEM((keys, queries), jnp.float32)] * PAIR
        + [pltpu.VMEM((keys, PAIR * queries), jnp.bfloat16)] * 2
        + [pltpu.VMEM(wide, jnp.float32)],
        compiler_params=pltpu.CompilerParams(
            dimension_semantics=("arbitrary", "arbitrary"), vmem_limit_bytes=48 * 1024 * 1024
        ),
        cost_estimate=pl.CostEstimate(
            flops=2 * 12 * 256 * keys * queries * PAIR * count,
            bytes_accessed=12 * count * queries * lanes * 2,
            transcendentals=keys * queries * PAIR * count,
        ),
    )(projected, g, bias, hot)


def window_columns(lat_first, tile_rows, total_rows, lanes):
    key_rows, key_cols = QROWS + 2 * RADIUS, QCOLS + 2 * MARGIN
    base = lat_first + QROWS * jnp.arange(tile_rows, dtype=jnp.int32)[:, None, None]
    q_row = base + jnp.arange(QROWS, dtype=jnp.int32)[None, None, :]
    k_row = base - RADIUS + jnp.arange(key_rows, dtype=jnp.int32)[None, :, None]
    start = jnp.clip(q_row - RADIUS, 0, total_rows - 2 * RADIUS - 1)
    row_in = (k_row >= start) & (k_row <= start + 2 * RADIUS)
    q_col = jnp.arange(QCOLS, dtype=jnp.int32)[None, :]
    k_col = jnp.arange(key_cols, dtype=jnp.int32)[:, None] - MARGIN
    col_in = (k_col >= q_col - RADIUS) & (k_col <= q_col + RADIUS)
    shape = (tile_rows, key_rows, key_cols)
    row_part = jnp.broadcast_to(jnp.where(row_in, 0.0, OUTSIDE)[:, :, None, :], shape + (QROWS,))
    col_part = jnp.broadcast_to(jnp.where(col_in, 0.0, OUTSIDE)[None, None], shape + (QCOLS,))
    rest = jnp.zeros(shape + (lanes - QROWS - QCOLS,), jnp.float32)
    columns = jnp.concatenate([row_part, col_part, rest], axis=-1).astype(jnp.bfloat16)
    columns = columns.reshape(tile_rows, key_rows * key_cols, lanes)
    r, c = jnp.arange(QROWS * QCOLS) // QCOLS, jnp.arange(QROWS * QCOLS) % QCOLS
    lane = jnp.arange(lanes)[None, :]
    hot = ((lane == r[:, None]) | (lane == QROWS + c[:, None])).astype(jnp.bfloat16)
    return columns, hot


def routed(value, route):
    lats, lons = lax.axis_size("lat"), lax.axis_size("lon")
    pairs = []
    for a in range(lats):
        for o in range(lons):
            to_lat, to_lon = route(a, o)
            if 0 <= to_lat < lats:
                pairs.append((a * lons + o, to_lat * lons + to_lon % lons))
    return lax.ppermute(value, ("lat", "lon"), pairs)


def partner(value):
    return routed(value, lambda a, o: (a, o ^ 1))


def beside(o):
    return o + 1 if o % 2 else o - 1


def by_core(core, mine, other, axis):
    return jnp.where(
        core == 0, jnp.concatenate([mine, other], axis=axis), jnp.concatenate([other, mine], axis=axis)
    )


def turned(parts, by):
    count = len(parts)
    whole = jnp.zeros((count,) + parts[0].shape, parts[0].dtype)
    for d, part in enumerate(parts):
        whole = lax.dynamic_update_index_in_dim(whole, part, (by - d) % count, 0)
    return whole


def lat_moves(blocks):
    lats = lax.axis_size("lat")
    return [routed(part, lambda a, o, d=d + 1: ((a + d) % lats, o)) for d, part in enumerate(blocks)]


def chip_moves(blocks):
    return [routed(part, lambda a, o, d=d + 1: (a, o + 2 * d)) for d, part in enumerate(blocks)]


def gather_rows(parts, chip):
    grid = turned(parts, chip)
    return jnp.swapaxes(grid, 0, 1).reshape((-1,) + grid.shape[3:])


def pick(value, index, count, dim):
    return lax.dynamic_index_in_dim(value, index % count, dim, keepdims=False)


def scatter_split(totals, chip):
    lats, chips = lax.axis_size("lat"), lax.axis_size("lon") // 2
    totals = [total.reshape(lats, chips, -1, total.shape[1]) for total in totals]
    blocks = [jnp.concatenate([pick(total, chip + d, chips, 1) for total in totals], axis=-1) for d in range(chips)]
    return blocks[0].astype(jnp.float32), blocks[1:]


def added(kept, parts):
    for part in parts:
        kept = kept + part.astype(jnp.float32)
    return kept


def scatter_rest(kept, lat):
    lats = lax.axis_size("lat")
    moved = lat_moves([pick(kept, lat + d, lats, 0).astype(jnp.bfloat16) for d in range(1, lats)])
    return added(pick(kept, lat, lats, 0), moved)


def after(value, *others):
    return lax.optimization_barrier((value,) + others)[0]


def shards(features, grad_output, qkv_weight, out_weight):
    lat_rows, lon_cols, width = features.shape
    head = width // HEADS
    lanes = PAIR * head
    groups = HEADS // PAIR // 2
    half = width // 2
    lats, chips = lax.axis_size("lat"), lax.axis_size("lon") // 2
    lat, lon = lax.axis_index("lat"), lax.axis_index("lon")
    core, chip = lon % 2, lon // 2
    rows = qkv_weight.shape[0]
    per = 3 * lanes
    cells = lat_rows * lon_cols
    block_cols = 2 * lon_cols
    half_cols = lon_cols + MARGIN

    edge = jnp.where(core == 0, features[:, :MARGIN], features[:, lon_cols - MARGIN :])
    side = routed(edge, lambda a, o: (a, beside(o)))

    by_heads = qkv_weight.reshape(rows, 3, 2, groups, lanes)
    first = [by_heads[:, i, c, 0] for c in range(2) for i in range(3)]
    first = after(jnp.concatenate(first + [out_weight], axis=1), edge)
    first_moved = lat_moves([first] * (lats - 1))

    def columns(which):
        qkv = lax.dynamic_index_in_dim(by_heads, which, 2, keepdims=False)[:, :, 1:]
        return jnp.swapaxes(qkv, 1, 2).reshape(rows, -1)

    both = [features.reshape(cells, width), grad_output.reshape(cells, width), side.reshape(-1, width)]
    both.append(columns(1 - core).reshape(-1, width))
    both = jnp.concatenate(both, axis=0)
    near = jnp.where(
        core == 0, jnp.concatenate([side, features], axis=1), jnp.concatenate([features, side], axis=1)
    )
    top, bottom = near[:RADIUS], near[lat_rows - RADIUS :]
    first = after(turned([first] + first_moved, lat), both, top, bottom)
    both = partner(both)
    above = routed(bottom, lambda a, o: (a + 1, o))
    below = routed(top, lambda a, o: (a - 1, o))
    first_moved = chip_moves([first] * (chips - 1))
    margin = MARGIN * lat_rows
    x_partner = both[:cells].reshape(features.shape)
    go_partner = both[cells : 2 * cells].reshape(features.shape)
    side_partner = both[2 * cells : 2 * cells + margin].reshape(side.shape)
    rest = by_core(core, columns(core), both[2 * cells + margin :].reshape(rows, -1), 0)
    far = jnp.where(
        core == 0,
        jnp.concatenate([x_partner, side_partner], axis=1),
        jnp.concatenate([side_partner, x_partner], axis=1),
    )
    rest, above, below, far = lax.optimization_barrier((rest, above, below, far))
    rest_moved = lat_moves([rest] * (lats - 1))
    moved = lax.optimization_barrier((above, below, *first_moved, *rest_moved[:-1]))
    above, below, first_moved, rest_moved[:-1] = moved[0], moved[1], list(moved[2 : chips + 1]), moved[chips + 1 :]
    caps = partner(jnp.concatenate([above, below], axis=0))
    near = jnp.concatenate([above, near, below], axis=0)
    far = jnp.concatenate([caps[:RADIUS], far, caps[RADIUS:]], axis=0)
    wide_rows = near.shape[0]
    first = turned([first] + first_moved, chip)
    first = jnp.swapaxes(first, 0, 1).reshape(lats * chips, rows, -1)
    x_wide = by_core(core, near, far, 1)
    wide_cols = x_wide.shape[1]
    x_wide = x_wide.reshape(-1, width)
    x_turned = lax.optimization_barrier(x_wide.T)
    go = by_core(core, grad_output, go_partner, 1)
    go = go.reshape(lat_rows // QROWS, QROWS, block_cols // QCOLS, QCOLS, width)
    go = lax.optimization_barrier(jnp.swapaxes(go, 1, 2).reshape(-1, width))

    def heads_of(which):
        qkv = lax.dynamic_slice_in_dim(first, which * per, per, 2).reshape(half, per)
        count = lats * chips // 2
        out = lax.dynamic_slice_in_dim(first, which * count, count, 0)[..., 2 * per :].reshape(-1, width)
        return qkv, out

    qkv_mine, out_mine = heads_of(core)
    qkv_other, out_other = heads_of(1 - core)
    cut = out_other.shape[0]
    swap = jnp.concatenate([jnp.concatenate([qkv_other[:cut], qkv_other[cut:]], axis=1), out_other], axis=0)
    swap = partner(swap)
    qkv_got = jnp.concatenate([swap[:cut, :per], swap[:cut, per:]], axis=0)

    def interleaved(mine, got):
        mine, got = (part.reshape(-1, rows, part.shape[1]) for part in (mine, got))
        return by_core(core, mine, got, 1).reshape(-1, mine.shape[2])

    qkv_first = interleaved(qkv_mine, qkv_got)
    out_heads = interleaved(out_mine, swap[cut:])

    bias, hot = window_columns(lat * lat_rows, lat_rows // QROWS, lat_rows * lats, lanes)
    scale = jnp.concatenate(
        [jnp.full((lanes,), LOG2E / math.sqrt(head), jnp.float32), jnp.ones((2 * lanes,), jnp.float32)]
    )

    def project(weights):
        result = dot(x_wide, weights) * jnp.tile(scale, weights.shape[1] // per)
        return result.astype(jnp.bfloat16).reshape(wide_rows, wide_cols, -1)

    def half_rows(grads, which):
        return lax.dynamic_slice_in_dim(grads, which * (grads.shape[0] // 2), grads.shape[0] // 2, 0)

    projected = project(qkv_first)
    g = dot(go, out_heads, NT).astype(jnp.bfloat16)
    rest = turned([rest] + list(rest_moved), lat)
    projected, g, rest = lax.optimization_barrier((projected, g, rest))
    rest_moved = chip_moves([rest] * (chips - 1))
    att_0, grads_0 = attention(projected, g, bias, hot, 0, 0, lanes)
    grads_0 = grads_0.reshape(-1, per)
    early_0 = dot(x_turned, grads_0).astype(jnp.bfloat16)
    early_0, *rest_moved = lax.optimization_barrier((early_0, *rest_moved))
    qkv_rest = gather_rows([rest] + rest_moved, chip)
    projected = project(qkv_rest[:, :per])
    att_1, grads_1 = attention(projected, g, bias, hot, 0, 1, lanes)
    projected = project(qkv_rest[:, per:])

    grads_1 = grads_1.reshape(-1, per)
    early = [early_0, dot(x_turned, grads_1).astype(jnp.bfloat16)]
    early_kept, early_moved = scatter_split(early, chip)

    def gx_early(which):
        first_part = dot(half_rows(grads_0, which), qkv_first, NT)
        return (first_part + dot(half_rows(grads_1, which), qkv_rest[:, :per], NT)).astype(jnp.bfloat16)

    give_early, keep_early = gx_early(1 - core), gx_early(core)
    out_rows = [dot(part, go).astype(jnp.bfloat16) for part in (att_0, att_1)]
    g, early_kept, give_early, keep_early, *early_moved, = lax.optimization_barrier(
        (g, early_kept, give_early, keep_early, *early_moved)
    )
    early_moved = chip_moves(early_moved)
    att_2, grads_2 = attention(projected, g, bias, hot, 0, 2, lanes)
    grads_2 = grads_2.reshape(-1, per)

    def gx_late(which, before):
        return dot(half_rows(grads_2, which), qkv_rest[:, per:], NT) + before.astype(jnp.float32)

    give = gx_late(1 - core, give_early).astype(jnp.bfloat16)
    give, att_2, grads_2, *early_moved = lax.optimization_barrier((give, att_2, grads_2, *early_moved))
    given = partner(give)
    out_rows.append(dot(att_2, go).astype(jnp.bfloat16))
    out_rows = jnp.concatenate(out_rows, axis=0)
    swapped = partner(lax.dynamic_slice_in_dim(out_rows, (1 - core) * half, half, 1))
    late = dot(x_turned, grads_2).astype(jnp.bfloat16)
    out_mine = by_core(core, lax.dynamic_slice_in_dim(out_rows, core * half, half, 1), swapped, 0)
    late_kept, late_moved = scatter_split([late, out_mine], chip)
    given, *late_moved = lax.optimization_barrier((given, *late_moved))
    late_moved = chip_moves(late_moved)
    early = added(early_kept, early_moved)
    gx = gx_late(core, keep_early) + given.astype(jnp.float32)
    gx = gx.reshape(wide_rows // 2, wide_cols, width)
    own = wide_rows // 2 - RADIUS
    outer = jnp.where(core == 0, gx[:RADIUS], gx[own:]).astype(jnp.bfloat16)
    gx = jnp.where(core == 0, gx[RADIUS:], gx[:own])
    inner = routed(outer, lambda a, o: (a + 1, o - 1) if o % 2 else (a - 1, o + 1))
    early = after(early, outer)
    early_moved = [pick(early, lat + d, lats, 0).astype(jnp.bfloat16) for d in range(1, lats)]
    for d in range(1, min(lats, chips) - 1):
        early_moved[d], late_moved[d - 1] = lax.optimization_barrier((early_moved[d], late_moved[d - 1]))
    early_moved = lat_moves(early_moved)
    inner, *moved = lax.optimization_barrier((inner, *early_moved, *late_moved))
    early = added(pick(early, lat, lats, 0), moved[: lats - 1])
    late_moved = moved[lats - 1 :]
    inner = inner.astype(jnp.float32)
    late = scatter_rest(added(late_kept, late_moved), lat)
    gap = jnp.zeros((own - RADIUS,) + gx.shape[1:], jnp.float32)
    gx = gx + by_core(core, inner, gap, 0)
    other_half = lax.dynamic_slice_in_dim(gx, MARGIN + (1 - core) * lon_cols, lon_cols, 1)
    mine_half = lax.dynamic_slice_in_dim(gx, MARGIN + core * lon_cols, lon_cols, 1)
    left, right = gx[:, :MARGIN].astype(jnp.bfloat16), gx[:, wide_cols - MARGIN :].astype(jnp.bfloat16)
    same = routed(jnp.where(core == 0, right, left), lambda a, o: (a, o - 2 if o % 2 else o + 2))
    cross = routed(jnp.where(core == 0, left, right), lambda a, o: (a, o + 1 if o % 2 else o - 1))
    swapped_x = partner(other_half.astype(jnp.bfloat16))
    pad = jnp.zeros((own, lon_cols - MARGIN, width), jnp.float32)
    here = mine_half + by_core(core, same.astype(jnp.float32), pad, 1)
    there = swapped_x.astype(jnp.float32) + by_core(core, cross.astype(jnp.float32), pad, 1)
    grad_x = by_core(core, here.astype(jnp.bfloat16), there.astype(jnp.bfloat16), 0)

    total = jnp.concatenate([early, late], axis=1).reshape(2, rows, -1)
    keep = lax.dynamic_index_in_dim(total, core, 0, keepdims=False)
    give = lax.dynamic_index_in_dim(total, 1 - core, 0, keepdims=False).astype(jnp.bfloat16)
    got = partner(give).astype(jnp.float32)
    order = jnp.where(core == 0, jnp.stack([keep, got]), jnp.stack([got, keep]))
    grad_qkv = order[:, :, : groups * per].reshape(2, rows, groups, 3, lanes)
    grad_qkv = jnp.transpose(grad_qkv, (1, 3, 0, 2, 4)).reshape(rows, 3 * width)
    grad_out = jnp.transpose(order[:, :, groups * per :], (1, 0, 2)).reshape(rows, width)
    return grad_x, grad_qkv, grad_out


def solution(mesh):
    placed = (
        P("lat", "lon", None),
        P("lat", "lon", None),
        P(("lat", "lon"), None),
        P(("lat", "lon"), None),
    )
    return jax.shard_map(
        shards,
        mesh=mesh,
        in_specs=placed,
        out_specs=(P("lat", "lon", None), P(("lat", "lon"), None), P(("lat", "lon"), None)),
        check_vma=False,
    )
```

```python
import math

import jax
import jax.numpy as jnp
from jax import lax
from jax.experimental import pallas as pl
from jax.experimental.pallas import tpu as pltpu
from jax.sharding import PartitionSpec as P

HEADS = 12
RADIUS = 6
QROWS = 16
QCOLS = 16
MARGIN = 8
PAIR = 2
OUTSIDE = -1e30
LOG2E = math.log2(math.e)

NT = (((1,), (1,)), ((), ()))
NN = (((1,), (0,)), ((), ()))


def dot(a, b, dims=NN):
    return lax.dot_general(a, b, dims, preferred_element_type=jnp.float32)


def attention_kernel(p_ref, g_ref, bias_ref, hot_ref, att_ref, grad_ref, *scratch):
    scores, e_both, ds_both, sums = scratch[:PAIR], scratch[PAIR], scratch[PAIR + 1], scratch[PAIR + 2]
    tile_row, tile_col = pl.program_id(0), pl.program_id(1)
    key_rows, key_cols = QROWS + 2 * RADIUS, QCOLS + 2 * MARGIN
    keys, queries = key_rows * key_cols, QROWS * QCOLS
    lanes = g_ref.shape[-1]
    head = lanes // PAIR
    chunk = 64
    first_row = tile_row * QROWS
    first_col = pl.multiple_of(tile_col * QCOLS, QCOLS)
    at_rows, at_cols = pl.ds(first_row, key_rows), pl.ds(first_col, key_cols)
    q_lanes, k_lanes, v_lanes = (slice(i * lanes, (i + 1) * lanes) for i in range(3))
    heads = range(PAIR)
    rows = [slice(h * head, (h + 1) * head) for h in heads]
    cols = [slice(h * queries, (h + 1) * queries) for h in heads]

    @pl.when((tile_row == 0) & (tile_col == 0))
    def _():
        sums[...] = jnp.zeros_like(sums)

    q = p_ref[pl.ds(first_row + RADIUS, QROWS), at_cols, q_lanes].astype(jnp.float32)
    q = q[:, MARGIN : MARGIN + QCOLS].reshape(queries, lanes).astype(jnp.bfloat16)
    g_t = g_ref[...].astype(jnp.float32).T
    k = p_ref[at_rows, at_cols, k_lanes].reshape(keys, lanes)
    v = p_ref[at_rows, at_cols, v_lanes].reshape(keys, lanes)
    k_wide = jnp.concatenate([k, bias_ref[0]], axis=1)
    ones = jnp.ones((16, keys), jnp.bfloat16)
    lane = lax.broadcasted_iota(jnp.int32, (queries, lanes), 1) // head
    q_heads = [jnp.where(lane == h, q, jnp.zeros_like(q)) for h in heads]
    for h in heads:
        scores[h][...] = dot(k_wide, jnp.concatenate([q_heads[h], hot_ref[...]], axis=1), NT)
    k_t, v_t = k.T, v.T
    g_heads, att_t, dq_t, terms = [], [], [], []
    for h in heads:
        top = jnp.max(scores[h][...], axis=0, keepdims=True)
        for c in range(0, keys, chunk):
            e_both[c : c + chunk, cols[h]] = jnp.exp2(scores[h][c : c + chunk] - top).astype(jnp.bfloat16)
        out = dot(jnp.concatenate([v_t[rows[h]], ones], axis=0), e_both[:, cols[h]])
        inverse = 1.0 / out[head : head + 1]
        attended = (out[:head] * inverse).astype(jnp.bfloat16).astype(jnp.float32)
        att_t.append(attended)
        g_one = g_t[rows[h]] * inverse
        terms.append(jnp.sum(g_one * attended, axis=0, keepdims=True))
        empty = jnp.zeros_like(g_one)
        g_one = jnp.concatenate([empty] * h + [g_one] + [empty] * (PAIR - 1 - h), axis=0).astype(jnp.bfloat16)
        g_heads.append(g_one)
    for h in heads:
        scores[h][...] = dot(v, g_heads[h])
    for h in heads:
        for c in range(0, keys, chunk):
            ds_both[c : c + chunk, cols[h]] = (
                e_both[c : c + chunk, cols[h]].astype(jnp.float32) * (scores[h][c : c + chunk] - terms[h])
            ).astype(jnp.bfloat16)
        dq_t.append(dot(k_t[rows[h]], ds_both[:, cols[h]]))
    tile = (key_rows, key_cols, lanes)
    sums[at_rows, at_cols, v_lanes] += dot(e_both[...], jnp.concatenate(g_heads, axis=1), NT).reshape(tile)
    sums[at_rows, at_cols, k_lanes] += dot(ds_both[...], jnp.concatenate(q_heads, axis=0)).reshape(tile)
    att_ref[...] = jnp.concatenate(att_t, axis=0).astype(jnp.bfloat16)
    dq = jnp.concatenate(dq_t, axis=0).T * (1.0 / math.sqrt(head))
    sums[pl.ds(first_row + RADIUS, QROWS), pl.ds(pl.multiple_of(first_col + MARGIN, 8), QCOLS), q_lanes] = dq.reshape(
        QROWS, QCOLS, lanes
    )

    @pl.when((tile_row == pl.num_programs(0) - 1) & (tile_col == pl.num_programs(1) - 1))
    def _():
        grad_ref[:, :, q_lanes] = sums[:, :, q_lanes].astype(jnp.bfloat16)
        grad_ref[:, :, k_lanes] = (sums[:, :, k_lanes] * (1.0 / LOG2E)).astype(jnp.bfloat16)
        grad_ref[:, :, v_lanes] = sums[:, :, v_lanes].astype(jnp.bfloat16)


def attention(projected, g, bias, hot, place, g_place, lanes):
    wide = projected.shape[:2] + (3 * lanes,)
    queries, keys = QROWS * QCOLS, (QROWS + 2 * RADIUS) * (QCOLS + 2 * MARGIN)
    tiles = ((wide[0] - 2 * RADIUS) // QROWS, (wide[1] - 2 * MARGIN) // QCOLS)
    count = tiles[0] * tiles[1]
    return pl.pallas_call(
        attention_kernel,
        grid=tiles,
        in_specs=[
            pl.BlockSpec(wide, lambda r, c: (0, 0, place)),
            pl.BlockSpec((queries, lanes), lambda r, c: (r * tiles[1] + c, g_place)),
            pl.BlockSpec((1, keys, lanes), lambda r, c: (r, 0, 0)),
            pl.BlockSpec((queries, lanes), lambda r, c: (0, 0)),
        ],
        out_specs=[
            pl.BlockSpec((lanes, queries), lambda r, c: (0, r * tiles[1] + c)),
            pl.BlockSpec(wide, lambda r, c: (0, 0, 0)),
        ],
        out_shape=[
            jax.ShapeDtypeStruct((lanes, count * queries), jnp.bfloat16),
            jax.ShapeDtypeStruct(wide, jnp.bfloat16),
        ],
        scratch_shapes=[pltpu.VMEM((keys, queries), jnp.float32)] * PAIR
        + [pltpu.VMEM((keys, PAIR * queries), jnp.bfloat16)] * 2
        + [pltpu.VMEM(wide, jnp.float32)],
        compiler_params=pltpu.CompilerParams(
            dimension_semantics=("arbitrary", "arbitrary"), vmem_limit_bytes=48 * 1024 * 1024
        ),
        cost_estimate=pl.CostEstimate(
            flops=2 * 12 * 256 * keys * queries * PAIR * count,
            bytes_accessed=12 * count * queries * lanes * 2,
            transcendentals=keys * queries * PAIR * count,
        ),
    )(projected, g, bias, hot)


def window_columns(lat_first, tile_rows, total_rows, lanes):
    key_rows, key_cols = QROWS + 2 * RADIUS, QCOLS + 2 * MARGIN
    base = lat_first + QROWS * jnp.arange(tile_rows, dtype=jnp.int32)[:, None, None]
    q_row = base + jnp.arange(QROWS, dtype=jnp.int32)[None, None, :]
    k_row = base - RADIUS + jnp.arange(key_rows, dtype=jnp.int32)[None, :, None]
    start = jnp.clip(q_row - RADIUS, 0, total_rows - 2 * RADIUS - 1)
    row_in = (k_row >= start) & (k_row <= start + 2 * RADIUS)
    q_col = jnp.arange(QCOLS, dtype=jnp.int32)[None, :]
    k_col = jnp.arange(key_cols, dtype=jnp.int32)[:, None] - MARGIN
    col_in = (k_col >= q_col - RADIUS) & (k_col <= q_col + RADIUS)
    shape = (tile_rows, key_rows, key_cols)
    row_part = jnp.broadcast_to(jnp.where(row_in, 0.0, OUTSIDE)[:, :, None, :], shape + (QROWS,))
    col_part = jnp.broadcast_to(jnp.where(col_in, 0.0, OUTSIDE)[None, None], shape + (QCOLS,))
    rest = jnp.zeros(shape + (lanes - QROWS - QCOLS,), jnp.float32)
    columns = jnp.concatenate([row_part, col_part, rest], axis=-1).astype(jnp.bfloat16)
    columns = columns.reshape(tile_rows, key_rows * key_cols, lanes)
    r, c = jnp.arange(QROWS * QCOLS) // QCOLS, jnp.arange(QROWS * QCOLS) % QCOLS
    lane = jnp.arange(lanes)[None, :]
    hot = ((lane == r[:, None]) | (lane == QROWS + c[:, None])).astype(jnp.bfloat16)
    return columns, hot


def routed(value, route):
    lats, lons = lax.axis_size("lat"), lax.axis_size("lon")
    pairs = []
    for a in range(lats):
        for o in range(lons):
            to_lat, to_lon = route(a, o)
            if 0 <= to_lat < lats:
                pairs.append((a * lons + o, to_lat * lons + to_lon % lons))
    return lax.ppermute(value, ("lat", "lon"), pairs)


def partner(value):
    return routed(value, lambda a, o: (a, o ^ 1))


def beside(o):
    return o + 1 if o % 2 else o - 1


def by_core(core, mine, other, axis):
    return jnp.where(
        core == 0, jnp.concatenate([mine, other], axis=axis), jnp.concatenate([other, mine], axis=axis)
    )


def turned(parts, by):
    count = len(parts)
    whole = jnp.zeros((count,) + parts[0].shape, parts[0].dtype)
    for d, part in enumerate(parts):
        whole = lax.dynamic_update_index_in_dim(whole, part, (by - d) % count, 0)
    return whole


def lat_moves(blocks):
    lats = lax.axis_size("lat")
    return [routed(part, lambda a, o, d=d + 1: ((a + d) % lats, o)) for d, part in enumerate(blocks)]


def lon_bits():
    return (lax.axis_size("lon") // 2 - 1).bit_length()


def across(value, phase):
    last = lon_bits() - 1
    return routed(value, lambda a, o: (a, o ^ (2 << (last - phase if o % 2 else phase))))


def own_bit(core, chip, phase):
    return (chip >> jnp.where(core == 0, phase, lon_bits() - 1 - phase)) & 1


def joined(held, got, core, chip, phase):
    bit = own_bit(core, chip, phase)
    low, high = jnp.where(bit == 0, held, got), jnp.where(bit == 0, got, held)
    if phase == 0:
        return jnp.stack([low, high], 0)
    return jnp.where(core == 0, jnp.stack([low, high], 0), jnp.stack([low, high], phase))


def halved(total, core, chip, phase):
    bit = own_bit(core, chip, phase)
    lats, left = total.shape[:2]
    by_low = total.reshape((lats, left // 2, 2) + total.shape[2:])
    by_high = total.reshape((lats, 2, left // 2) + total.shape[2:])

    def half(which):
        low = lax.dynamic_index_in_dim(by_low, which, 2, keepdims=False)
        return jnp.where(core == 0, low, lax.dynamic_index_in_dim(by_high, which, 1, keepdims=False))

    return half(bit), half(1 - bit).astype(jnp.bfloat16)


def grown(kept, got):
    return kept.astype(jnp.float32) + got.astype(jnp.float32)


def pick(value, index, count, dim):
    return lax.dynamic_index_in_dim(value, index % count, dim, keepdims=False)


def added(kept, parts):
    for part in parts:
        kept = kept + part.astype(jnp.float32)
    return kept


def scatter_rest(kept, lat):
    lats = lax.axis_size("lat")
    moved = lat_moves([pick(kept, lat + d, lats, 0).astype(jnp.bfloat16) for d in range(1, lats)])
    return added(pick(kept, lat, lats, 0), moved)


def after(value, *others):
    return lax.optimization_barrier((value,) + others)[0]


def shards(features, grad_output, qkv_weight, out_weight):
    lat_rows, lon_cols, width = features.shape
    head = width // HEADS
    lanes = PAIR * head
    groups = HEADS // PAIR // 2
    half = width // 2
    lats, chips = lax.axis_size("lat"), lax.axis_size("lon") // 2
    lat, lon = lax.axis_index("lat"), lax.axis_index("lon")
    core, chip = lon % 2, lon // 2
    rows = qkv_weight.shape[0]
    per = 3 * lanes
    cells = lat_rows * lon_cols
    block_cols = 2 * lon_cols
    half_cols = lon_cols + MARGIN

    edge = jnp.where(core == 0, features[:, :MARGIN], features[:, lon_cols - MARGIN :])
    side = routed(edge, lambda a, o: (a, beside(o)))

    by_heads = qkv_weight.reshape(rows, 3, 2, groups, lanes)
    first = [by_heads[:, i, c, 0] for c in range(2) for i in range(3)]
    first = after(jnp.concatenate(first + [out_weight], axis=1), edge)
    first_moved = lat_moves([first] * (lats - 1))

    def columns(which):
        qkv = lax.dynamic_index_in_dim(by_heads, which, 2, keepdims=False)[:, :, 1:]
        return jnp.swapaxes(qkv, 1, 2).reshape(rows, -1)

    both = [features.reshape(cells, width), grad_output.reshape(cells, width), side.reshape(-1, width)]
    both.append(columns(1 - core).reshape(-1, width))
    both = jnp.concatenate(both, axis=0)
    near = jnp.where(
        core == 0, jnp.concatenate([side, features], axis=1), jnp.concatenate([features, side], axis=1)
    )
    top, bottom = near[:RADIUS], near[lat_rows - RADIUS :]
    first = after(turned([first] + first_moved, lat), both, top, bottom)
    both = partner(both)
    above = routed(bottom, lambda a, o: (a + 1, o))
    below = routed(top, lambda a, o: (a - 1, o))
    bits = lon_bits()
    for phase in range(bits - 1):
        first = joined(first, across(first, phase), core, chip, phase)
    first_got = across(first, bits - 1)
    margin = MARGIN * lat_rows
    x_partner = both[:cells].reshape(features.shape)
    go_partner = both[cells : 2 * cells].reshape(features.shape)
    side_partner = both[2 * cells : 2 * cells + margin].reshape(side.shape)
    rest = by_core(core, columns(core), both[2 * cells + margin :].reshape(rows, -1), 0)
    far = jnp.where(
        core == 0,
        jnp.concatenate([x_partner, side_partner], axis=1),
        jnp.concatenate([side_partner, x_partner], axis=1),
    )
    rest, above, below, far = lax.optimization_barrier((rest, above, below, far))
    rest_moved = lat_moves([rest] * (lats - 1))
    above, below, first_got, *moved = lax.optimization_barrier((above, below, first_got, *rest_moved[:-1]))
    rest_moved[:-1] = moved
    caps = partner(jnp.concatenate([above, below], axis=0))
    near = jnp.concatenate([above, near, below], axis=0)
    far = jnp.concatenate([caps[:RADIUS], far, caps[RADIUS:]], axis=0)
    wide_rows = near.shape[0]

    def in_rows(grid):
        grid = grid.reshape((chips,) + grid.shape[bits:])
        return jnp.swapaxes(grid, 0, 1).reshape((lats * chips,) + grid.shape[2:])

    first = in_rows(joined(first, first_got, core, chip, bits - 1))
    x_wide = by_core(core, near, far, 1)
    wide_cols = x_wide.shape[1]
    x_wide = x_wide.reshape(-1, width)
    x_turned = lax.optimization_barrier(x_wide.T)
    go = by_core(core, grad_output, go_partner, 1)
    go = go.reshape(lat_rows // QROWS, QROWS, block_cols // QCOLS, QCOLS, width)
    go = lax.optimization_barrier(jnp.swapaxes(go, 1, 2).reshape(-1, width))

    def heads_of(which):
        qkv = lax.dynamic_slice_in_dim(first, which * per, per, 2).reshape(half, per)
        count = lats * chips // 2
        out = lax.dynamic_slice_in_dim(first, which * count, count, 0)[..., 2 * per :].reshape(-1, width)
        return qkv, out

    qkv_mine, out_mine = heads_of(core)
    qkv_other, out_other = heads_of(1 - core)
    cut = out_other.shape[0]
    swap = jnp.concatenate([jnp.concatenate([qkv_other[:cut], qkv_other[cut:]], axis=1), out_other], axis=0)
    swap = partner(swap)
    qkv_got = jnp.concatenate([swap[:cut, :per], swap[:cut, per:]], axis=0)

    def interleaved(mine, got):
        mine, got = (part.reshape(-1, rows, part.shape[1]) for part in (mine, got))
        return by_core(core, mine, got, 1).reshape(-1, mine.shape[2])

    qkv_first = interleaved(qkv_mine, qkv_got)
    out_heads = interleaved(out_mine, swap[cut:])

    bias, hot = window_columns(lat * lat_rows, lat_rows // QROWS, lat_rows * lats, lanes)
    scale = jnp.concatenate(
        [jnp.full((lanes,), LOG2E / math.sqrt(head), jnp.float32), jnp.ones((2 * lanes,), jnp.float32)]
    )

    def project(weights):
        result = dot(x_wide, weights) * jnp.tile(scale, weights.shape[1] // per)
        return result.astype(jnp.bfloat16).reshape(wide_rows, wide_cols, -1)

    def half_rows(grads, which):
        return lax.dynamic_slice_in_dim(grads, which * (grads.shape[0] // 2), grads.shape[0] // 2, 0)

    rest = turned([rest] + list(rest_moved), lat)
    for phase in range(bits - 1):
        rest = joined(rest, across(rest, phase), core, chip, phase)
    projected = project(qkv_first)
    g = dot(go, out_heads, NT).astype(jnp.bfloat16)
    projected, g, rest = lax.optimization_barrier((projected, g, rest))
    rest_got = across(rest, bits - 1)
    att_0, grads_0 = attention(projected, g, bias, hot, 0, 0, lanes)
    att_0, grads_0, rest_got = lax.optimization_barrier((att_0, grads_0, rest_got))
    rest = in_rows(joined(rest, rest_got, core, chip, bits - 1))
    qkv_rest = rest.reshape(half * 2, -1)
    grads_0 = grads_0.reshape(-1, per)
    early_0 = dot(x_turned, grads_0).astype(jnp.bfloat16)
    projected = project(qkv_rest[:, :per])
    att_1, grads_1 = attention(projected, g, bias, hot, 0, 1, lanes)
    projected = project(qkv_rest[:, per:])

    grads_1 = grads_1.reshape(-1, per)
    early = [early_0, dot(x_turned, grads_1).astype(jnp.bfloat16)]
    early = [halved(part.reshape(lats, chips, -1, per), core, chip, 0) for part in early]
    early_kept, early_moved = (jnp.concatenate(parts, axis=-1) for parts in zip(*early))

    def gx_early(which):
        first_part = dot(half_rows(grads_0, which), qkv_first, NT)
        return (first_part + dot(half_rows(grads_1, which), qkv_rest[:, :per], NT)).astype(jnp.bfloat16)

    give_early, keep_early = gx_early(1 - core), gx_early(core)
    out_rows = [dot(part, go).astype(jnp.bfloat16) for part in (att_0, att_1)]
    g, early_kept, give_early, keep_early, early_moved, *out_rows = lax.optimization_barrier(
        (g, early_kept, give_early, keep_early, early_moved, *out_rows)
    )
    early_moved = across(early_moved, 0)
    att_2, grads_2 = attention(projected, g, bias, hot, 0, 2, lanes)
    grads_2 = grads_2.reshape(-1, per)

    def gx_late(which, before):
        return dot(half_rows(grads_2, which), qkv_rest[:, per:], NT) + before.astype(jnp.float32)

    give = gx_late(1 - core, give_early).astype(jnp.bfloat16)
    give, att_2, grads_2, early_moved = lax.optimization_barrier((give, att_2, grads_2, early_moved))
    given = partner(give)
    out_rows = jnp.concatenate(out_rows + [dot(att_2, go).astype(jnp.bfloat16)], axis=0)
    swapped = partner(lax.dynamic_slice_in_dim(out_rows, (1 - core) * half, half, 1))
    early = grown(early_kept, early_moved)
    for phase in range(1, bits):
        early, early_moved = halved(early, core, chip, phase)
        early = grown(early, across(early_moved, phase))
    early = early[:, 0]
    late = dot(x_turned, grads_2).astype(jnp.bfloat16)
    out_mine = by_core(core, lax.dynamic_slice_in_dim(out_rows, core * half, half, 1), swapped, 0)
    late = jnp.concatenate([late, out_mine], axis=1).reshape(lats, chips, -1, per + half)
    given, late = lax.optimization_barrier((given, late))
    late, late_moved = halved(late, core, chip, 0)
    late_moved = across(late_moved, 0)
    gx = gx_late(core, keep_early) + given.astype(jnp.float32)
    gx = gx.reshape(wide_rows // 2, wide_cols, width)
    own = wide_rows // 2 - RADIUS
    outer = jnp.where(core == 0, gx[:RADIUS], gx[own:]).astype(jnp.bfloat16)
    gx = jnp.where(core == 0, gx[RADIUS:], gx[:own])
    inner = routed(outer, lambda a, o: (a + 1, o - 1) if o % 2 else (a - 1, o + 1))
    early_moved = lat_moves([pick(early, lat + d, lats, 0).astype(jnp.bfloat16) for d in range(1, lats)])
    late = grown(late, late_moved)
    for phase in range(1, bits):
        late, late_moved = halved(late, core, chip, phase)
        late_moved = across(late_moved, phase)
        if phase < bits - 1:
            late = grown(late, late_moved)
    gap = jnp.zeros((own - RADIUS,) + gx.shape[1:], jnp.float32)
    gx = gx + by_core(core, inner.astype(jnp.float32), gap, 0)
    other_half = lax.dynamic_slice_in_dim(gx, MARGIN + (1 - core) * lon_cols, lon_cols, 1).astype(jnp.bfloat16)
    mine_half = lax.dynamic_slice_in_dim(gx, MARGIN + core * lon_cols, lon_cols, 1)
    left, right = gx[:, :MARGIN].astype(jnp.bfloat16), gx[:, wide_cols - MARGIN :].astype(jnp.bfloat16)
    left, right, mine_half, other_half, late_moved, *early_moved = lax.optimization_barrier(
        (left, right, mine_half, other_half, late_moved, *early_moved)
    )
    early = added(pick(early, lat, lats, 0), early_moved)
    late = scatter_rest(grown(late, late_moved)[:, 0], lat)
    same = routed(jnp.where(core == 0, right, left), lambda a, o: (a, o - 2 if o % 2 else o + 2))
    cross = routed(jnp.where(core == 0, left, right), lambda a, o: (a, o + 1 if o % 2 else o - 1))
    swapped_x = partner(other_half)
    pad = jnp.zeros((own, lon_cols - MARGIN, width), jnp.float32)
    here = mine_half + by_core(core, same.astype(jnp.float32), pad, 1)
    there = swapped_x.astype(jnp.float32) + by_core(core, cross.astype(jnp.float32), pad, 1)
    grad_x = by_core(core, here.astype(jnp.bfloat16), there.astype(jnp.bfloat16), 0)

    total = jnp.concatenate([early, late], axis=1).reshape(2, rows, -1)
    keep = lax.dynamic_index_in_dim(total, core, 0, keepdims=False)
    give = lax.dynamic_index_in_dim(total, 1 - core, 0, keepdims=False).astype(jnp.bfloat16)
    got = partner(give).astype(jnp.float32)
    order = jnp.where(core == 0, jnp.stack([keep, got]), jnp.stack([got, keep]))
    grad_qkv = order[:, :, : groups * per].reshape(2, rows, groups, 3, lanes)
    grad_qkv = jnp.transpose(grad_qkv, (1, 3, 0, 2, 4)).reshape(rows, 3 * width)
    grad_out = jnp.transpose(order[:, :, groups * per :], (1, 0, 2)).reshape(rows, width)
    return grad_x, grad_qkv, grad_out


def solution(mesh):
    placed = (
        P("lat", "lon", None),
        P("lat", "lon", None),
        P(("lat", "lon"), None),
        P(("lat", "lon"), None),
    )
    return jax.shard_map(
        shards,
        mesh=mesh,
        in_specs=placed,
        out_specs=(P("lat", "lon", None), P(("lat", "lon"), None), P(("lat", "lon"), None)),
        check_vma=False,
    )
```

```python
import math

import jax
import jax.numpy as jnp
from jax import lax
from jax.experimental import pallas as pl
from jax.experimental.pallas import tpu as pltpu
from jax.sharding import PartitionSpec as P

HEADS = 12
RADIUS = 6
QROWS = 16
QCOLS = 16
MARGIN = 8
PAIR = 2
OUTSIDE = -1e30
LOG2E = math.log2(math.e)

NT = (((1,), (1,)), ((), ()))
NN = (((1,), (0,)), ((), ()))


def dot(a, b, dims=NN):
    return lax.dot_general(a, b, dims, preferred_element_type=jnp.float32)


def attention_kernel(p_ref, g_ref, bias_ref, hot_ref, att_ref, grad_ref, *scratch):
    scores, e_both, ds_both, sums = scratch[:PAIR], scratch[PAIR], scratch[PAIR + 1], scratch[PAIR + 2]
    tile_row, tile_col = pl.program_id(0), pl.program_id(1)
    key_rows, key_cols = QROWS + 2 * RADIUS, QCOLS + 2 * MARGIN
    keys, queries = key_rows * key_cols, QROWS * QCOLS
    lanes = g_ref.shape[-1]
    head = lanes // PAIR
    chunk = 64
    first_row = tile_row * QROWS
    first_col = pl.multiple_of(tile_col * QCOLS, QCOLS)
    at_rows, at_cols = pl.ds(first_row, key_rows), pl.ds(first_col, key_cols)
    q_lanes, k_lanes, v_lanes = (slice(i * lanes, (i + 1) * lanes) for i in range(3))
    heads = range(PAIR)
    rows = [slice(h * head, (h + 1) * head) for h in heads]
    cols = [slice(h * queries, (h + 1) * queries) for h in heads]

    @pl.when((tile_row == 0) & (tile_col == 0))
    def _():
        sums[...] = jnp.zeros_like(sums)

    q = p_ref[pl.ds(first_row + RADIUS, QROWS), at_cols, q_lanes].astype(jnp.float32)
    q = q[:, MARGIN : MARGIN + QCOLS].reshape(queries, lanes).astype(jnp.bfloat16)
    g_t = g_ref[...].astype(jnp.float32).T
    k = p_ref[at_rows, at_cols, k_lanes].reshape(keys, lanes)
    v = p_ref[at_rows, at_cols, v_lanes].reshape(keys, lanes)
    k_wide = jnp.concatenate([k, bias_ref[0]], axis=1)
    ones = jnp.ones((16, keys), jnp.bfloat16)
    lane = lax.broadcasted_iota(jnp.int32, (queries, lanes), 1) // head
    q_heads = [jnp.where(lane == h, q, jnp.zeros_like(q)) for h in heads]
    for h in heads:
        scores[h][...] = dot(k_wide, jnp.concatenate([q_heads[h], hot_ref[...]], axis=1), NT)
    k_t, v_t = k.T, v.T
    g_heads, att_t, dq_t, terms = [], [], [], []
    for h in heads:
        top = jnp.max(scores[h][...], axis=0, keepdims=True)
        for c in range(0, keys, chunk):
            e_both[c : c + chunk, cols[h]] = jnp.exp2(scores[h][c : c + chunk] - top).astype(jnp.bfloat16)
        out = dot(jnp.concatenate([v_t[rows[h]], ones], axis=0), e_both[:, cols[h]])
        inverse = 1.0 / out[head : head + 1]
        attended = (out[:head] * inverse).astype(jnp.bfloat16).astype(jnp.float32)
        att_t.append(attended)
        g_one = g_t[rows[h]] * inverse
        terms.append(jnp.sum(g_one * attended, axis=0, keepdims=True))
        empty = jnp.zeros_like(g_one)
        g_one = jnp.concatenate([empty] * h + [g_one] + [empty] * (PAIR - 1 - h), axis=0).astype(jnp.bfloat16)
        g_heads.append(g_one)
    for h in heads:
        scores[h][...] = dot(v, g_heads[h])
    for h in heads:
        for c in range(0, keys, chunk):
            ds_both[c : c + chunk, cols[h]] = (
                e_both[c : c + chunk, cols[h]].astype(jnp.float32) * (scores[h][c : c + chunk] - terms[h])
            ).astype(jnp.bfloat16)
        dq_t.append(dot(k_t[rows[h]], ds_both[:, cols[h]]))
    tile = (key_rows, key_cols, lanes)
    sums[at_rows, at_cols, v_lanes] += dot(e_both[...], jnp.concatenate(g_heads, axis=1), NT).reshape(tile)
    sums[at_rows, at_cols, k_lanes] += dot(ds_both[...], jnp.concatenate(q_heads, axis=0)).reshape(tile)
    att_ref[...] = jnp.concatenate(att_t, axis=0).astype(jnp.bfloat16)
    dq = jnp.concatenate(dq_t, axis=0).T * (1.0 / math.sqrt(head))
    sums[pl.ds(first_row + RADIUS, QROWS), pl.ds(pl.multiple_of(first_col + MARGIN, 8), QCOLS), q_lanes] = dq.reshape(
        QROWS, QCOLS, lanes
    )

    @pl.when((tile_row == pl.num_programs(0) - 1) & (tile_col == pl.num_programs(1) - 1))
    def _():
        grad_ref[:, :, q_lanes] = sums[:, :, q_lanes].astype(jnp.bfloat16)
        grad_ref[:, :, k_lanes] = (sums[:, :, k_lanes] * (1.0 / LOG2E)).astype(jnp.bfloat16)
        grad_ref[:, :, v_lanes] = sums[:, :, v_lanes].astype(jnp.bfloat16)


def attention(projected, g, bias, hot, place, g_place, lanes):
    wide = projected.shape[:2] + (3 * lanes,)
    queries, keys = QROWS * QCOLS, (QROWS + 2 * RADIUS) * (QCOLS + 2 * MARGIN)
    tiles = ((wide[0] - 2 * RADIUS) // QROWS, (wide[1] - 2 * MARGIN) // QCOLS)
    count = tiles[0] * tiles[1]
    return pl.pallas_call(
        attention_kernel,
        grid=tiles,
        in_specs=[
            pl.BlockSpec(wide, lambda r, c: (0, 0, place)),
            pl.BlockSpec((queries, lanes), lambda r, c: (r * tiles[1] + c, g_place)),
            pl.BlockSpec((1, keys, lanes), lambda r, c: (r, 0, 0)),
            pl.BlockSpec((queries, lanes), lambda r, c: (0, 0)),
        ],
        out_specs=[
            pl.BlockSpec((lanes, queries), lambda r, c: (0, r * tiles[1] + c)),
            pl.BlockSpec(wide, lambda r, c: (0, 0, 0)),
        ],
        out_shape=[
            jax.ShapeDtypeStruct((lanes, count * queries), jnp.bfloat16),
            jax.ShapeDtypeStruct(wide, jnp.bfloat16),
        ],
        scratch_shapes=[pltpu.VMEM((keys, queries), jnp.float32)] * PAIR
        + [pltpu.VMEM((keys, PAIR * queries), jnp.bfloat16)] * 2
        + [pltpu.VMEM(wide, jnp.float32)],
        compiler_params=pltpu.CompilerParams(
            dimension_semantics=("arbitrary", "arbitrary"), vmem_limit_bytes=48 * 1024 * 1024
        ),
        cost_estimate=pl.CostEstimate(
            flops=2 * 12 * 256 * keys * queries * PAIR * count,
            bytes_accessed=12 * count * queries * lanes * 2,
            transcendentals=keys * queries * PAIR * count,
        ),
    )(projected, g, bias, hot)


def window_columns(lat_first, tile_rows, total_rows, lanes):
    key_rows, key_cols = QROWS + 2 * RADIUS, QCOLS + 2 * MARGIN
    base = lat_first + QROWS * jnp.arange(tile_rows, dtype=jnp.int32)[:, None, None]
    q_row = base + jnp.arange(QROWS, dtype=jnp.int32)[None, None, :]
    k_row = base - RADIUS + jnp.arange(key_rows, dtype=jnp.int32)[None, :, None]
    start = jnp.clip(q_row - RADIUS, 0, total_rows - 2 * RADIUS - 1)
    row_in = (k_row >= start) & (k_row <= start + 2 * RADIUS)
    q_col = jnp.arange(QCOLS, dtype=jnp.int32)[None, :]
    k_col = jnp.arange(key_cols, dtype=jnp.int32)[:, None] - MARGIN
    col_in = (k_col >= q_col - RADIUS) & (k_col <= q_col + RADIUS)
    shape = (tile_rows, key_rows, key_cols)
    row_part = jnp.broadcast_to(jnp.where(row_in, 0.0, OUTSIDE)[:, :, None, :], shape + (QROWS,))
    col_part = jnp.broadcast_to(jnp.where(col_in, 0.0, OUTSIDE)[None, None], shape + (QCOLS,))
    rest = jnp.zeros(shape + (lanes - QROWS - QCOLS,), jnp.float32)
    columns = jnp.concatenate([row_part, col_part, rest], axis=-1).astype(jnp.bfloat16)
    columns = columns.reshape(tile_rows, key_rows * key_cols, lanes)
    r, c = jnp.arange(QROWS * QCOLS) // QCOLS, jnp.arange(QROWS * QCOLS) % QCOLS
    lane = jnp.arange(lanes)[None, :]
    hot = ((lane == r[:, None]) | (lane == QROWS + c[:, None])).astype(jnp.bfloat16)
    return columns, hot


def routed(value, route):
    lats, lons = lax.axis_size("lat"), lax.axis_size("lon")
    pairs = []
    for a in range(lats):
        for o in range(lons):
            to_lat, to_lon = route(a, o)
            if 0 <= to_lat < lats:
                pairs.append((a * lons + o, to_lat * lons + to_lon % lons))
    return lax.ppermute(value, ("lat", "lon"), pairs)


def partner(value):
    return routed(value, lambda a, o: (a, o ^ 1))


def beside(o):
    return o + 1 if o % 2 else o - 1


def by_core(core, mine, other, axis):
    return jnp.where(
        core == 0, jnp.concatenate([mine, other], axis=axis), jnp.concatenate([other, mine], axis=axis)
    )


def turned(parts, by):
    count = len(parts)
    whole = jnp.zeros((count,) + parts[0].shape, parts[0].dtype)
    for d, part in enumerate(parts):
        whole = lax.dynamic_update_index_in_dim(whole, part, (by - d) % count, 0)
    return whole


def lat_moves(blocks):
    lats = lax.axis_size("lat")
    return [routed(part, lambda a, o, d=d + 1: ((a + d) % lats, o)) for d, part in enumerate(blocks)]


def lon_bits():
    return (lax.axis_size("lon") // 2 - 1).bit_length()


def across(value, phase):
    last = lon_bits() - 1
    return routed(value, lambda a, o: (a, o ^ (2 << (last - phase if o % 2 else phase))))


def own_bit(core, chip, phase):
    return (chip >> jnp.where(core == 0, phase, lon_bits() - 1 - phase)) & 1


def joined(held, got, core, chip, phase):
    bit = own_bit(core, chip, phase)
    low, high = jnp.where(bit == 0, held, got), jnp.where(bit == 0, got, held)
    if phase == 0:
        return jnp.stack([low, high], 0)
    return jnp.where(core == 0, jnp.stack([low, high], 0), jnp.stack([low, high], phase))


def halved(total, core, chip, phase):
    bit = own_bit(core, chip, phase)
    lats, left = total.shape[:2]
    by_low = total.reshape((lats, left // 2, 2) + total.shape[2:])
    by_high = total.reshape((lats, 2, left // 2) + total.shape[2:])

    def half(which):
        low = lax.dynamic_index_in_dim(by_low, which, 2, keepdims=False)
        return jnp.where(core == 0, low, lax.dynamic_index_in_dim(by_high, which, 1, keepdims=False))

    return half(bit), half(1 - bit).astype(jnp.bfloat16)


def grown(kept, got):
    return kept.astype(jnp.float32) + got.astype(jnp.float32)


def pick(value, index, count, dim):
    return lax.dynamic_index_in_dim(value, index % count, dim, keepdims=False)


def added(kept, parts):
    for part in parts:
        kept = kept + part.astype(jnp.float32)
    return kept


def scatter_rest(kept, lat):
    lats = lax.axis_size("lat")
    moved = lat_moves([pick(kept, lat + d, lats, 0).astype(jnp.bfloat16) for d in range(1, lats)])
    return added(pick(kept, lat, lats, 0), moved)


def after(value, *others):
    return lax.optimization_barrier((value,) + others)[0]


def shards(features, grad_output, qkv_weight, out_weight):
    lat_rows, lon_cols, width = features.shape
    head = width // HEADS
    lanes = PAIR * head
    groups = HEADS // PAIR // 2
    half = width // 2
    lats, chips = lax.axis_size("lat"), lax.axis_size("lon") // 2
    lat, lon = lax.axis_index("lat"), lax.axis_index("lon")
    core, chip = lon % 2, lon // 2
    rows = qkv_weight.shape[0]
    per = 3 * lanes
    cells = lat_rows * lon_cols
    block_cols = 2 * lon_cols
    half_cols = lon_cols + MARGIN

    edge = jnp.where(core == 0, features[:, :MARGIN], features[:, lon_cols - MARGIN :])
    side = routed(edge, lambda a, o: (a, beside(o)))

    by_heads = qkv_weight.reshape(rows, 3, 2, groups, lanes)
    first = [by_heads[:, i, c, 0] for c in range(2) for i in range(3)]
    first = after(jnp.concatenate(first + [out_weight], axis=1), edge)
    first_moved = lat_moves([first] * (lats - 1))

    def columns(which):
        qkv = lax.dynamic_index_in_dim(by_heads, which, 2, keepdims=False)[:, :, 1:]
        return jnp.swapaxes(qkv, 1, 2).reshape(rows, -1)

    both = [features.reshape(cells, width), grad_output.reshape(cells, width), side.reshape(-1, width)]
    both.append(columns(1 - core).reshape(-1, width))
    both = jnp.concatenate(both, axis=0)
    near = jnp.where(
        core == 0, jnp.concatenate([side, features], axis=1), jnp.concatenate([features, side], axis=1)
    )
    top, bottom = near[:RADIUS], near[lat_rows - RADIUS :]
    first = after(turned([first] + first_moved, lat), both, top, bottom)
    both = partner(both)
    above = routed(bottom, lambda a, o: (a + 1, o))
    below = routed(top, lambda a, o: (a - 1, o))
    bits = lon_bits()
    for phase in range(bits - 1):
        first = joined(first, across(first, phase), core, chip, phase)
    first_got = across(first, bits - 1)
    margin = MARGIN * lat_rows
    x_partner = both[:cells].reshape(features.shape)
    go_partner = both[cells : 2 * cells].reshape(features.shape)
    side_partner = both[2 * cells : 2 * cells + margin].reshape(side.shape)
    rest = by_core(core, columns(core), both[2 * cells + margin :].reshape(rows, -1), 0)
    far = jnp.where(
        core == 0,
        jnp.concatenate([x_partner, side_partner], axis=1),
        jnp.concatenate([side_partner, x_partner], axis=1),
    )
    rest, far = lax.optimization_barrier((rest, far))
    rest_moved = lat_moves([rest] * (lats - 1))
    above, below, first_got, *moved = lax.optimization_barrier((above, below, first_got, *rest_moved[:-1]))
    rest_moved[:-1] = moved
    caps = partner(jnp.concatenate([above, below], axis=0))
    near = jnp.concatenate([above, near, below], axis=0)
    far = jnp.concatenate([caps[:RADIUS], far, caps[RADIUS:]], axis=0)
    wide_rows = near.shape[0]

    def in_rows(grid):
        grid = grid.reshape((chips,) + grid.shape[bits:])
        return jnp.swapaxes(grid, 0, 1).reshape((lats * chips,) + grid.shape[2:])

    first = in_rows(joined(first, first_got, core, chip, bits - 1))
    x_wide = by_core(core, near, far, 1)
    wide_cols = x_wide.shape[1]
    x_wide = x_wide.reshape(-1, width)
    x_turned = lax.optimization_barrier(x_wide.T)
    go = by_core(core, grad_output, go_partner, 1)
    go = go.reshape(lat_rows // QROWS, QROWS, block_cols // QCOLS, QCOLS, width)
    go = lax.optimization_barrier(jnp.swapaxes(go, 1, 2).reshape(-1, width))

    def heads_of(which):
        qkv = lax.dynamic_slice_in_dim(first, which * per, per, 2).reshape(half, per)
        count = lats * chips // 2
        out = lax.dynamic_slice_in_dim(first, which * count, count, 0)[..., 2 * per :].reshape(-1, width)
        return qkv, out

    qkv_mine, out_mine = heads_of(core)
    qkv_other, out_other = heads_of(1 - core)
    cut = out_other.shape[0]
    swap = jnp.concatenate([jnp.concatenate([qkv_other[:cut], qkv_other[cut:]], axis=1), out_other], axis=0)
    swap = partner(swap)
    qkv_got = jnp.concatenate([swap[:cut, :per], swap[:cut, per:]], axis=0)

    def interleaved(mine, got):
        mine, got = (part.reshape(-1, rows, part.shape[1]) for part in (mine, got))
        return by_core(core, mine, got, 1).reshape(-1, mine.shape[2])

    qkv_first = interleaved(qkv_mine, qkv_got)
    out_heads = interleaved(out_mine, swap[cut:])

    bias, hot = window_columns(lat * lat_rows, lat_rows // QROWS, lat_rows * lats, lanes)
    scale = jnp.concatenate(
        [jnp.full((lanes,), LOG2E / math.sqrt(head), jnp.float32), jnp.ones((2 * lanes,), jnp.float32)]
    )

    def project(weights):
        result = dot(x_wide, weights) * jnp.tile(scale, weights.shape[1] // per)
        return result.astype(jnp.bfloat16).reshape(wide_rows, wide_cols, -1)

    def half_rows(grads, which):
        return lax.dynamic_slice_in_dim(grads, which * (grads.shape[0] // 2), grads.shape[0] // 2, 0)

    rest = turned([rest] + list(rest_moved), lat)
    for phase in range(bits - 1):
        rest = joined(rest, across(rest, phase), core, chip, phase)
    projected = project(qkv_first)
    g = dot(go, out_heads, NT).astype(jnp.bfloat16)
    projected, g, rest = lax.optimization_barrier((projected, g, rest))
    rest_got = across(rest, bits - 1)
    att_0, grads_0 = attention(projected, g, bias, hot, 0, 0, lanes)
    att_0, grads_0, rest_got = lax.optimization_barrier((att_0, grads_0, rest_got))
    rest = in_rows(joined(rest, rest_got, core, chip, bits - 1))
    qkv_rest = rest.reshape(half * 2, -1)
    grads_0 = grads_0.reshape(-1, per)
    early_0 = dot(x_turned, grads_0).astype(jnp.bfloat16)
    projected = project(qkv_rest[:, :per])
    att_1, grads_1 = attention(projected, g, bias, hot, 0, 1, lanes)
    projected = project(qkv_rest[:, per:])

    grads_1 = grads_1.reshape(-1, per)
    early = [early_0, dot(x_turned, grads_1).astype(jnp.bfloat16)]
    early = [halved(part.reshape(lats, chips, -1, per), core, chip, 0) for part in early]
    early_kept, early_moved = (jnp.concatenate(parts, axis=-1) for parts in zip(*early))
    grads_0, grads_1, early_kept, early_moved = lax.optimization_barrier((grads_0, grads_1, early_kept, early_moved))
    early_moved = across(early_moved, 0)

    def gx_early(which):
        first_part = dot(half_rows(grads_0, which), qkv_first, NT)
        return (first_part + dot(half_rows(grads_1, which), qkv_rest[:, :per], NT)).astype(jnp.bfloat16)

    give_early, keep_early = gx_early(1 - core), gx_early(core)
    out_rows = [dot(part, go).astype(jnp.bfloat16) for part in (att_0, att_1)]
    for phase in range(1, bits):
        give_early, keep_early, early_moved, *out_rows = lax.optimization_barrier(
            (give_early, keep_early, early_moved, *out_rows)
        )
        early_kept, early_moved = halved(grown(early_kept, early_moved), core, chip, phase)
        if phase == bits - 1:
            g, early_kept, early_moved = lax.optimization_barrier((g, early_kept, early_moved))
        early_moved = across(early_moved, phase)
    att_2, grads_2 = attention(projected, g, bias, hot, 0, 2, lanes)
    grads_2 = grads_2.reshape(-1, per)

    def gx_late(which, before):
        return dot(half_rows(grads_2, which), qkv_rest[:, per:], NT) + before.astype(jnp.float32)

    att_2, grads_2, early_moved = lax.optimization_barrier((att_2, grads_2, early_moved))
    give = gx_late(1 - core, give_early).astype(jnp.bfloat16)
    given = partner(give)
    out_rows = jnp.concatenate(out_rows + [dot(att_2, go).astype(jnp.bfloat16)], axis=0)
    swapped = partner(lax.dynamic_slice_in_dim(out_rows, (1 - core) * half, half, 1))
    early = grown(early_kept, early_moved)[:, 0]
    early_moved = lat_moves([pick(early, lat + d, lats, 0).astype(jnp.bfloat16) for d in range(1, lats)])
    late = dot(x_turned, grads_2).astype(jnp.bfloat16)
    out_mine = by_core(core, lax.dynamic_slice_in_dim(out_rows, core * half, half, 1), swapped, 0)
    late = jnp.concatenate([late, out_mine], axis=1).reshape(lats, chips, -1, per + half)
    given, late, early = lax.optimization_barrier((given, late, early))
    late, late_moved = halved(late, core, chip, 0)
    late_moved = across(late_moved, 0)
    gx = gx_late(core, keep_early) + given.astype(jnp.float32)
    gx = gx.reshape(wide_rows // 2, wide_cols, width)
    own = wide_rows // 2 - RADIUS
    outer = jnp.where(core == 0, gx[:RADIUS], gx[own:]).astype(jnp.bfloat16)
    gx = jnp.where(core == 0, gx[RADIUS:], gx[:own])
    inner = routed(outer, lambda a, o: (a + 1, o - 1) if o % 2 else (a - 1, o + 1))
    late_moved, *early_moved = lax.optimization_barrier((late_moved, *early_moved))
    late = grown(late, late_moved)
    for phase in range(1, bits):
        late, late_moved = halved(late, core, chip, phase)
        late_moved = across(late_moved, phase)
        if phase < bits - 1:
            late = grown(late, late_moved)
    gap = jnp.zeros((own - RADIUS,) + gx.shape[1:], jnp.float32)
    gx = gx + by_core(core, inner.astype(jnp.float32), gap, 0)
    other_half = lax.dynamic_slice_in_dim(gx, MARGIN + (1 - core) * lon_cols, lon_cols, 1).astype(jnp.bfloat16)
    mine_half = lax.dynamic_slice_in_dim(gx, MARGIN + core * lon_cols, lon_cols, 1)
    left, right = gx[:, :MARGIN].astype(jnp.bfloat16), gx[:, wide_cols - MARGIN :].astype(jnp.bfloat16)
    left, right, mine_half, other_half, late_moved = lax.optimization_barrier(
        (left, right, mine_half, other_half, late_moved)
    )
    early = added(pick(early, lat, lats, 0), early_moved)
    late = scatter_rest(grown(late, late_moved)[:, 0], lat)
    same = routed(jnp.where(core == 0, right, left), lambda a, o: (a, o - 2 if o % 2 else o + 2))
    cross = routed(jnp.where(core == 0, left, right), lambda a, o: (a, o + 1 if o % 2 else o - 1))
    swapped_x = partner(other_half)
    pad = jnp.zeros((own, lon_cols - MARGIN, width), jnp.float32)
    here = mine_half + by_core(core, same.astype(jnp.float32), pad, 1)
    there = swapped_x.astype(jnp.float32) + by_core(core, cross.astype(jnp.float32), pad, 1)
    grad_x = by_core(core, here.astype(jnp.bfloat16), there.astype(jnp.bfloat16), 0)

    total = jnp.concatenate([early, late], axis=1).reshape(2, rows, -1)
    keep = lax.dynamic_index_in_dim(total, core, 0, keepdims=False)
    give = lax.dynamic_index_in_dim(total, 1 - core, 0, keepdims=False).astype(jnp.bfloat16)
    got = partner(give).astype(jnp.float32)
    order = jnp.where(core == 0, jnp.stack([keep, got]), jnp.stack([got, keep]))
    grad_qkv = order[:, :, : groups * per].reshape(2, rows, groups, 3, lanes)
    grad_qkv = jnp.transpose(grad_qkv, (1, 3, 0, 2, 4)).reshape(rows, 3 * width)
    grad_out = jnp.transpose(order[:, :, groups * per :], (1, 0, 2)).reshape(rows, width)
    return grad_x, grad_qkv, grad_out


def solution(mesh):
    placed = (
        P("lat", "lon", None),
        P("lat", "lon", None),
        P(("lat", "lon"), None),
        P(("lat", "lon"), None),
    )
    return jax.shard_map(
        shards,
        mesh=mesh,
        in_specs=placed,
        out_specs=(P("lat", "lon", None), P(("lat", "lon"), None), P(("lat", "lon"), None)),
        check_vma=False,
    )
```

```python
import math

import jax
import jax.numpy as jnp
from jax import lax
from jax.experimental import pallas as pl
from jax.experimental.pallas import tpu as pltpu
from jax.sharding import PartitionSpec as P

HEADS = 12
RADIUS = 6
QROWS = 16
QCOLS = 16
MARGIN = 8
PAIR = 2
OUTSIDE = -1e30
LOG2E = math.log2(math.e)

NT = (((1,), (1,)), ((), ()))
NN = (((1,), (0,)), ((), ()))


def dot(a, b, dims=NN):
    return lax.dot_general(a, b, dims, preferred_element_type=jnp.float32)


def attention_kernel(p_ref, g_ref, bias_ref, hot_ref, att_ref, grad_ref, *scratch):
    scores, e_both, ds_both, sums = scratch[:PAIR], scratch[PAIR], scratch[PAIR + 1], scratch[PAIR + 2]
    tile_row, tile_col = pl.program_id(0), pl.program_id(1)
    key_rows, key_cols = QROWS + 2 * RADIUS, QCOLS + 2 * MARGIN
    keys, queries = key_rows * key_cols, QROWS * QCOLS
    lanes = g_ref.shape[-1]
    head = lanes // PAIR
    chunk = 64
    first_row = tile_row * QROWS
    first_col = pl.multiple_of(tile_col * QCOLS, QCOLS)
    at_rows, at_cols = pl.ds(first_row, key_rows), pl.ds(first_col, key_cols)
    q_lanes, k_lanes, v_lanes = (slice(i * lanes, (i + 1) * lanes) for i in range(3))
    heads = range(PAIR)
    rows = [slice(h * head, (h + 1) * head) for h in heads]
    cols = [slice(h * queries, (h + 1) * queries) for h in heads]

    @pl.when((tile_row == 0) & (tile_col == 0))
    def _():
        sums[...] = jnp.zeros_like(sums)

    q = p_ref[pl.ds(first_row + RADIUS, QROWS), at_cols, q_lanes].astype(jnp.float32)
    q = q[:, MARGIN : MARGIN + QCOLS].reshape(queries, lanes).astype(jnp.bfloat16)
    g_t = g_ref[...].astype(jnp.float32).T
    k = p_ref[at_rows, at_cols, k_lanes].reshape(keys, lanes)
    v = p_ref[at_rows, at_cols, v_lanes].reshape(keys, lanes)
    k_wide = jnp.concatenate([k, bias_ref[0]], axis=1)
    ones = jnp.ones((16, keys), jnp.bfloat16)
    lane = lax.broadcasted_iota(jnp.int32, (queries, lanes), 1) // head
    q_heads = [jnp.where(lane == h, q, jnp.zeros_like(q)) for h in heads]
    for h in heads:
        scores[h][...] = dot(k_wide, jnp.concatenate([q_heads[h], hot_ref[...]], axis=1), NT)
    k_t, v_t = k.T, v.T
    g_heads, att_t, dq_t, terms = [], [], [], []
    for h in heads:
        top = jnp.max(scores[h][...], axis=0, keepdims=True)
        for c in range(0, keys, chunk):
            e_both[c : c + chunk, cols[h]] = jnp.exp2(scores[h][c : c + chunk] - top).astype(jnp.bfloat16)
        out = dot(jnp.concatenate([v_t[rows[h]], ones], axis=0), e_both[:, cols[h]])
        inverse = 1.0 / out[head : head + 1]
        attended = (out[:head] * inverse).astype(jnp.bfloat16).astype(jnp.float32)
        att_t.append(attended)
        g_one = g_t[rows[h]] * inverse
        terms.append(jnp.sum(g_one * attended, axis=0, keepdims=True))
        empty = jnp.zeros_like(g_one)
        g_one = jnp.concatenate([empty] * h + [g_one] + [empty] * (PAIR - 1 - h), axis=0).astype(jnp.bfloat16)
        g_heads.append(g_one)
    for h in heads:
        scores[h][...] = dot(v, g_heads[h])
    for h in heads:
        for c in range(0, keys, chunk):
            ds_both[c : c + chunk, cols[h]] = (
                e_both[c : c + chunk, cols[h]].astype(jnp.float32) * (scores[h][c : c + chunk] - terms[h])
            ).astype(jnp.bfloat16)
        dq_t.append(dot(k_t[rows[h]], ds_both[:, cols[h]]))
    tile = (key_rows, key_cols, lanes)
    sums[at_rows, at_cols, v_lanes] += dot(e_both[...], jnp.concatenate(g_heads, axis=1), NT).reshape(tile)
    sums[at_rows, at_cols, k_lanes] += dot(ds_both[...], jnp.concatenate(q_heads, axis=0)).reshape(tile)
    att_ref[...] = jnp.concatenate(att_t, axis=0).astype(jnp.bfloat16)
    dq = jnp.concatenate(dq_t, axis=0).T * (1.0 / math.sqrt(head))
    sums[pl.ds(first_row + RADIUS, QROWS), pl.ds(pl.multiple_of(first_col + MARGIN, 8), QCOLS), q_lanes] = dq.reshape(
        QROWS, QCOLS, lanes
    )

    @pl.when((tile_row == pl.num_programs(0) - 1) & (tile_col == pl.num_programs(1) - 1))
    def _():
        grad_ref[:, :, q_lanes] = sums[:, :, q_lanes].astype(jnp.bfloat16)
        grad_ref[:, :, k_lanes] = (sums[:, :, k_lanes] * (1.0 / LOG2E)).astype(jnp.bfloat16)
        grad_ref[:, :, v_lanes] = sums[:, :, v_lanes].astype(jnp.bfloat16)


def attention(projected, g, bias, hot, place, g_place, lanes):
    wide = projected.shape[:2] + (3 * lanes,)
    queries, keys = QROWS * QCOLS, (QROWS + 2 * RADIUS) * (QCOLS + 2 * MARGIN)
    tiles = ((wide[0] - 2 * RADIUS) // QROWS, (wide[1] - 2 * MARGIN) // QCOLS)
    count = tiles[0] * tiles[1]
    return pl.pallas_call(
        attention_kernel,
        grid=tiles,
        in_specs=[
            pl.BlockSpec(wide, lambda r, c: (0, 0, place)),
            pl.BlockSpec((queries, lanes), lambda r, c: (r * tiles[1] + c, g_place)),
            pl.BlockSpec((1, keys, lanes), lambda r, c: (r, 0, 0)),
            pl.BlockSpec((queries, lanes), lambda r, c: (0, 0)),
        ],
        out_specs=[
            pl.BlockSpec((lanes, queries), lambda r, c: (0, r * tiles[1] + c)),
            pl.BlockSpec(wide, lambda r, c: (0, 0, 0)),
        ],
        out_shape=[
            jax.ShapeDtypeStruct((lanes, count * queries), jnp.bfloat16),
            jax.ShapeDtypeStruct(wide, jnp.bfloat16),
        ],
        scratch_shapes=[pltpu.VMEM((keys, queries), jnp.float32)] * PAIR
        + [pltpu.VMEM((keys, PAIR * queries), jnp.bfloat16)] * 2
        + [pltpu.VMEM(wide, jnp.float32)],
        compiler_params=pltpu.CompilerParams(
            dimension_semantics=("arbitrary", "arbitrary"), vmem_limit_bytes=48 * 1024 * 1024
        ),
        cost_estimate=pl.CostEstimate(
            flops=2 * 12 * 256 * keys * queries * PAIR * count,
            bytes_accessed=12 * count * queries * lanes * 2,
            transcendentals=keys * queries * PAIR * count,
        ),
    )(projected, g, bias, hot)


def window_columns(lat_first, tile_rows, total_rows, lanes):
    key_rows, key_cols = QROWS + 2 * RADIUS, QCOLS + 2 * MARGIN
    base = lat_first + QROWS * jnp.arange(tile_rows, dtype=jnp.int32)[:, None, None]
    q_row = base + jnp.arange(QROWS, dtype=jnp.int32)[None, None, :]
    k_row = base - RADIUS + jnp.arange(key_rows, dtype=jnp.int32)[None, :, None]
    start = jnp.clip(q_row - RADIUS, 0, total_rows - 2 * RADIUS - 1)
    row_in = (k_row >= start) & (k_row <= start + 2 * RADIUS)
    q_col = jnp.arange(QCOLS, dtype=jnp.int32)[None, :]
    k_col = jnp.arange(key_cols, dtype=jnp.int32)[:, None] - MARGIN
    col_in = (k_col >= q_col - RADIUS) & (k_col <= q_col + RADIUS)
    shape = (tile_rows, key_rows, key_cols)
    row_part = jnp.broadcast_to(jnp.where(row_in, 0.0, OUTSIDE)[:, :, None, :], shape + (QROWS,))
    col_part = jnp.broadcast_to(jnp.where(col_in, 0.0, OUTSIDE)[None, None], shape + (QCOLS,))
    rest = jnp.zeros(shape + (lanes - QROWS - QCOLS,), jnp.float32)
    columns = jnp.concatenate([row_part, col_part, rest], axis=-1).astype(jnp.bfloat16)
    columns = columns.reshape(tile_rows, key_rows * key_cols, lanes)
    r, c = jnp.arange(QROWS * QCOLS) // QCOLS, jnp.arange(QROWS * QCOLS) % QCOLS
    lane = jnp.arange(lanes)[None, :]
    hot = ((lane == r[:, None]) | (lane == QROWS + c[:, None])).astype(jnp.bfloat16)
    return columns, hot


def routed(value, route):
    lats, lons = lax.axis_size("lat"), lax.axis_size("lon")
    pairs = []
    for a in range(lats):
        for o in range(lons):
            to_lat, to_lon = route(a, o)
            if 0 <= to_lat < lats:
                pairs.append((a * lons + o, to_lat * lons + to_lon % lons))
    return lax.ppermute(value, ("lat", "lon"), pairs)


def partner(value):
    return routed(value, lambda a, o: (a, o ^ 1))


def beside(o):
    return o + 1 if o % 2 else o - 1


def by_core(core, mine, other, axis):
    return jnp.where(
        core == 0, jnp.concatenate([mine, other], axis=axis), jnp.concatenate([other, mine], axis=axis)
    )


def turned(parts, by):
    count = len(parts)
    whole = jnp.zeros((count,) + parts[0].shape, parts[0].dtype)
    for d, part in enumerate(parts):
        whole = lax.dynamic_update_index_in_dim(whole, part, (by - d) % count, 0)
    return whole


def lat_moves(blocks):
    lats = lax.axis_size("lat")
    return [routed(part, lambda a, o, d=d + 1: ((a + d) % lats, o)) for d, part in enumerate(blocks)]


def lon_bits():
    return (lax.axis_size("lon") // 2 - 1).bit_length()


def across(value, phase):
    last = lon_bits() - 1
    return routed(value, lambda a, o: (a, o ^ (2 << (last - phase if o % 2 else phase))))


def own_bit(core, chip, phase):
    return (chip >> jnp.where(core == 0, phase, lon_bits() - 1 - phase)) & 1


def joined(held, got, core, chip, phase):
    bit = own_bit(core, chip, phase)
    low, high = jnp.where(bit == 0, held, got), jnp.where(bit == 0, got, held)
    if phase == 0:
        return jnp.stack([low, high], 0)
    return jnp.where(core == 0, jnp.stack([low, high], 0), jnp.stack([low, high], phase))


def halved(total, core, chip, phase):
    bit = own_bit(core, chip, phase)
    lats, left = total.shape[:2]
    by_low = total.reshape((lats, left // 2, 2) + total.shape[2:])
    by_high = total.reshape((lats, 2, left // 2) + total.shape[2:])

    def half(which):
        low = lax.dynamic_index_in_dim(by_low, which, 2, keepdims=False)
        return jnp.where(core == 0, low, lax.dynamic_index_in_dim(by_high, which, 1, keepdims=False))

    return half(bit), half(1 - bit).astype(jnp.bfloat16)


def grown(kept, got):
    return kept.astype(jnp.float32) + got.astype(jnp.float32)


def pick(value, index, count, dim):
    return lax.dynamic_index_in_dim(value, index % count, dim, keepdims=False)


def added(kept, parts):
    for part in parts:
        kept = kept + part.astype(jnp.float32)
    return kept


def scatter_rest(kept, lat):
    lats = lax.axis_size("lat")
    moved = lat_moves([pick(kept, lat + d, lats, 0).astype(jnp.bfloat16) for d in range(1, lats)])
    return added(pick(kept, lat, lats, 0), moved)


def after(value, *others):
    return lax.optimization_barrier((value,) + others)[0]


def shards(features, grad_output, qkv_weight, out_weight):
    lat_rows, lon_cols, width = features.shape
    head = width // HEADS
    lanes = PAIR * head
    groups = HEADS // PAIR // 2
    half = width // 2
    lats, chips = lax.axis_size("lat"), lax.axis_size("lon") // 2
    lat, lon = lax.axis_index("lat"), lax.axis_index("lon")
    core, chip = lon % 2, lon // 2
    rows = qkv_weight.shape[0]
    per = 3 * lanes
    cells = lat_rows * lon_cols
    block_cols = 2 * lon_cols
    half_cols = lon_cols + MARGIN

    edge = jnp.where(core == 0, features[:, :MARGIN], features[:, lon_cols - MARGIN :])
    side = routed(edge, lambda a, o: (a, beside(o)))

    by_heads = qkv_weight.reshape(rows, 3, 2, groups, lanes)
    first = [by_heads[:, i, c, 0] for c in range(2) for i in range(3)]
    first = after(jnp.concatenate(first + [out_weight], axis=1), edge)
    first_moved = lat_moves([first] * (lats - 1))

    def columns(which):
        qkv = lax.dynamic_index_in_dim(by_heads, which, 2, keepdims=False)[:, :, 1:]
        return jnp.swapaxes(qkv, 1, 2).reshape(rows, -1)

    rest = by_core(core, columns(core), partner(columns(1 - core)), 0)
    both = [features.reshape(cells, width), grad_output.reshape(cells, width), side.reshape(-1, width)]
    both = jnp.concatenate(both, axis=0)
    near = jnp.where(
        core == 0, jnp.concatenate([side, features], axis=1), jnp.concatenate([features, side], axis=1)
    )
    top, bottom = near[:RADIUS], near[lat_rows - RADIUS :]
    first, both, top, bottom, rest = lax.optimization_barrier(
        (turned([first] + first_moved, lat), both, top, bottom, rest)
    )
    rest_moved = lat_moves([rest] * (lats - 1))
    both = partner(both)
    above = routed(bottom, lambda a, o: (a + 1, o))
    below = routed(top, lambda a, o: (a - 1, o))
    bits = lon_bits()
    for phase in range(bits - 1):
        first = joined(first, across(first, phase), core, chip, phase)
    first_got = across(first, bits - 1)
    x_partner = both[:cells].reshape(features.shape)
    go_partner = both[cells : 2 * cells].reshape(features.shape)
    side_partner = both[2 * cells :].reshape(side.shape)
    far = jnp.where(
        core == 0,
        jnp.concatenate([x_partner, side_partner], axis=1),
        jnp.concatenate([side_partner, x_partner], axis=1),
    )
    above, below, far, first_got, *moved = lax.optimization_barrier((above, below, far, first_got, *rest_moved[:-1]))
    rest_moved[:-1] = moved
    caps = partner(jnp.concatenate([above, below], axis=0))
    near = jnp.concatenate([above, near, below], axis=0)
    far = jnp.concatenate([caps[:RADIUS], far, caps[RADIUS:]], axis=0)
    wide_rows = near.shape[0]

    def in_rows(grid):
        grid = grid.reshape((chips,) + grid.shape[bits:])
        return jnp.swapaxes(grid, 0, 1).reshape((lats * chips,) + grid.shape[2:])

    first = in_rows(joined(first, first_got, core, chip, bits - 1))
    x_wide = by_core(core, near, far, 1)
    wide_cols = x_wide.shape[1]
    x_wide = x_wide.reshape(-1, width)
    x_turned = lax.optimization_barrier(x_wide.T)
    go = by_core(core, grad_output, go_partner, 1)
    go = go.reshape(lat_rows // QROWS, QROWS, block_cols // QCOLS, QCOLS, width)
    go = lax.optimization_barrier(jnp.swapaxes(go, 1, 2).reshape(-1, width))

    def heads_of(which):
        qkv = lax.dynamic_slice_in_dim(first, which * per, per, 2).reshape(half, per)
        count = lats * chips // 2
        out = lax.dynamic_slice_in_dim(first, which * count, count, 0)[..., 2 * per :].reshape(-1, width)
        return qkv, out

    qkv_mine, out_mine = heads_of(core)
    qkv_other, out_other = heads_of(1 - core)
    cut = out_other.shape[0]
    swap = jnp.concatenate([jnp.concatenate([qkv_other[:cut], qkv_other[cut:]], axis=1), out_other], axis=0)
    swap = partner(swap)
    qkv_got = jnp.concatenate([swap[:cut, :per], swap[:cut, per:]], axis=0)

    def interleaved(mine, got):
        mine, got = (part.reshape(-1, rows, part.shape[1]) for part in (mine, got))
        return by_core(core, mine, got, 1).reshape(-1, mine.shape[2])

    qkv_first = interleaved(qkv_mine, qkv_got)
    out_heads = interleaved(out_mine, swap[cut:])

    bias, hot = window_columns(lat * lat_rows, lat_rows // QROWS, lat_rows * lats, lanes)
    scale = jnp.concatenate(
        [jnp.full((lanes,), LOG2E / math.sqrt(head), jnp.float32), jnp.ones((2 * lanes,), jnp.float32)]
    )

    def project(weights):
        result = dot(x_wide, weights) * jnp.tile(scale, weights.shape[1] // per)
        return result.astype(jnp.bfloat16).reshape(wide_rows, wide_cols, -1)

    def half_rows(grads, which):
        return lax.dynamic_slice_in_dim(grads, which * (grads.shape[0] // 2), grads.shape[0] // 2, 0)

    rest = turned([rest] + list(rest_moved), lat)
    for phase in range(bits - 1):
        rest = joined(rest, across(rest, phase), core, chip, phase)
    projected = project(qkv_first)
    g = dot(go, out_heads, NT).astype(jnp.bfloat16)
    projected, g, rest = lax.optimization_barrier((projected, g, rest))
    rest_got = across(rest, bits - 1)
    att_0, grads_0 = attention(projected, g, bias, hot, 0, 0, lanes)
    att_0, grads_0, rest_got = lax.optimization_barrier((att_0, grads_0, rest_got))
    rest = in_rows(joined(rest, rest_got, core, chip, bits - 1))
    qkv_rest = rest.reshape(half * 2, -1)
    grads_0 = grads_0.reshape(-1, per)
    early_0 = dot(x_turned, grads_0).astype(jnp.bfloat16)
    projected = project(qkv_rest[:, :per])
    att_1, grads_1 = attention(projected, g, bias, hot, 0, 1, lanes)
    projected = project(qkv_rest[:, per:])

    grads_1 = grads_1.reshape(-1, per)
    early = [early_0, dot(x_turned, grads_1).astype(jnp.bfloat16)]
    early = [halved(part.reshape(lats, chips, -1, per), core, chip, 0) for part in early]
    early_kept, early_moved = (jnp.concatenate(parts, axis=-1) for parts in zip(*early))

    def gx_early(which):
        first_part = dot(half_rows(grads_0, which), qkv_first, NT)
        return (first_part + dot(half_rows(grads_1, which), qkv_rest[:, :per], NT)).astype(jnp.bfloat16)

    give_early, keep_early = gx_early(1 - core), gx_early(core)
    out_rows = [dot(part, go).astype(jnp.bfloat16) for part in (att_0, att_1)]
    g, early_kept, give_early, keep_early, early_moved, *out_rows = lax.optimization_barrier(
        (g, early_kept, give_early, keep_early, early_moved, *out_rows)
    )
    early_moved = across(early_moved, 0)
    att_2, grads_2 = attention(projected, g, bias, hot, 0, 2, lanes)
    grads_2 = grads_2.reshape(-1, per)

    def gx_late(which, before):
        return dot(half_rows(grads_2, which), qkv_rest[:, per:], NT) + before.astype(jnp.float32)

    give = gx_late(1 - core, give_early).astype(jnp.bfloat16)
    give, att_2, grads_2, early_moved = lax.optimization_barrier((give, att_2, grads_2, early_moved))
    given = partner(give)
    out_rows = jnp.concatenate(out_rows + [dot(att_2, go).astype(jnp.bfloat16)], axis=0)
    swapped = partner(lax.dynamic_slice_in_dim(out_rows, (1 - core) * half, half, 1))
    early = grown(early_kept, early_moved)
    for phase in range(1, bits):
        early, early_moved = halved(early, core, chip, phase)
        early = grown(early, across(early_moved, phase))
    early = early[:, 0]
    late = dot(x_turned, grads_2).astype(jnp.bfloat16)
    out_mine = by_core(core, lax.dynamic_slice_in_dim(out_rows, core * half, half, 1), swapped, 0)
    late = jnp.concatenate([late, out_mine], axis=1).reshape(lats, chips, -1, per + half)
    given, late = lax.optimization_barrier((given, late))
    late, late_moved = halved(late, core, chip, 0)
    late_moved = across(late_moved, 0)
    gx = gx_late(core, keep_early) + given.astype(jnp.float32)
    gx = gx.reshape(wide_rows // 2, wide_cols, width)
    own = wide_rows // 2 - RADIUS
    outer = jnp.where(core == 0, gx[:RADIUS], gx[own:]).astype(jnp.bfloat16)
    gx = jnp.where(core == 0, gx[RADIUS:], gx[:own])
    inner = routed(outer, lambda a, o: (a + 1, o - 1) if o % 2 else (a - 1, o + 1))
    early_moved = lat_moves([pick(early, lat + d, lats, 0).astype(jnp.bfloat16) for d in range(1, lats)])
    late = grown(late, late_moved)
    for phase in range(1, bits):
        late, late_moved = halved(late, core, chip, phase)
        late_moved = across(late_moved, phase)
        if phase < bits - 1:
            late = grown(late, late_moved)
    gap = jnp.zeros((own - RADIUS,) + gx.shape[1:], jnp.float32)
    gx = gx + by_core(core, inner.astype(jnp.float32), gap, 0)
    other_half = lax.dynamic_slice_in_dim(gx, MARGIN + (1 - core) * lon_cols, lon_cols, 1).astype(jnp.bfloat16)
    mine_half = lax.dynamic_slice_in_dim(gx, MARGIN + core * lon_cols, lon_cols, 1)
    left, right = gx[:, :MARGIN].astype(jnp.bfloat16), gx[:, wide_cols - MARGIN :].astype(jnp.bfloat16)
    left, right, mine_half, other_half, late_moved = lax.optimization_barrier(
        (left, right, mine_half, other_half, late_moved)
    )
    early = added(pick(early, lat, lats, 0), early_moved)
    late = scatter_rest(grown(late, late_moved)[:, 0], lat)
    same = routed(jnp.where(core == 0, right, left), lambda a, o: (a, o - 2 if o % 2 else o + 2))
    cross = routed(jnp.where(core == 0, left, right), lambda a, o: (a, o + 1 if o % 2 else o - 1))
    swapped_x = partner(other_half)
    pad = jnp.zeros((own, lon_cols - MARGIN, width), jnp.float32)
    here = mine_half + by_core(core, same.astype(jnp.float32), pad, 1)
    there = swapped_x.astype(jnp.float32) + by_core(core, cross.astype(jnp.float32), pad, 1)
    grad_x = by_core(core, here.astype(jnp.bfloat16), there.astype(jnp.bfloat16), 0)

    total = jnp.concatenate([early, late], axis=1).reshape(2, rows, -1)
    keep = lax.dynamic_index_in_dim(total, core, 0, keepdims=False)
    give = lax.dynamic_index_in_dim(total, 1 - core, 0, keepdims=False).astype(jnp.bfloat16)
    got = partner(give).astype(jnp.float32)
    order = jnp.where(core == 0, jnp.stack([keep, got]), jnp.stack([got, keep]))
    grad_qkv = order[:, :, : groups * per].reshape(2, rows, groups, 3, lanes)
    grad_qkv = jnp.transpose(grad_qkv, (1, 3, 0, 2, 4)).reshape(rows, 3 * width)
    grad_out = jnp.transpose(order[:, :, groups * per :], (1, 0, 2)).reshape(rows, width)
    return grad_x, grad_qkv, grad_out


def solution(mesh):
    placed = (
        P("lat", "lon", None),
        P("lat", "lon", None),
        P(("lat", "lon"), None),
        P(("lat", "lon"), None),
    )
    return jax.shard_map(
        shards,
        mesh=mesh,
        in_specs=placed,
        out_specs=(P("lat", "lon", None), P(("lat", "lon"), None), P(("lat", "lon"), None)),
        check_vma=False,
    )
```

```python
import math

import jax
import jax.numpy as jnp
from jax import lax
from jax.experimental import pallas as pl
from jax.experimental.pallas import tpu as pltpu
from jax.sharding import PartitionSpec as P

HEADS = 12
RADIUS = 6
QROWS = 16
QCOLS = 16
MARGIN = 8
PAIR = 2
OUTSIDE = -1e30
LOG2E = math.log2(math.e)

NT = (((1,), (1,)), ((), ()))
NN = (((1,), (0,)), ((), ()))


def dot(a, b, dims=NN):
    return lax.dot_general(a, b, dims, preferred_element_type=jnp.float32)


def attention_kernel(p_ref, g_ref, bias_ref, hot_ref, att_ref, grad_ref, *scratch):
    scores, e_both, ds_both, sums = scratch[:PAIR], scratch[PAIR], scratch[PAIR + 1], scratch[PAIR + 2]
    tile_row, tile_col = pl.program_id(0), pl.program_id(1)
    key_rows, key_cols = QROWS + 2 * RADIUS, QCOLS + 2 * MARGIN
    keys, queries = key_rows * key_cols, QROWS * QCOLS
    lanes = g_ref.shape[-1]
    head = lanes // PAIR
    chunk = 64
    first_row = tile_row * QROWS
    first_col = pl.multiple_of(tile_col * QCOLS, QCOLS)
    at_rows, at_cols = pl.ds(first_row, key_rows), pl.ds(first_col, key_cols)
    q_lanes, k_lanes, v_lanes = (slice(i * lanes, (i + 1) * lanes) for i in range(3))
    heads = range(PAIR)
    rows = [slice(h * head, (h + 1) * head) for h in heads]
    cols = [slice(h * queries, (h + 1) * queries) for h in heads]

    @pl.when((tile_row == 0) & (tile_col == 0))
    def _():
        sums[...] = jnp.zeros_like(sums)

    q = p_ref[pl.ds(first_row + RADIUS, QROWS), at_cols, q_lanes].astype(jnp.float32)
    q = q[:, MARGIN : MARGIN + QCOLS].reshape(queries, lanes).astype(jnp.bfloat16)
    g_t = g_ref[...].astype(jnp.float32).T
    k = p_ref[at_rows, at_cols, k_lanes].reshape(keys, lanes)
    v = p_ref[at_rows, at_cols, v_lanes].reshape(keys, lanes)
    k_wide = jnp.concatenate([k, bias_ref[0]], axis=1)
    ones = jnp.ones((16, keys), jnp.bfloat16)
    lane = lax.broadcasted_iota(jnp.int32, (queries, lanes), 1) // head
    q_heads = [jnp.where(lane == h, q, jnp.zeros_like(q)) for h in heads]
    for h in heads:
        scores[h][...] = dot(k_wide, jnp.concatenate([q_heads[h], hot_ref[...]], axis=1), NT)
    k_t, v_t = k.T, v.T
    g_heads, att_t, dq_t, terms = [], [], [], []
    for h in heads:
        top = jnp.max(scores[h][...], axis=0, keepdims=True)
        for c in range(0, keys, chunk):
            e_both[c : c + chunk, cols[h]] = jnp.exp2(scores[h][c : c + chunk] - top).astype(jnp.bfloat16)
        out = dot(jnp.concatenate([v_t[rows[h]], ones], axis=0), e_both[:, cols[h]])
        inverse = 1.0 / out[head : head + 1]
        attended = (out[:head] * inverse).astype(jnp.bfloat16).astype(jnp.float32)
        att_t.append(attended)
        g_one = g_t[rows[h]] * inverse
        terms.append(jnp.sum(g_one * attended, axis=0, keepdims=True))
        empty = jnp.zeros_like(g_one)
        g_one = jnp.concatenate([empty] * h + [g_one] + [empty] * (PAIR - 1 - h), axis=0).astype(jnp.bfloat16)
        g_heads.append(g_one)
    for h in heads:
        scores[h][...] = dot(v, g_heads[h])
    for h in heads:
        for c in range(0, keys, chunk):
            ds_both[c : c + chunk, cols[h]] = (
                e_both[c : c + chunk, cols[h]].astype(jnp.float32) * (scores[h][c : c + chunk] - terms[h])
            ).astype(jnp.bfloat16)
        dq_t.append(dot(k_t[rows[h]], ds_both[:, cols[h]]))
    tile = (key_rows, key_cols, lanes)
    sums[at_rows, at_cols, v_lanes] += dot(e_both[...], jnp.concatenate(g_heads, axis=1), NT).reshape(tile)
    sums[at_rows, at_cols, k_lanes] += dot(ds_both[...], jnp.concatenate(q_heads, axis=0)).reshape(tile)
    att_ref[...] = jnp.concatenate(att_t, axis=0).astype(jnp.bfloat16)
    dq = jnp.concatenate(dq_t, axis=0).T * (1.0 / math.sqrt(head))
    sums[pl.ds(first_row + RADIUS, QROWS), pl.ds(pl.multiple_of(first_col + MARGIN, 8), QCOLS), q_lanes] = dq.reshape(
        QROWS, QCOLS, lanes
    )

    @pl.when((tile_row == pl.num_programs(0) - 1) & (tile_col == pl.num_programs(1) - 1))
    def _():
        grad_ref[:, :, q_lanes] = sums[:, :, q_lanes].astype(jnp.bfloat16)
        grad_ref[:, :, k_lanes] = (sums[:, :, k_lanes] * (1.0 / LOG2E)).astype(jnp.bfloat16)
        grad_ref[:, :, v_lanes] = sums[:, :, v_lanes].astype(jnp.bfloat16)


def attention(projected, g, bias, hot, place, g_place, lanes):
    wide = projected.shape[:2] + (3 * lanes,)
    queries, keys = QROWS * QCOLS, (QROWS + 2 * RADIUS) * (QCOLS + 2 * MARGIN)
    tiles = ((wide[0] - 2 * RADIUS) // QROWS, (wide[1] - 2 * MARGIN) // QCOLS)
    count = tiles[0] * tiles[1]
    return pl.pallas_call(
        attention_kernel,
        grid=tiles,
        in_specs=[
            pl.BlockSpec(wide, lambda r, c: (0, 0, place)),
            pl.BlockSpec((queries, lanes), lambda r, c: (r * tiles[1] + c, g_place)),
            pl.BlockSpec((1, keys, lanes), lambda r, c: (r, 0, 0)),
            pl.BlockSpec((queries, lanes), lambda r, c: (0, 0)),
        ],
        out_specs=[
            pl.BlockSpec((lanes, queries), lambda r, c: (0, r * tiles[1] + c)),
            pl.BlockSpec(wide, lambda r, c: (0, 0, 0)),
        ],
        out_shape=[
            jax.ShapeDtypeStruct((lanes, count * queries), jnp.bfloat16),
            jax.ShapeDtypeStruct(wide, jnp.bfloat16),
        ],
        scratch_shapes=[pltpu.VMEM((keys, queries), jnp.float32)] * PAIR
        + [pltpu.VMEM((keys, PAIR * queries), jnp.bfloat16)] * 2
        + [pltpu.VMEM(wide, jnp.float32)],
        compiler_params=pltpu.CompilerParams(
            dimension_semantics=("arbitrary", "arbitrary"), vmem_limit_bytes=48 * 1024 * 1024
        ),
        cost_estimate=pl.CostEstimate(
            flops=2 * 12 * 256 * keys * queries * PAIR * count,
            bytes_accessed=12 * count * queries * lanes * 2,
            transcendentals=keys * queries * PAIR * count,
        ),
    )(projected, g, bias, hot)


def window_columns(lat_first, tile_rows, total_rows, lanes):
    key_rows, key_cols = QROWS + 2 * RADIUS, QCOLS + 2 * MARGIN
    base = lat_first + QROWS * jnp.arange(tile_rows, dtype=jnp.int32)[:, None, None]
    q_row = base + jnp.arange(QROWS, dtype=jnp.int32)[None, None, :]
    k_row = base - RADIUS + jnp.arange(key_rows, dtype=jnp.int32)[None, :, None]
    start = jnp.clip(q_row - RADIUS, 0, total_rows - 2 * RADIUS - 1)
    row_in = (k_row >= start) & (k_row <= start + 2 * RADIUS)
    q_col = jnp.arange(QCOLS, dtype=jnp.int32)[None, :]
    k_col = jnp.arange(key_cols, dtype=jnp.int32)[:, None] - MARGIN
    col_in = (k_col >= q_col - RADIUS) & (k_col <= q_col + RADIUS)
    shape = (tile_rows, key_rows, key_cols)
    row_part = jnp.broadcast_to(jnp.where(row_in, 0.0, OUTSIDE)[:, :, None, :], shape + (QROWS,))
    col_part = jnp.broadcast_to(jnp.where(col_in, 0.0, OUTSIDE)[None, None], shape + (QCOLS,))
    rest = jnp.zeros(shape + (lanes - QROWS - QCOLS,), jnp.float32)
    columns = jnp.concatenate([row_part, col_part, rest], axis=-1).astype(jnp.bfloat16)
    columns = columns.reshape(tile_rows, key_rows * key_cols, lanes)
    r, c = jnp.arange(QROWS * QCOLS) // QCOLS, jnp.arange(QROWS * QCOLS) % QCOLS
    lane = jnp.arange(lanes)[None, :]
    hot = ((lane == r[:, None]) | (lane == QROWS + c[:, None])).astype(jnp.bfloat16)
    return columns, hot


def routed(value, route):
    lats, lons = lax.axis_size("lat"), lax.axis_size("lon")
    pairs = []
    for a in range(lats):
        for o in range(lons):
            to_lat, to_lon = route(a, o)
            if 0 <= to_lat < lats:
                pairs.append((a * lons + o, to_lat * lons + to_lon % lons))
    return lax.ppermute(value, ("lat", "lon"), pairs)


def partner(value):
    return routed(value, lambda a, o: (a, o ^ 1))


def beside(o):
    return o + 1 if o % 2 else o - 1


def by_core(core, mine, other, axis):
    return jnp.where(
        core == 0, jnp.concatenate([mine, other], axis=axis), jnp.concatenate([other, mine], axis=axis)
    )


def turned(parts, by):
    count = len(parts)
    whole = jnp.zeros((count,) + parts[0].shape, parts[0].dtype)
    for d, part in enumerate(parts):
        whole = lax.dynamic_update_index_in_dim(whole, part, (by - d) % count, 0)
    return whole


def lat_moves(blocks):
    lats = lax.axis_size("lat")
    return [routed(part, lambda a, o, d=d + 1: ((a + d) % lats, o)) for d, part in enumerate(blocks)]


def lon_bits():
    return (lax.axis_size("lon") // 2 - 1).bit_length()


def across(value, phase):
    last = lon_bits() - 1
    return routed(value, lambda a, o: (a, o ^ (2 << (last - phase if o % 2 else phase))))


def own_bit(core, chip, phase):
    return (chip >> jnp.where(core == 0, phase, lon_bits() - 1 - phase)) & 1


def joined(held, got, core, chip, phase):
    bit = own_bit(core, chip, phase)
    low, high = jnp.where(bit == 0, held, got), jnp.where(bit == 0, got, held)
    if phase == 0:
        return jnp.stack([low, high], 0)
    return jnp.where(core == 0, jnp.stack([low, high], 0), jnp.stack([low, high], phase))


def halved(total, core, chip, phase):
    bit = own_bit(core, chip, phase)
    lats, left = total.shape[:2]
    by_low = total.reshape((lats, left // 2, 2) + total.shape[2:])
    by_high = total.reshape((lats, 2, left // 2) + total.shape[2:])

    def half(which):
        low = lax.dynamic_index_in_dim(by_low, which, 2, keepdims=False)
        return jnp.where(core == 0, low, lax.dynamic_index_in_dim(by_high, which, 1, keepdims=False))

    return half(bit), half(1 - bit).astype(jnp.bfloat16)


def grown(kept, got):
    return kept.astype(jnp.float32) + got.astype(jnp.float32)


def pick(value, index, count, dim):
    return lax.dynamic_index_in_dim(value, index % count, dim, keepdims=False)


def added(kept, parts):
    for part in parts:
        kept = kept + part.astype(jnp.float32)
    return kept


def scatter_rest(kept, lat):
    lats = lax.axis_size("lat")
    moved = lat_moves([pick(kept, lat + d, lats, 0).astype(jnp.bfloat16) for d in range(1, lats)])
    return added(pick(kept, lat, lats, 0), moved)


def after(value, *others):
    return lax.optimization_barrier((value,) + others)[0]


def shards(features, grad_output, qkv_weight, out_weight):
    lat_rows, lon_cols, width = features.shape
    head = width // HEADS
    lanes = PAIR * head
    groups = HEADS // PAIR // 2
    half = width // 2
    lats, chips = lax.axis_size("lat"), lax.axis_size("lon") // 2
    lat, lon = lax.axis_index("lat"), lax.axis_index("lon")
    core, chip = lon % 2, lon // 2
    rows = qkv_weight.shape[0]
    per = 3 * lanes
    cells = lat_rows * lon_cols
    block_cols = 2 * lon_cols
    half_cols = lon_cols + MARGIN

    edge = jnp.where(core == 0, features[:, :MARGIN], features[:, lon_cols - MARGIN :])
    side = routed(edge, lambda a, o: (a, beside(o)))

    by_heads = qkv_weight.reshape(rows, 3, 2, groups, lanes)
    first = [by_heads[:, i, c, 0] for c in range(2) for i in range(3)]
    first = after(jnp.concatenate(first + [out_weight], axis=1), side)
    first_moved = lat_moves([first] * (lats - 1))

    def columns(which):
        qkv = lax.dynamic_index_in_dim(by_heads, which, 2, keepdims=False)[:, :, 1:]
        return jnp.swapaxes(qkv, 1, 2).reshape(rows, -1)

    near = jnp.where(
        core == 0, jnp.concatenate([side, features], axis=1), jnp.concatenate([features, side], axis=1)
    )
    above = routed(near[lat_rows - RADIUS :], lambda a, o: (a + 1, o))
    below = routed(near[:RADIUS], lambda a, o: (a - 1, o))
    rest = by_core(core, columns(core), partner(columns(1 - core)), 0)
    first, rest, above, below = lax.optimization_barrier((turned([first] + first_moved, lat), rest, above, below))
    rest_moved = lat_moves([rest] * (lats - 1))

    both = [features.reshape(cells, width), grad_output.reshape(cells, width), side.reshape(-1, width)]
    both = partner(jnp.concatenate(both, axis=0))
    bits = lon_bits()
    for phase in range(bits - 1):
        first = joined(first, across(first, phase), core, chip, phase)
    first_got = across(first, bits - 1)
    x_partner = both[:cells].reshape(features.shape)
    go_partner = both[cells : 2 * cells].reshape(features.shape)
    side_partner = both[2 * cells :].reshape(side.shape)
    far = jnp.where(
        core == 0,
        jnp.concatenate([x_partner, side_partner], axis=1),
        jnp.concatenate([side_partner, x_partner], axis=1),
    )
    above, below, far, first_got, *moved = lax.optimization_barrier((above, below, far, first_got, *rest_moved[:-1]))
    rest_moved[:-1] = moved
    caps = partner(jnp.concatenate([above, below], axis=0))
    near = jnp.concatenate([above, near, below], axis=0)
    far = jnp.concatenate([caps[:RADIUS], far, caps[RADIUS:]], axis=0)
    wide_rows = near.shape[0]

    def in_rows(grid):
        grid = grid.reshape((chips,) + grid.shape[bits:])
        return jnp.swapaxes(grid, 0, 1).reshape((lats * chips,) + grid.shape[2:])

    first = in_rows(joined(first, first_got, core, chip, bits - 1))
    x_wide = by_core(core, near, far, 1)
    wide_cols = x_wide.shape[1]
    x_wide = x_wide.reshape(-1, width)
    x_turned = lax.optimization_barrier(x_wide.T)
    go = by_core(core, grad_output, go_partner, 1)
    go = go.reshape(lat_rows // QROWS, QROWS, block_cols // QCOLS, QCOLS, width)
    go = lax.optimization_barrier(jnp.swapaxes(go, 1, 2).reshape(-1, width))

    def heads_of(which):
        qkv = lax.dynamic_slice_in_dim(first, which * per, per, 2).reshape(half, per)
        count = lats * chips // 2
        out = lax.dynamic_slice_in_dim(first, which * count, count, 0)[..., 2 * per :].reshape(-1, width)
        return qkv, out

    qkv_mine, out_mine = heads_of(core)
    qkv_other, out_other = heads_of(1 - core)
    cut = out_other.shape[0]
    swap = jnp.concatenate([jnp.concatenate([qkv_other[:cut], qkv_other[cut:]], axis=1), out_other], axis=0)
    swap = partner(swap)
    qkv_got = jnp.concatenate([swap[:cut, :per], swap[:cut, per:]], axis=0)

    def interleaved(mine, got):
        mine, got = (part.reshape(-1, rows, part.shape[1]) for part in (mine, got))
        return by_core(core, mine, got, 1).reshape(-1, mine.shape[2])

    qkv_first = interleaved(qkv_mine, qkv_got)
    out_heads = interleaved(out_mine, swap[cut:])

    bias, hot = window_columns(lat * lat_rows, lat_rows // QROWS, lat_rows * lats, lanes)
    scale = jnp.concatenate(
        [jnp.full((lanes,), LOG2E / math.sqrt(head), jnp.float32), jnp.ones((2 * lanes,), jnp.float32)]
    )

    def project(weights):
        result = dot(x_wide, weights) * jnp.tile(scale, weights.shape[1] // per)
        return result.astype(jnp.bfloat16).reshape(wide_rows, wide_cols, -1)

    def half_rows(grads, which):
        return lax.dynamic_slice_in_dim(grads, which * (grads.shape[0] // 2), grads.shape[0] // 2, 0)

    rest = turned([rest] + list(rest_moved), lat)
    for phase in range(bits - 1):
        rest = joined(rest, across(rest, phase), core, chip, phase)
    projected = project(qkv_first)
    g = dot(go, out_heads, NT).astype(jnp.bfloat16)
    projected, g, rest = lax.optimization_barrier((projected, g, rest))
    rest_got = across(rest, bits - 1)
    att_0, grads_0 = attention(projected, g, bias, hot, 0, 0, lanes)
    att_0, grads_0, rest_got = lax.optimization_barrier((att_0, grads_0, rest_got))
    rest = in_rows(joined(rest, rest_got, core, chip, bits - 1))
    qkv_rest = rest.reshape(half * 2, -1)
    grads_0 = grads_0.reshape(-1, per)
    early_0 = dot(x_turned, grads_0).astype(jnp.bfloat16)
    projected = project(qkv_rest[:, :per])
    att_1, grads_1 = attention(projected, g, bias, hot, 0, 1, lanes)
    projected = project(qkv_rest[:, per:])

    grads_1 = grads_1.reshape(-1, per)
    early = [early_0, dot(x_turned, grads_1).astype(jnp.bfloat16)]
    early = [halved(part.reshape(lats, chips, -1, per), core, chip, 0) for part in early]
    early_kept, early_moved = (jnp.concatenate(parts, axis=-1) for parts in zip(*early))

    def gx_early(which):
        first_part = dot(half_rows(grads_0, which), qkv_first, NT)
        return (first_part + dot(half_rows(grads_1, which), qkv_rest[:, :per], NT)).astype(jnp.bfloat16)

    give_early, keep_early = gx_early(1 - core), gx_early(core)
    out_rows = [dot(part, go).astype(jnp.bfloat16) for part in (att_0, att_1)]
    g, early_kept, give_early, keep_early, early_moved, *out_rows = lax.optimization_barrier(
        (g, early_kept, give_early, keep_early, early_moved, *out_rows)
    )
    early_moved = across(early_moved, 0)
    att_2, grads_2 = attention(projected, g, bias, hot, 0, 2, lanes)
    grads_2 = grads_2.reshape(-1, per)

    def gx_late(which, before):
        return dot(half_rows(grads_2, which), qkv_rest[:, per:], NT) + before.astype(jnp.float32)

    give = gx_late(1 - core, give_early).astype(jnp.bfloat16)
    give, att_2, grads_2, early_moved = lax.optimization_barrier((give, att_2, grads_2, early_moved))
    given = partner(give)
    out_rows = jnp.concatenate(out_rows + [dot(att_2, go).astype(jnp.bfloat16)], axis=0)
    swapped = partner(lax.dynamic_slice_in_dim(out_rows, (1 - core) * half, half, 1))
    early = grown(early_kept, early_moved)
    for phase in range(1, bits):
        early_kept, early_moved = halved(early, core, chip, phase)
        early_moved = across(early_moved, phase)
        if phase < bits - 1:
            early = grown(early_kept, early_moved)
    late = dot(x_turned, grads_2).astype(jnp.bfloat16)
    out_mine = by_core(core, lax.dynamic_slice_in_dim(out_rows, core * half, half, 1), swapped, 0)
    late = jnp.concatenate([late, out_mine], axis=1).reshape(lats, chips, -1, per + half)
    given, late = lax.optimization_barrier((given, late))
    late, late_moved = halved(late, core, chip, 0)
    late_moved = across(late_moved, 0)
    gx = gx_late(core, keep_early) + given.astype(jnp.float32)
    gx = gx.reshape(wide_rows // 2, wide_cols, width)
    own = wide_rows // 2 - RADIUS
    outer = jnp.where(core == 0, gx[:RADIUS], gx[own:]).astype(jnp.bfloat16)
    gx = jnp.where(core == 0, gx[RADIUS:], gx[:own])
    inner = routed(outer, lambda a, o: (a + 1, o - 1) if o % 2 else (a - 1, o + 1))
    early_moved, late_moved = lax.optimization_barrier((early_moved, late_moved))
    early = grown(early_kept, early_moved)[:, 0]
    early_moved = lat_moves([pick(early, lat + d, lats, 0).astype(jnp.bfloat16) for d in range(1, lats)])
    late = grown(late, late_moved)
    for phase in range(1, bits):
        late, late_moved = halved(late, core, chip, phase)
        late_moved = across(late_moved, phase)
        if phase < bits - 1:
            late = grown(late, late_moved)
    gap = jnp.zeros((own - RADIUS,) + gx.shape[1:], jnp.float32)
    gx = gx + by_core(core, inner.astype(jnp.float32), gap, 0)
    other_half = lax.dynamic_slice_in_dim(gx, MARGIN + (1 - core) * lon_cols, lon_cols, 1).astype(jnp.bfloat16)
    mine_half = lax.dynamic_slice_in_dim(gx, MARGIN + core * lon_cols, lon_cols, 1)
    left, right = gx[:, :MARGIN].astype(jnp.bfloat16), gx[:, wide_cols - MARGIN :].astype(jnp.bfloat16)
    left, right, mine_half, other_half, late_moved = lax.optimization_barrier(
        (left, right, mine_half, other_half, late_moved)
    )
    early = added(pick(early, lat, lats, 0), early_moved)
    late = scatter_rest(grown(late, late_moved)[:, 0], lat)
    same = routed(jnp.where(core == 0, right, left), lambda a, o: (a, o - 2 if o % 2 else o + 2))
    cross = routed(jnp.where(core == 0, left, right), lambda a, o: (a, o + 1 if o % 2 else o - 1))
    swapped_x = partner(other_half)
    pad = jnp.zeros((own, lon_cols - MARGIN, width), jnp.float32)
    here = mine_half + by_core(core, same.astype(jnp.float32), pad, 1)
    there = swapped_x.astype(jnp.float32) + by_core(core, cross.astype(jnp.float32), pad, 1)
    grad_x = by_core(core, here.astype(jnp.bfloat16), there.astype(jnp.bfloat16), 0)

    total = jnp.concatenate([early, late], axis=1).reshape(2, rows, -1)
    keep = lax.dynamic_index_in_dim(total, core, 0, keepdims=False)
    give = lax.dynamic_index_in_dim(total, 1 - core, 0, keepdims=False).astype(jnp.bfloat16)
    got = partner(give).astype(jnp.float32)
    order = jnp.where(core == 0, jnp.stack([keep, got]), jnp.stack([got, keep]))
    grad_qkv = order[:, :, : groups * per].reshape(2, rows, groups, 3, lanes)
    grad_qkv = jnp.transpose(grad_qkv, (1, 3, 0, 2, 4)).reshape(rows, 3 * width)
    grad_out = jnp.transpose(order[:, :, groups * per :], (1, 0, 2)).reshape(rows, width)
    return grad_x, grad_qkv, grad_out


def solution(mesh):
    placed = (
        P("lat", "lon", None),
        P("lat", "lon", None),
        P(("lat", "lon"), None),
        P(("lat", "lon"), None),
    )
    return jax.shard_map(
        shards,
        mesh=mesh,
        in_specs=placed,
        out_specs=(P("lat", "lon", None), P(("lat", "lon"), None), P(("lat", "lon"), None)),
        check_vma=False,
    )
```

```python
import math

import jax
import jax.numpy as jnp
from jax import lax
from jax.experimental import pallas as pl
from jax.experimental.pallas import tpu as pltpu
from jax.sharding import PartitionSpec as P

HEADS = 12
RADIUS = 6
QROWS = 16
QCOLS = 16
MARGIN = 8
PAIR = 2
OUTSIDE = -1e30
LOG2E = math.log2(math.e)

NT = (((1,), (1,)), ((), ()))
NN = (((1,), (0,)), ((), ()))


def dot(a, b, dims=NN):
    return lax.dot_general(a, b, dims, preferred_element_type=jnp.float32)


def attention_kernel(p_ref, g_ref, bias_ref, hot_ref, att_ref, grad_ref, *scratch):
    scores, e_both, ds_both, sums = scratch[:PAIR], scratch[PAIR], scratch[PAIR + 1], scratch[PAIR + 2]
    tile_row, tile_col = pl.program_id(0), pl.program_id(1)
    key_rows, key_cols = QROWS + 2 * RADIUS, QCOLS + 2 * MARGIN
    keys, queries = key_rows * key_cols, QROWS * QCOLS
    lanes = g_ref.shape[-1]
    head = lanes // PAIR
    chunk = 64
    first_row = tile_row * QROWS
    first_col = pl.multiple_of(tile_col * QCOLS, QCOLS)
    at_rows, at_cols = pl.ds(first_row, key_rows), pl.ds(first_col, key_cols)
    q_lanes, k_lanes, v_lanes = (slice(i * lanes, (i + 1) * lanes) for i in range(3))
    heads = range(PAIR)
    rows = [slice(h * head, (h + 1) * head) for h in heads]
    cols = [slice(h * queries, (h + 1) * queries) for h in heads]

    @pl.when((tile_row == 0) & (tile_col == 0))
    def _():
        sums[...] = jnp.zeros_like(sums)

    q = p_ref[pl.ds(first_row + RADIUS, QROWS), at_cols, q_lanes].astype(jnp.float32)
    q = q[:, MARGIN : MARGIN + QCOLS].reshape(queries, lanes).astype(jnp.bfloat16)
    g_t = g_ref[...].astype(jnp.float32).T
    k = p_ref[at_rows, at_cols, k_lanes].reshape(keys, lanes)
    v = p_ref[at_rows, at_cols, v_lanes].reshape(keys, lanes)
    k_wide = jnp.concatenate([k, bias_ref[0]], axis=1)
    ones = jnp.ones((16, keys), jnp.bfloat16)
    lane = lax.broadcasted_iota(jnp.int32, (queries, lanes), 1) // head
    q_heads = [jnp.where(lane == h, q, jnp.zeros_like(q)) for h in heads]
    for h in heads:
        scores[h][...] = dot(k_wide, jnp.concatenate([q_heads[h], hot_ref[...]], axis=1), NT)
    k_t, v_t = k.T, v.T
    g_heads, att_t, dq_t, terms = [], [], [], []
    for h in heads:
        top = jnp.max(scores[h][...], axis=0, keepdims=True)
        for c in range(0, keys, chunk):
            e_both[c : c + chunk, cols[h]] = jnp.exp2(scores[h][c : c + chunk] - top).astype(jnp.bfloat16)
        out = dot(jnp.concatenate([v_t[rows[h]], ones], axis=0), e_both[:, cols[h]])
        inverse = 1.0 / out[head : head + 1]
        attended = (out[:head] * inverse).astype(jnp.bfloat16).astype(jnp.float32)
        att_t.append(attended)
        g_one = g_t[rows[h]] * inverse
        terms.append(jnp.sum(g_one * attended, axis=0, keepdims=True))
        empty = jnp.zeros_like(g_one)
        g_one = jnp.concatenate([empty] * h + [g_one] + [empty] * (PAIR - 1 - h), axis=0).astype(jnp.bfloat16)
        g_heads.append(g_one)
    for h in heads:
        scores[h][...] = dot(v, g_heads[h])
    for h in heads:
        for c in range(0, keys, chunk):
            ds_both[c : c + chunk, cols[h]] = (
                e_both[c : c + chunk, cols[h]].astype(jnp.float32) * (scores[h][c : c + chunk] - terms[h])
            ).astype(jnp.bfloat16)
        dq_t.append(dot(k_t[rows[h]], ds_both[:, cols[h]]))
    tile = (key_rows, key_cols, lanes)
    sums[at_rows, at_cols, v_lanes] += dot(e_both[...], jnp.concatenate(g_heads, axis=1), NT).reshape(tile)
    sums[at_rows, at_cols, k_lanes] += dot(ds_both[...], jnp.concatenate(q_heads, axis=0)).reshape(tile)
    att_ref[...] = jnp.concatenate(att_t, axis=0).astype(jnp.bfloat16)
    dq = jnp.concatenate(dq_t, axis=0).T * (1.0 / math.sqrt(head))
    sums[pl.ds(first_row + RADIUS, QROWS), pl.ds(pl.multiple_of(first_col + MARGIN, 8), QCOLS), q_lanes] = dq.reshape(
        QROWS, QCOLS, lanes
    )

    @pl.when((tile_row == pl.num_programs(0) - 1) & (tile_col == pl.num_programs(1) - 1))
    def _():
        grad_ref[:, :, q_lanes] = sums[:, :, q_lanes].astype(jnp.bfloat16)
        grad_ref[:, :, k_lanes] = (sums[:, :, k_lanes] * (1.0 / LOG2E)).astype(jnp.bfloat16)
        grad_ref[:, :, v_lanes] = sums[:, :, v_lanes].astype(jnp.bfloat16)


def attention(projected, g, bias, hot, place, g_place, lanes):
    wide = projected.shape[:2] + (3 * lanes,)
    queries, keys = QROWS * QCOLS, (QROWS + 2 * RADIUS) * (QCOLS + 2 * MARGIN)
    tiles = ((wide[0] - 2 * RADIUS) // QROWS, (wide[1] - 2 * MARGIN) // QCOLS)
    count = tiles[0] * tiles[1]
    return pl.pallas_call(
        attention_kernel,
        grid=tiles,
        in_specs=[
            pl.BlockSpec(wide, lambda r, c: (0, 0, place)),
            pl.BlockSpec((queries, lanes), lambda r, c: (r * tiles[1] + c, g_place)),
            pl.BlockSpec((1, keys, lanes), lambda r, c: (r, 0, 0)),
            pl.BlockSpec((queries, lanes), lambda r, c: (0, 0)),
        ],
        out_specs=[
            pl.BlockSpec((lanes, queries), lambda r, c: (0, r * tiles[1] + c)),
            pl.BlockSpec(wide, lambda r, c: (0, 0, 0)),
        ],
        out_shape=[
            jax.ShapeDtypeStruct((lanes, count * queries), jnp.bfloat16),
            jax.ShapeDtypeStruct(wide, jnp.bfloat16),
        ],
        scratch_shapes=[pltpu.VMEM((keys, queries), jnp.float32)] * PAIR
        + [pltpu.VMEM((keys, PAIR * queries), jnp.bfloat16)] * 2
        + [pltpu.VMEM(wide, jnp.float32)],
        compiler_params=pltpu.CompilerParams(
            dimension_semantics=("arbitrary", "arbitrary"), vmem_limit_bytes=48 * 1024 * 1024
        ),
        cost_estimate=pl.CostEstimate(
            flops=2 * 12 * 256 * keys * queries * PAIR * count,
            bytes_accessed=12 * count * queries * lanes * 2,
            transcendentals=keys * queries * PAIR * count,
        ),
    )(projected, g, bias, hot)


def window_columns(lat_first, tile_rows, total_rows, lanes):
    key_rows, key_cols = QROWS + 2 * RADIUS, QCOLS + 2 * MARGIN
    base = lat_first + QROWS * jnp.arange(tile_rows, dtype=jnp.int32)[:, None, None]
    q_row = base + jnp.arange(QROWS, dtype=jnp.int32)[None, None, :]
    k_row = base - RADIUS + jnp.arange(key_rows, dtype=jnp.int32)[None, :, None]
    start = jnp.clip(q_row - RADIUS, 0, total_rows - 2 * RADIUS - 1)
    row_in = (k_row >= start) & (k_row <= start + 2 * RADIUS)
    q_col = jnp.arange(QCOLS, dtype=jnp.int32)[None, :]
    k_col = jnp.arange(key_cols, dtype=jnp.int32)[:, None] - MARGIN
    col_in = (k_col >= q_col - RADIUS) & (k_col <= q_col + RADIUS)
    shape = (tile_rows, key_rows, key_cols)
    row_part = jnp.broadcast_to(jnp.where(row_in, 0.0, OUTSIDE)[:, :, None, :], shape + (QROWS,))
    col_part = jnp.broadcast_to(jnp.where(col_in, 0.0, OUTSIDE)[None, None], shape + (QCOLS,))
    rest = jnp.zeros(shape + (lanes - QROWS - QCOLS,), jnp.float32)
    columns = jnp.concatenate([row_part, col_part, rest], axis=-1).astype(jnp.bfloat16)
    columns = columns.reshape(tile_rows, key_rows * key_cols, lanes)
    r, c = jnp.arange(QROWS * QCOLS) // QCOLS, jnp.arange(QROWS * QCOLS) % QCOLS
    lane = jnp.arange(lanes)[None, :]
    hot = ((lane == r[:, None]) | (lane == QROWS + c[:, None])).astype(jnp.bfloat16)
    return columns, hot


def routed(value, route):
    lats, lons = lax.axis_size("lat"), lax.axis_size("lon")
    pairs = []
    for a in range(lats):
        for o in range(lons):
            to_lat, to_lon = route(a, o)
            if 0 <= to_lat < lats:
                pairs.append((a * lons + o, to_lat * lons + to_lon % lons))
    return lax.ppermute(value, ("lat", "lon"), pairs)


def partner(value):
    return routed(value, lambda a, o: (a, o ^ 1))


def beside(o):
    return o + 1 if o % 2 else o - 1


def by_core(core, mine, other, axis):
    return jnp.where(
        core == 0, jnp.concatenate([mine, other], axis=axis), jnp.concatenate([other, mine], axis=axis)
    )


def turned(parts, by):
    count = len(parts)
    whole = jnp.zeros((count,) + parts[0].shape, parts[0].dtype)
    for d, part in enumerate(parts):
        whole = lax.dynamic_update_index_in_dim(whole, part, (by - d) % count, 0)
    return whole


def lat_moves(blocks):
    lats = lax.axis_size("lat")
    return [routed(part, lambda a, o, d=d + 1: ((a + d) % lats, o)) for d, part in enumerate(blocks)]


def chip_moves(blocks):
    return [routed(part, lambda a, o, d=d + 1: (a, o + 2 * d)) for d, part in enumerate(blocks)]


def lon_bits():
    return (lax.axis_size("lon") // 2 - 1).bit_length()


def across(value, phase):
    last = lon_bits() - 1
    return routed(value, lambda a, o: (a, o ^ (2 << (last - phase if o % 2 else phase))))


def own_bit(core, chip, phase):
    return (chip >> jnp.where(core == 0, phase, lon_bits() - 1 - phase)) & 1


def joined(held, got, core, chip, phase):
    bit = own_bit(core, chip, phase)
    low, high = jnp.where(bit == 0, held, got), jnp.where(bit == 0, got, held)
    if phase == 0:
        return jnp.stack([low, high], 0)
    return jnp.where(core == 0, jnp.stack([low, high], 0), jnp.stack([low, high], phase))


def halved(total, core, chip, phase):
    bit = own_bit(core, chip, phase)
    lats, left = total.shape[:2]
    by_low = total.reshape((lats, left // 2, 2) + total.shape[2:])
    by_high = total.reshape((lats, 2, left // 2) + total.shape[2:])

    def half(which):
        low = lax.dynamic_index_in_dim(by_low, which, 2, keepdims=False)
        return jnp.where(core == 0, low, lax.dynamic_index_in_dim(by_high, which, 1, keepdims=False))

    return half(bit), half(1 - bit).astype(jnp.bfloat16)


def grown(kept, got):
    return kept.astype(jnp.float32) + got.astype(jnp.float32)


def pick(value, index, count, dim):
    return lax.dynamic_index_in_dim(value, index % count, dim, keepdims=False)


def added(kept, parts):
    for part in parts:
        kept = kept + part.astype(jnp.float32)
    return kept


def scatter_rest(kept, lat):
    lats = lax.axis_size("lat")
    moved = lat_moves([pick(kept, lat + d, lats, 0).astype(jnp.bfloat16) for d in range(1, lats)])
    return added(pick(kept, lat, lats, 0), moved)


def after(value, *others):
    return lax.optimization_barrier((value,) + others)[0]


def shards(features, grad_output, qkv_weight, out_weight):
    lat_rows, lon_cols, width = features.shape
    head = width // HEADS
    lanes = PAIR * head
    groups = HEADS // PAIR // 2
    half = width // 2
    lats, chips = lax.axis_size("lat"), lax.axis_size("lon") // 2
    lat, lon = lax.axis_index("lat"), lax.axis_index("lon")
    core, chip = lon % 2, lon // 2
    rows = qkv_weight.shape[0]
    per = 3 * lanes
    cells = lat_rows * lon_cols
    block_cols = 2 * lon_cols
    half_cols = lon_cols + MARGIN

    edge = jnp.where(core == 0, features[:, :MARGIN], features[:, lon_cols - MARGIN :])
    side = routed(edge, lambda a, o: (a, beside(o)))

    by_heads = qkv_weight.reshape(rows, 3, 2, groups, lanes)
    first = [by_heads[:, i, c, 0] for c in range(2) for i in range(3)]
    first = after(jnp.concatenate(first + [out_weight], axis=1), edge)
    first_moved = lat_moves([first] * (lats - 1))

    def columns(which):
        qkv = lax.dynamic_index_in_dim(by_heads, which, 2, keepdims=False)[:, :, 1:]
        return jnp.swapaxes(qkv, 1, 2).reshape(rows, -1)

    both = [features.reshape(cells, width), grad_output.reshape(cells, width), side.reshape(-1, width)]
    both.append(columns(1 - core).reshape(-1, width))
    both = jnp.concatenate(both, axis=0)
    near = jnp.where(
        core == 0, jnp.concatenate([side, features], axis=1), jnp.concatenate([features, side], axis=1)
    )
    top, bottom = near[:RADIUS], near[lat_rows - RADIUS :]
    first = after(turned([first] + first_moved, lat), both, top, bottom)
    both = partner(both)
    above = routed(bottom, lambda a, o: (a + 1, o))
    below = routed(top, lambda a, o: (a - 1, o))
    first_moved = chip_moves([first] * (chips - 1))
    margin = MARGIN * lat_rows
    x_partner = both[:cells].reshape(features.shape)
    go_partner = both[cells : 2 * cells].reshape(features.shape)
    side_partner = both[2 * cells : 2 * cells + margin].reshape(side.shape)
    rest = by_core(core, columns(core), both[2 * cells + margin :].reshape(rows, -1), 0)
    far = jnp.where(
        core == 0,
        jnp.concatenate([x_partner, side_partner], axis=1),
        jnp.concatenate([side_partner, x_partner], axis=1),
    )
    rest, above, below, far = lax.optimization_barrier((rest, above, below, far))
    rest_moved = lat_moves([rest] * (lats - 1))
    moved = lax.optimization_barrier((above, below, *first_moved, *rest_moved[:-1]))
    above, below, first_moved, rest_moved[:-1] = moved[0], moved[1], list(moved[2 : chips + 1]), moved[chips + 1 :]
    caps = partner(jnp.concatenate([above, below], axis=0))
    near = jnp.concatenate([above, near, below], axis=0)
    far = jnp.concatenate([caps[:RADIUS], far, caps[RADIUS:]], axis=0)
    wide_rows = near.shape[0]

    bits = lon_bits()

    def in_rows(grid, dims):
        grid = grid.reshape((chips,) + grid.shape[dims:])
        return jnp.swapaxes(grid, 0, 1).reshape((lats * chips,) + grid.shape[2:])

    first = in_rows(turned([first] + first_moved, chip), 1)
    x_wide = by_core(core, near, far, 1)
    wide_cols = x_wide.shape[1]
    x_wide = x_wide.reshape(-1, width)
    x_turned = lax.optimization_barrier(x_wide.T)
    go = by_core(core, grad_output, go_partner, 1)
    go = go.reshape(lat_rows // QROWS, QROWS, block_cols // QCOLS, QCOLS, width)
    go = lax.optimization_barrier(jnp.swapaxes(go, 1, 2).reshape(-1, width))

    def heads_of(which):
        qkv = lax.dynamic_slice_in_dim(first, which * per, per, 2).reshape(half, per)
        count = lats * chips // 2
        out = lax.dynamic_slice_in_dim(first, which * count, count, 0)[..., 2 * per :].reshape(-1, width)
        return qkv, out

    qkv_mine, out_mine = heads_of(core)
    qkv_other, out_other = heads_of(1 - core)
    cut = out_other.shape[0]
    swap = jnp.concatenate([jnp.concatenate([qkv_other[:cut], qkv_other[cut:]], axis=1), out_other], axis=0)
    swap = partner(swap)
    qkv_got = jnp.concatenate([swap[:cut, :per], swap[:cut, per:]], axis=0)

    def interleaved(mine, got):
        mine, got = (part.reshape(-1, rows, part.shape[1]) for part in (mine, got))
        return by_core(core, mine, got, 1).reshape(-1, mine.shape[2])

    qkv_first = interleaved(qkv_mine, qkv_got)
    out_heads = interleaved(out_mine, swap[cut:])

    bias, hot = window_columns(lat * lat_rows, lat_rows // QROWS, lat_rows * lats, lanes)
    scale = jnp.concatenate(
        [jnp.full((lanes,), LOG2E / math.sqrt(head), jnp.float32), jnp.ones((2 * lanes,), jnp.float32)]
    )

    def project(weights):
        result = dot(x_wide, weights) * jnp.tile(scale, weights.shape[1] // per)
        return result.astype(jnp.bfloat16).reshape(wide_rows, wide_cols, -1)

    def half_rows(grads, which):
        return lax.dynamic_slice_in_dim(grads, which * (grads.shape[0] // 2), grads.shape[0] // 2, 0)

    rest = turned([rest] + list(rest_moved), lat)
    for phase in range(bits - 1):
        rest = joined(rest, across(rest, phase), core, chip, phase)
    projected = project(qkv_first)
    g = dot(go, out_heads, NT).astype(jnp.bfloat16)
    projected, g, rest = lax.optimization_barrier((projected, g, rest))
    rest_got = across(rest, bits - 1)
    att_0, grads_0 = attention(projected, g, bias, hot, 0, 0, lanes)
    att_0, grads_0, rest_got = lax.optimization_barrier((att_0, grads_0, rest_got))
    rest = in_rows(joined(rest, rest_got, core, chip, bits - 1), bits)
    qkv_rest = rest.reshape(half * 2, -1)
    grads_0 = grads_0.reshape(-1, per)
    early_0 = dot(x_turned, grads_0).astype(jnp.bfloat16)
    projected = project(qkv_rest[:, :per])
    att_1, grads_1 = attention(projected, g, bias, hot, 0, 1, lanes)
    projected = project(qkv_rest[:, per:])

    grads_1 = grads_1.reshape(-1, per)
    early = [early_0, dot(x_turned, grads_1).astype(jnp.bfloat16)]
    early = [halved(part.reshape(lats, chips, -1, per), core, chip, 0) for part in early]
    early_kept, early_moved = (jnp.concatenate(parts, axis=-1) for parts in zip(*early))

    def gx_early(which):
        first_part = dot(half_rows(grads_0, which), qkv_first, NT)
        return (first_part + dot(half_rows(grads_1, which), qkv_rest[:, :per], NT)).astype(jnp.bfloat16)

    give_early, keep_early = gx_early(1 - core), gx_early(core)
    out_rows = [dot(part, go).astype(jnp.bfloat16) for part in (att_0, att_1)]
    g, early_kept, give_early, keep_early, early_moved, *out_rows = lax.optimization_barrier(
        (g, early_kept, give_early, keep_early, early_moved, *out_rows)
    )
    early_moved = across(early_moved, 0)
    att_2, grads_2 = attention(projected, g, bias, hot, 0, 2, lanes)
    grads_2 = grads_2.reshape(-1, per)

    def gx_late(which, before):
        return dot(half_rows(grads_2, which), qkv_rest[:, per:], NT) + before.astype(jnp.float32)

    att_2, grads_2, early_moved = lax.optimization_barrier((att_2, grads_2, early_moved))
    early = grown(early_kept, early_moved)
    for phase in range(1, bits):
        early_kept, early_moved = halved(early, core, chip, phase)
        att_2, grads_2, early_moved = lax.optimization_barrier((att_2, grads_2, early_moved))
        early = grown(early_kept, across(early_moved, phase))
    early = early[:, 0]
    give = gx_late(1 - core, give_early).astype(jnp.bfloat16)
    given = partner(give)
    out_rows = jnp.concatenate(out_rows + [dot(att_2, go).astype(jnp.bfloat16)], axis=0)
    swapped = partner(lax.dynamic_slice_in_dim(out_rows, (1 - core) * half, half, 1))
    late = dot(x_turned, grads_2).astype(jnp.bfloat16)
    out_mine = by_core(core, lax.dynamic_slice_in_dim(out_rows, core * half, half, 1), swapped, 0)
    late = jnp.concatenate([late, out_mine], axis=1).reshape(lats, chips, -1, per + half)
    given, late = lax.optimization_barrier((given, late))
    late, late_moved = halved(late, core, chip, 0)
    late_moved = across(late_moved, 0)
    gx = gx_late(core, keep_early) + given.astype(jnp.float32)
    gx = gx.reshape(wide_rows // 2, wide_cols, width)
    own = wide_rows // 2 - RADIUS
    outer = jnp.where(core == 0, gx[:RADIUS], gx[own:]).astype(jnp.bfloat16)
    gx = jnp.where(core == 0, gx[RADIUS:], gx[:own])
    inner = routed(outer, lambda a, o: (a + 1, o - 1) if o % 2 else (a - 1, o + 1))
    early_moved = lat_moves([pick(early, lat + d, lats, 0).astype(jnp.bfloat16) for d in range(1, lats)])
    late = grown(late, late_moved)
    for phase in range(1, bits):
        late, late_moved = halved(late, core, chip, phase)
        late_moved = across(late_moved, phase)
        if phase < bits - 1:
            late = grown(late, late_moved)
    gap = jnp.zeros((own - RADIUS,) + gx.shape[1:], jnp.float32)
    gx = gx + by_core(core, inner.astype(jnp.float32), gap, 0)
    other_half = lax.dynamic_slice_in_dim(gx, MARGIN + (1 - core) * lon_cols, lon_cols, 1).astype(jnp.bfloat16)
    mine_half = lax.dynamic_slice_in_dim(gx, MARGIN + core * lon_cols, lon_cols, 1)
    left, right = gx[:, :MARGIN].astype(jnp.bfloat16), gx[:, wide_cols - MARGIN :].astype(jnp.bfloat16)
    left, right, mine_half, other_half, late_moved = lax.optimization_barrier(
        (left, right, mine_half, other_half, late_moved)
    )
    early = added(pick(early, lat, lats, 0), early_moved)
    late = scatter_rest(grown(late, late_moved)[:, 0], lat)
    same = routed(jnp.where(core == 0, right, left), lambda a, o: (a, o - 2 if o % 2 else o + 2))
    cross = routed(jnp.where(core == 0, left, right), lambda a, o: (a, o + 1 if o % 2 else o - 1))
    swapped_x = partner(other_half)
    pad = jnp.zeros((own, lon_cols - MARGIN, width), jnp.float32)
    here = mine_half + by_core(core, same.astype(jnp.float32), pad, 1)
    there = swapped_x.astype(jnp.float32) + by_core(core, cross.astype(jnp.float32), pad, 1)
    grad_x = by_core(core, here.astype(jnp.bfloat16), there.astype(jnp.bfloat16), 0)

    total = jnp.concatenate([early, late], axis=1).reshape(2, rows, -1)
    keep = lax.dynamic_index_in_dim(total, core, 0, keepdims=False)
    give = lax.dynamic_index_in_dim(total, 1 - core, 0, keepdims=False).astype(jnp.bfloat16)
    got = partner(give).astype(jnp.float32)
    order = jnp.where(core == 0, jnp.stack([keep, got]), jnp.stack([got, keep]))
    grad_qkv = order[:, :, : groups * per].reshape(2, rows, groups, 3, lanes)
    grad_qkv = jnp.transpose(grad_qkv, (1, 3, 0, 2, 4)).reshape(rows, 3 * width)
    grad_out = jnp.transpose(order[:, :, groups * per :], (1, 0, 2)).reshape(rows, width)
    return grad_x, grad_qkv, grad_out


def solution(mesh):
    placed = (
        P("lat", "lon", None),
        P("lat", "lon", None),
        P(("lat", "lon"), None),
        P(("lat", "lon"), None),
    )
    return jax.shard_map(
        shards,
        mesh=mesh,
        in_specs=placed,
        out_specs=(P("lat", "lon", None), P(("lat", "lon"), None), P(("lat", "lon"), None)),
        check_vma=False,
    )
```

```python
import math

import jax
import jax.numpy as jnp
from jax import lax
from jax.experimental import pallas as pl
from jax.experimental.pallas import tpu as pltpu
from jax.sharding import PartitionSpec as P

HEADS = 12
RADIUS = 6
QROWS = 16
QCOLS = 16
MARGIN = 8
PAIR = 2
OUTSIDE = -1e30
LOG2E = math.log2(math.e)

NT = (((1,), (1,)), ((), ()))
NN = (((1,), (0,)), ((), ()))


def dot(a, b, dims=NN):
    return lax.dot_general(a, b, dims, preferred_element_type=jnp.float32)


def attention_kernel(p_ref, g_ref, bias_ref, hot_ref, att_ref, grad_ref, *scratch):
    scores, e_both, ds_both, sums = scratch[:PAIR], scratch[PAIR], scratch[PAIR + 1], scratch[PAIR + 2]
    tile_row, tile_col = pl.program_id(0), pl.program_id(1)
    key_rows, key_cols = QROWS + 2 * RADIUS, QCOLS + 2 * MARGIN
    keys, queries = key_rows * key_cols, QROWS * QCOLS
    lanes = g_ref.shape[-1]
    head = lanes // PAIR
    chunk = 64
    first_row = tile_row * QROWS
    first_col = pl.multiple_of(tile_col * QCOLS, QCOLS)
    at_rows, at_cols = pl.ds(first_row, key_rows), pl.ds(first_col, key_cols)
    q_lanes, k_lanes, v_lanes = (slice(i * lanes, (i + 1) * lanes) for i in range(3))
    heads = range(PAIR)
    rows = [slice(h * head, (h + 1) * head) for h in heads]
    cols = [slice(h * queries, (h + 1) * queries) for h in heads]

    @pl.when((tile_row == 0) & (tile_col == 0))
    def _():
        sums[...] = jnp.zeros_like(sums)

    q = p_ref[pl.ds(first_row + RADIUS, QROWS), at_cols, q_lanes].astype(jnp.float32)
    q = q[:, MARGIN : MARGIN + QCOLS].reshape(queries, lanes).astype(jnp.bfloat16)
    g_t = g_ref[...].astype(jnp.float32).T
    k = p_ref[at_rows, at_cols, k_lanes].reshape(keys, lanes)
    v = p_ref[at_rows, at_cols, v_lanes].reshape(keys, lanes)
    k_wide = jnp.concatenate([k, bias_ref[0]], axis=1)
    ones = jnp.ones((16, keys), jnp.bfloat16)
    lane = lax.broadcasted_iota(jnp.int32, (queries, lanes), 1) // head
    q_heads = [jnp.where(lane == h, q, jnp.zeros_like(q)) for h in heads]
    for h in heads:
        scores[h][...] = dot(k_wide, jnp.concatenate([q_heads[h], hot_ref[...]], axis=1), NT)
    k_t, v_t = k.T, v.T
    g_heads, att_t, dq_t, terms = [], [], [], []
    for h in heads:
        top = jnp.max(scores[h][...], axis=0, keepdims=True)
        for c in range(0, keys, chunk):
            e_both[c : c + chunk, cols[h]] = jnp.exp2(scores[h][c : c + chunk] - top).astype(jnp.bfloat16)
        out = dot(jnp.concatenate([v_t[rows[h]], ones], axis=0), e_both[:, cols[h]])
        inverse = 1.0 / out[head : head + 1]
        attended = (out[:head] * inverse).astype(jnp.bfloat16).astype(jnp.float32)
        att_t.append(attended)
        g_one = g_t[rows[h]] * inverse
        terms.append(jnp.sum(g_one * attended, axis=0, keepdims=True))
        empty = jnp.zeros_like(g_one)
        g_one = jnp.concatenate([empty] * h + [g_one] + [empty] * (PAIR - 1 - h), axis=0).astype(jnp.bfloat16)
        g_heads.append(g_one)
    for h in heads:
        scores[h][...] = dot(v, g_heads[h])
    for h in heads:
        for c in range(0, keys, chunk):
            ds_both[c : c + chunk, cols[h]] = (
                e_both[c : c + chunk, cols[h]].astype(jnp.float32) * (scores[h][c : c + chunk] - terms[h])
            ).astype(jnp.bfloat16)
        dq_t.append(dot(k_t[rows[h]], ds_both[:, cols[h]]))
    tile = (key_rows, key_cols, lanes)
    sums[at_rows, at_cols, v_lanes] += dot(e_both[...], jnp.concatenate(g_heads, axis=1), NT).reshape(tile)
    sums[at_rows, at_cols, k_lanes] += dot(ds_both[...], jnp.concatenate(q_heads, axis=0)).reshape(tile)
    att_ref[...] = jnp.concatenate(att_t, axis=0).astype(jnp.bfloat16)
    dq = jnp.concatenate(dq_t, axis=0).T * (1.0 / math.sqrt(head))
    sums[pl.ds(first_row + RADIUS, QROWS), pl.ds(pl.multiple_of(first_col + MARGIN, 8), QCOLS), q_lanes] = dq.reshape(
        QROWS, QCOLS, lanes
    )

    @pl.when((tile_row == pl.num_programs(0) - 1) & (tile_col == pl.num_programs(1) - 1))
    def _():
        grad_ref[:, :, q_lanes] = sums[:, :, q_lanes].astype(jnp.bfloat16)
        grad_ref[:, :, k_lanes] = (sums[:, :, k_lanes] * (1.0 / LOG2E)).astype(jnp.bfloat16)
        grad_ref[:, :, v_lanes] = sums[:, :, v_lanes].astype(jnp.bfloat16)


def attention(projected, g, bias, hot, place, g_place, lanes):
    wide = projected.shape[:2] + (3 * lanes,)
    queries, keys = QROWS * QCOLS, (QROWS + 2 * RADIUS) * (QCOLS + 2 * MARGIN)
    tiles = ((wide[0] - 2 * RADIUS) // QROWS, (wide[1] - 2 * MARGIN) // QCOLS)
    count = tiles[0] * tiles[1]
    return pl.pallas_call(
        attention_kernel,
        grid=tiles,
        in_specs=[
            pl.BlockSpec(wide, lambda r, c: (0, 0, place)),
            pl.BlockSpec((queries, lanes), lambda r, c: (r * tiles[1] + c, g_place)),
            pl.BlockSpec((1, keys, lanes), lambda r, c: (r, 0, 0)),
            pl.BlockSpec((queries, lanes), lambda r, c: (0, 0)),
        ],
        out_specs=[
            pl.BlockSpec((lanes, queries), lambda r, c: (0, r * tiles[1] + c)),
            pl.BlockSpec(wide, lambda r, c: (0, 0, 0)),
        ],
        out_shape=[
            jax.ShapeDtypeStruct((lanes, count * queries), jnp.bfloat16),
            jax.ShapeDtypeStruct(wide, jnp.bfloat16),
        ],
        scratch_shapes=[pltpu.VMEM((keys, queries), jnp.float32)] * PAIR
        + [pltpu.VMEM((keys, PAIR * queries), jnp.bfloat16)] * 2
        + [pltpu.VMEM(wide, jnp.float32)],
        compiler_params=pltpu.CompilerParams(
            dimension_semantics=("arbitrary", "arbitrary"), vmem_limit_bytes=48 * 1024 * 1024
        ),
        cost_estimate=pl.CostEstimate(
            flops=2 * 12 * 256 * keys * queries * PAIR * count,
            bytes_accessed=12 * count * queries * lanes * 2,
            transcendentals=keys * queries * PAIR * count,
        ),
    )(projected, g, bias, hot)


def window_columns(lat_first, tile_rows, total_rows, lanes):
    key_rows, key_cols = QROWS + 2 * RADIUS, QCOLS + 2 * MARGIN
    base = lat_first + QROWS * jnp.arange(tile_rows, dtype=jnp.int32)[:, None, None]
    q_row = base + jnp.arange(QROWS, dtype=jnp.int32)[None, None, :]
    k_row = base - RADIUS + jnp.arange(key_rows, dtype=jnp.int32)[None, :, None]
    start = jnp.clip(q_row - RADIUS, 0, total_rows - 2 * RADIUS - 1)
    row_in = (k_row >= start) & (k_row <= start + 2 * RADIUS)
    q_col = jnp.arange(QCOLS, dtype=jnp.int32)[None, :]
    k_col = jnp.arange(key_cols, dtype=jnp.int32)[:, None] - MARGIN
    col_in = (k_col >= q_col - RADIUS) & (k_col <= q_col + RADIUS)
    shape = (tile_rows, key_rows, key_cols)
    row_part = jnp.broadcast_to(jnp.where(row_in, 0.0, OUTSIDE)[:, :, None, :], shape + (QROWS,))
    col_part = jnp.broadcast_to(jnp.where(col_in, 0.0, OUTSIDE)[None, None], shape + (QCOLS,))
    rest = jnp.zeros(shape + (lanes - QROWS - QCOLS,), jnp.float32)
    columns = jnp.concatenate([row_part, col_part, rest], axis=-1).astype(jnp.bfloat16)
    columns = columns.reshape(tile_rows, key_rows * key_cols, lanes)
    r, c = jnp.arange(QROWS * QCOLS) // QCOLS, jnp.arange(QROWS * QCOLS) % QCOLS
    lane = jnp.arange(lanes)[None, :]
    hot = ((lane == r[:, None]) | (lane == QROWS + c[:, None])).astype(jnp.bfloat16)
    return columns, hot


def routed(value, route):
    lats, lons = lax.axis_size("lat"), lax.axis_size("lon")
    pairs = []
    for a in range(lats):
        for o in range(lons):
            to_lat, to_lon = route(a, o)
            if 0 <= to_lat < lats:
                pairs.append((a * lons + o, to_lat * lons + to_lon % lons))
    return lax.ppermute(value, ("lat", "lon"), pairs)


def partner(value):
    return routed(value, lambda a, o: (a, o ^ 1))


def beside(o):
    return o + 1 if o % 2 else o - 1


def by_core(core, mine, other, axis):
    return jnp.where(
        core == 0, jnp.concatenate([mine, other], axis=axis), jnp.concatenate([other, mine], axis=axis)
    )


def turned(parts, by):
    count = len(parts)
    whole = jnp.zeros((count,) + parts[0].shape, parts[0].dtype)
    for d, part in enumerate(parts):
        whole = lax.dynamic_update_index_in_dim(whole, part, (by - d) % count, 0)
    return whole


def lat_moves(blocks):
    lats = lax.axis_size("lat")
    return [routed(part, lambda a, o, d=d + 1: ((a + d) % lats, o)) for d, part in enumerate(blocks)]


def chip_moves(blocks):
    return [routed(part, lambda a, o, d=d + 1: (a, o + 2 * d)) for d, part in enumerate(blocks)]


def lon_bits():
    return (lax.axis_size("lon") // 2 - 1).bit_length()


def across(value, phase):
    last = lon_bits() - 1
    return routed(value, lambda a, o: (a, o ^ (2 << (last - phase if o % 2 else phase))))


def own_bit(core, chip, phase):
    return (chip >> jnp.where(core == 0, phase, lon_bits() - 1 - phase)) & 1


def joined(held, got, core, chip, phase):
    bit = own_bit(core, chip, phase)
    low, high = jnp.where(bit == 0, held, got), jnp.where(bit == 0, got, held)
    if phase == 0:
        return jnp.stack([low, high], 0)
    return jnp.where(core == 0, jnp.stack([low, high], 0), jnp.stack([low, high], phase))


def halved(total, core, chip, phase):
    bit = own_bit(core, chip, phase)
    lats, left = total.shape[:2]
    by_low = total.reshape((lats, left // 2, 2) + total.shape[2:])
    by_high = total.reshape((lats, 2, left // 2) + total.shape[2:])

    def half(which):
        low = lax.dynamic_index_in_dim(by_low, which, 2, keepdims=False)
        return jnp.where(core == 0, low, lax.dynamic_index_in_dim(by_high, which, 1, keepdims=False))

    return half(bit), half(1 - bit).astype(jnp.bfloat16)


def grown(kept, got):
    return kept.astype(jnp.float32) + got.astype(jnp.float32)


def pick(value, index, count, dim):
    return lax.dynamic_index_in_dim(value, index % count, dim, keepdims=False)


def added(kept, parts):
    for part in parts:
        kept = kept + part.astype(jnp.float32)
    return kept


def scatter_rest(kept, lat):
    lats = lax.axis_size("lat")
    moved = lat_moves([pick(kept, lat + d, lats, 0).astype(jnp.bfloat16) for d in range(1, lats)])
    return added(pick(kept, lat, lats, 0), moved)


def after(value, *others):
    return lax.optimization_barrier((value,) + others)[0]


def shards(features, grad_output, qkv_weight, out_weight):
    lat_rows, lon_cols, width = features.shape
    head = width // HEADS
    lanes = PAIR * head
    groups = HEADS // PAIR // 2
    half = width // 2
    lats, chips = lax.axis_size("lat"), lax.axis_size("lon") // 2
    lat, lon = lax.axis_index("lat"), lax.axis_index("lon")
    core, chip = lon % 2, lon // 2
    rows = qkv_weight.shape[0]
    per = 3 * lanes
    cells = lat_rows * lon_cols
    block_cols = 2 * lon_cols
    half_cols = lon_cols + MARGIN

    edge = jnp.where(core == 0, features[:, :MARGIN], features[:, lon_cols - MARGIN :])
    side = routed(edge, lambda a, o: (a, beside(o)))

    by_heads = qkv_weight.reshape(rows, 3, 2, groups, lanes)
    first = [by_heads[:, i, c, 0] for c in range(2) for i in range(3)]
    first = after(jnp.concatenate(first + [out_weight], axis=1), edge)
    first_moved = lat_moves([first] * (lats - 1))

    def columns(which):
        qkv = lax.dynamic_index_in_dim(by_heads, which, 2, keepdims=False)[:, :, 1:]
        return jnp.swapaxes(qkv, 1, 2).reshape(rows, -1)

    both = [features.reshape(cells, width), grad_output.reshape(cells, width), side.reshape(-1, width)]
    both.append(columns(1 - core).reshape(-1, width))
    both = jnp.concatenate(both, axis=0)
    near = jnp.where(
        core == 0, jnp.concatenate([side, features], axis=1), jnp.concatenate([features, side], axis=1)
    )
    top, bottom = near[:RADIUS], near[lat_rows - RADIUS :]
    first = after(turned([first] + first_moved, lat), both, top, bottom)
    both = partner(both)
    above = routed(bottom, lambda a, o: (a + 1, o))
    below = routed(top, lambda a, o: (a - 1, o))
    first_moved = chip_moves([first] * (chips - 1))
    margin = MARGIN * lat_rows
    x_partner = both[:cells].reshape(features.shape)
    go_partner = both[cells : 2 * cells].reshape(features.shape)
    side_partner = both[2 * cells : 2 * cells + margin].reshape(side.shape)
    rest = by_core(core, columns(core), both[2 * cells + margin :].reshape(rows, -1), 0)
    far = jnp.where(
        core == 0,
        jnp.concatenate([x_partner, side_partner], axis=1),
        jnp.concatenate([side_partner, x_partner], axis=1),
    )
    rest, above, below, far = lax.optimization_barrier((rest, above, below, far))
    rest_moved = lat_moves([rest] * (lats - 1))
    caps = partner(jnp.concatenate([above, below], axis=0))
    caps, *moved = lax.optimization_barrier((caps, *first_moved, *rest_moved[:-1]))
    first_moved, rest_moved[:-1] = moved[: chips - 1], moved[chips - 1 :]
    near = jnp.concatenate([above, near, below], axis=0)
    far = jnp.concatenate([caps[:RADIUS], far, caps[RADIUS:]], axis=0)
    wide_rows = near.shape[0]

    bits = lon_bits()

    def in_rows(grid, dims):
        grid = grid.reshape((chips,) + grid.shape[dims:])
        return jnp.swapaxes(grid, 0, 1).reshape((lats * chips,) + grid.shape[2:])

    first = in_rows(turned([first] + first_moved, chip), 1)
    x_wide = by_core(core, near, far, 1)
    wide_cols = x_wide.shape[1]
    x_wide = x_wide.reshape(-1, width)
    x_turned = lax.optimization_barrier(x_wide.T)
    go = by_core(core, grad_output, go_partner, 1)
    go = go.reshape(lat_rows // QROWS, QROWS, block_cols // QCOLS, QCOLS, width)
    go = lax.optimization_barrier(jnp.swapaxes(go, 1, 2).reshape(-1, width))

    def heads_of(which):
        qkv = lax.dynamic_slice_in_dim(first, which * per, per, 2).reshape(half, per)
        count = lats * chips // 2
        out = lax.dynamic_slice_in_dim(first, which * count, count, 0)[..., 2 * per :].reshape(-1, width)
        return qkv, out

    qkv_mine, out_mine = heads_of(core)
    qkv_other, out_other = heads_of(1 - core)
    cut = out_other.shape[0]
    swap = jnp.concatenate([jnp.concatenate([qkv_other[:cut], qkv_other[cut:]], axis=1), out_other], axis=0)
    swap = partner(swap)
    qkv_got = jnp.concatenate([swap[:cut, :per], swap[:cut, per:]], axis=0)

    def interleaved(mine, got):
        mine, got = (part.reshape(-1, rows, part.shape[1]) for part in (mine, got))
        return by_core(core, mine, got, 1).reshape(-1, mine.shape[2])

    qkv_first = interleaved(qkv_mine, qkv_got)
    out_heads = interleaved(out_mine, swap[cut:])

    bias, hot = window_columns(lat * lat_rows, lat_rows // QROWS, lat_rows * lats, lanes)
    scale = jnp.concatenate(
        [jnp.full((lanes,), LOG2E / math.sqrt(head), jnp.float32), jnp.ones((2 * lanes,), jnp.float32)]
    )

    def project(weights):
        result = dot(x_wide, weights) * jnp.tile(scale, weights.shape[1] // per)
        return result.astype(jnp.bfloat16).reshape(wide_rows, wide_cols, -1)

    def half_rows(grads, which):
        return lax.dynamic_slice_in_dim(grads, which * (grads.shape[0] // 2), grads.shape[0] // 2, 0)

    rest = turned([rest] + list(rest_moved), lat)
    for phase in range(bits - 1):
        rest = joined(rest, across(rest, phase), core, chip, phase)
    projected = project(qkv_first)
    g = dot(go, out_heads, NT).astype(jnp.bfloat16)
    projected, g, rest = lax.optimization_barrier((projected, g, rest))
    rest_got = across(rest, bits - 1)
    att_0, grads_0 = attention(projected, g, bias, hot, 0, 0, lanes)
    att_0, grads_0, rest_got = lax.optimization_barrier((att_0, grads_0, rest_got))
    rest = in_rows(joined(rest, rest_got, core, chip, bits - 1), bits)
    qkv_rest = rest.reshape(half * 2, -1)
    grads_0 = grads_0.reshape(-1, per)
    early_0 = dot(x_turned, grads_0).astype(jnp.bfloat16)
    projected = project(qkv_rest[:, :per])
    att_1, grads_1 = attention(projected, g, bias, hot, 0, 1, lanes)
    projected = project(qkv_rest[:, per:])

    grads_1 = grads_1.reshape(-1, per)
    early = [early_0, dot(x_turned, grads_1).astype(jnp.bfloat16)]
    early = [halved(part.reshape(lats, chips, -1, per), core, chip, 0) for part in early]
    early_kept, early_moved = (jnp.concatenate(parts, axis=-1) for parts in zip(*early))

    def gx_early(which):
        first_part = dot(half_rows(grads_0, which), qkv_first, NT)
        return (first_part + dot(half_rows(grads_1, which), qkv_rest[:, :per], NT)).astype(jnp.bfloat16)

    give_early, keep_early = gx_early(1 - core), gx_early(core)
    out_rows = [dot(part, go).astype(jnp.bfloat16) for part in (att_0, att_1)]
    g, early_kept, give_early, keep_early, early_moved, *out_rows = lax.optimization_barrier(
        (g, early_kept, give_early, keep_early, early_moved, *out_rows)
    )
    early_moved = across(early_moved, 0)
    att_2, grads_2 = attention(projected, g, bias, hot, 0, 2, lanes)
    grads_2 = grads_2.reshape(-1, per)

    def gx_late(which, before):
        return dot(half_rows(grads_2, which), qkv_rest[:, per:], NT) + before.astype(jnp.float32)

    att_2, grads_2, early_moved = lax.optimization_barrier((att_2, grads_2, early_moved))
    for phase in range(1, bits):
        early_kept, early_moved = halved(grown(early_kept, early_moved), core, chip, phase)
        att_2, grads_2, early_moved = lax.optimization_barrier((att_2, grads_2, early_moved))
        early_moved = across(early_moved, phase)
    give = gx_late(1 - core, give_early).astype(jnp.bfloat16)
    given = partner(give)
    out_rows = jnp.concatenate(out_rows + [dot(att_2, go).astype(jnp.bfloat16)], axis=0)
    swapped = partner(lax.dynamic_slice_in_dim(out_rows, (1 - core) * half, half, 1))
    late = dot(x_turned, grads_2).astype(jnp.bfloat16)
    out_mine = by_core(core, lax.dynamic_slice_in_dim(out_rows, core * half, half, 1), swapped, 0)
    late = jnp.concatenate([late, out_mine], axis=1).reshape(lats, chips, -1, per + half)
    given, late = lax.optimization_barrier((given, late))
    late, late_moved = halved(late, core, chip, 0)
    late_moved = across(late_moved, 0)
    gx = gx_late(core, keep_early) + given.astype(jnp.float32)
    gx = gx.reshape(wide_rows // 2, wide_cols, width)
    own = wide_rows // 2 - RADIUS
    outer = jnp.where(core == 0, gx[:RADIUS], gx[own:]).astype(jnp.bfloat16)
    gx = jnp.where(core == 0, gx[RADIUS:], gx[:own])
    inner = routed(outer, lambda a, o: (a + 1, o - 1) if o % 2 else (a - 1, o + 1))
    early_moved, outer = lax.optimization_barrier((early_moved, outer))
    early = grown(early_kept, early_moved)[:, 0]
    early_moved = lat_moves([pick(early, lat + d, lats, 0).astype(jnp.bfloat16) for d in range(1, lats)])
    late = grown(late, late_moved)
    for phase in range(1, bits):
        late, late_moved = halved(late, core, chip, phase)
        late_moved = across(late_moved, phase)
        if phase < bits - 1:
            late = grown(late, late_moved)
    gap = jnp.zeros((own - RADIUS,) + gx.shape[1:], jnp.float32)
    gx = gx + by_core(core, inner.astype(jnp.float32), gap, 0)
    other_half = lax.dynamic_slice_in_dim(gx, MARGIN + (1 - core) * lon_cols, lon_cols, 1).astype(jnp.bfloat16)
    mine_half = lax.dynamic_slice_in_dim(gx, MARGIN + core * lon_cols, lon_cols, 1)
    left, right = gx[:, :MARGIN].astype(jnp.bfloat16), gx[:, wide_cols - MARGIN :].astype(jnp.bfloat16)
    left, right, mine_half, other_half, late_moved = lax.optimization_barrier(
        (left, right, mine_half, other_half, late_moved)
    )
    early = added(pick(early, lat, lats, 0), early_moved)
    late = scatter_rest(grown(late, late_moved)[:, 0], lat)
    same = routed(jnp.where(core == 0, right, left), lambda a, o: (a, o - 2 if o % 2 else o + 2))
    cross = routed(jnp.where(core == 0, left, right), lambda a, o: (a, o + 1 if o % 2 else o - 1))
    swapped_x = partner(other_half)
    pad = jnp.zeros((own, lon_cols - MARGIN, width), jnp.float32)
    here = mine_half + by_core(core, same.astype(jnp.float32), pad, 1)
    there = swapped_x.astype(jnp.float32) + by_core(core, cross.astype(jnp.float32), pad, 1)
    grad_x = by_core(core, here.astype(jnp.bfloat16), there.astype(jnp.bfloat16), 0)

    total = jnp.concatenate([early, late], axis=1).reshape(2, rows, -1)
    keep = lax.dynamic_index_in_dim(total, core, 0, keepdims=False)
    give = lax.dynamic_index_in_dim(total, 1 - core, 0, keepdims=False).astype(jnp.bfloat16)
    got = partner(give).astype(jnp.float32)
    order = jnp.where(core == 0, jnp.stack([keep, got]), jnp.stack([got, keep]))
    grad_qkv = order[:, :, : groups * per].reshape(2, rows, groups, 3, lanes)
    grad_qkv = jnp.transpose(grad_qkv, (1, 3, 0, 2, 4)).reshape(rows, 3 * width)
    grad_out = jnp.transpose(order[:, :, groups * per :], (1, 0, 2)).reshape(rows, width)
    return grad_x, grad_qkv, grad_out


def solution(mesh):
    placed = (
        P("lat", "lon", None),
        P("lat", "lon", None),
        P(("lat", "lon"), None),
        P(("lat", "lon"), None),
    )
    return jax.shard_map(
        shards,
        mesh=mesh,
        in_specs=placed,
        out_specs=(P("lat", "lon", None), P(("lat", "lon"), None), P(("lat", "lon"), None)),
        check_vma=False,
    )
```
